32 devices in a mesh: seq: 16 (over z, x, core), uly: 2 (over y).
Axes of the slice: x: 2, y: 2, z: 4, core: 2. Of those that a mesh axis runs over, the one named last changes fastest.
Arguments:
- normed: bfloat16 [4096, 5376], P('seq', 'uly'), may hold values from -6 to 6
- q_raw: bfloat16 [4096, 2048], P('seq', 'uly'), may hold values from -6 to 6
- key_weight: bfloat16 [5376, 1024], P('uly', 'seq'), may hold values from -0.078125 to 0.078125
- value_weight: bfloat16 [5376, 1024], P('uly', 'seq'), may hold values from -0.078125 to 0.078125
- q_gain: float32 [128], replicated, may hold values from 0.1 to 1.9
- k_gain: float32 [128], replicated, may hold values from 0.1 to 1.9
- segment_ids: int32 [4096], replicated, may hold values from 0 to 1, as said below
- grad_out: bfloat16 [4096, 2048], P('seq', 'uly'), may hold values from -6 to 6
Outputs:
- attention: bfloat16 [4096, 2048], P('seq', 'uly')
- grad_normed: bfloat16 [4096, 5376], P('seq', 'uly')
- grad_q: bfloat16 [4096, 2048], P('seq', 'uly')
- grad_key_weight: float32 [5376, 1024], P('uly', 'seq')
- grad_value_weight: float32 [5376, 1024], P('uly', 'seq')
The draws below stay inside these ranges and needn't reach their ends.
Inputs may be any that keep to these rules, and one draw needn't show every extreme that they name: `segment_ids`: 0 up to one position and 1 from it on; that position lies between 1024 and 3072.
All inputs are finite; a program needn't handle non-finite values.
Results may differ from the reference program's by a relative error of at most 0.025.
Values may be sent and summed in bfloat16 or wider, within the bound.
No kernel may reach another device: no remote copies, remote signals or barrier semaphores. Data moves between devices by JAX's collectives and lax.ppermute only.
A program may use at most 128 MiB of HBM per device.

```python
import jax
import jax.numpy as jnp
from jax import lax

D = 5376
HD = 128
HK = 8
WINDOW = 1024
HQ = 16
SPAN = 256
TOKENS = 4096
N_SEQ = 16
N_ULY = 2


def draw_segment_ids(key, part):
    boundary = jax.random.randint(key, (), TOKENS // 4, 3 * TOKENS // 4 + 1)
    return (jnp.arange(TOKENS) >= boundary).astype(jnp.int32)


def block_levels(stream_key, extent, cuts, low, high):
    level = 1.0
    for dim, shards_of in cuts:
        heights = jax.random.uniform(jax.random.fold_in(jax.random.fold_in(stream_key, 6), dim), (shards_of,), jnp.float32, low / len(cuts), high / len(cuts))
        level = level * jnp.repeat(jnp.exp(heights), extent[dim] // shards_of).reshape((-1,) + (1,) * (len(extent) - 1 - dim))
    return level


def gaussian(own_key, extent, scale, most, split=(), kind=jnp.bfloat16):
    level = block_levels(own_key, extent, split, -0.22, 0.18) if split else 1.0
    result = jax.random.normal(own_key, extent, jnp.float32) * scale * level
    return jnp.minimum(jnp.maximum(result, -most), most).astype(kind)


def setup_inputs(seed: int = 0) -> dict:
    key_of = jax.random.split(jax.random.key(seed), 9)
    return {
        "normed": gaussian(key_of[0], (TOKENS, D), 1.0, 6.0, ((0, 16), (1, 2))),
        "q_raw": gaussian(key_of[1], (TOKENS, HQ * HD), 1.0, 6.0, ((0, 16), (1, 2))),
        "key_weight": gaussian(key_of[2], (D, HK * HD), D ** -0.5, 0.078125, ((0, 2), (1, 16))),
        "value_weight": gaussian(key_of[3], (D, HK * HD), D ** -0.5, 0.078125, ((0, 2), (1, 16))),
        "q_gain": jnp.clip(1.0 + 0.18 * jax.random.normal(key_of[4], (HD,), jnp.float32), 0.1, 1.9),
        "k_gain": jnp.clip(1.0 + 0.18 * jax.random.normal(key_of[5], (HD,), jnp.float32), 0.1, 1.9),
        "segment_ids": draw_segment_ids(jax.random.fold_in(key_of[8], 71), 0),
        "grad_out": gaussian(key_of[7], (TOKENS, HQ * HD), 1.0, 6.0, ((0, 16), (1, 2))),
    }


epsilon = 1e-06
query_scale = 168.0 ** (-0.5)

def normalize(raw_vals, gain, factor):
    mean_sq = lax.optimization_barrier(jnp.mean(raw_vals * raw_vals, axis=-1, keepdims=True))
    return raw_vals * lax.rsqrt(mean_sq + epsilon) * gain * factor

def attend_block(queries, key_block, value_block, grad_block, query_pos, key_pos, query_seg, key_seg):
    query_f = queries.astype(jnp.float32)
    key_f = key_block.astype(jnp.float32)
    value_f = value_block.astype(jnp.float32)
    grad_f = grad_block.astype(jnp.float32)
    scores = jnp.einsum('bhge,lhe->hgbl', query_f, key_f)
    allowed = (key_pos[None, :] <= query_pos[:, None]) & (key_pos[None, :] > query_pos[:, None] - WINDOW) & (key_seg[None, :] == query_seg[:, None])
    exp_scores = jnp.where(allowed[None, None], jnp.exp(scores), 0.0)
    probs = exp_scores / lax.optimization_barrier(jnp.sum(exp_scores, axis=-1, keepdims=True))
    weights = probs.astype(jnp.bfloat16)
    weight_f = weights.astype(jnp.float32)
    attended = jnp.einsum('hgbl,lhe->bhge', weight_f, value_f).astype(jnp.bfloat16)
    dprob = jnp.einsum('bhge,lhe->hgbl', grad_f, value_f)
    delta_row = lax.optimization_barrier(jnp.sum(probs * dprob, axis=-1, keepdims=True))
    dscore = (probs * (dprob - delta_row)).astype(jnp.bfloat16)
    dscore_f = dscore.astype(jnp.float32)
    dquery = jnp.einsum('hgbl,lhe->bhge', dscore_f, key_f)
    dkey = jnp.einsum('hgbl,bhge->lhe', dscore_f, query_f)
    dvalue = jnp.einsum('hgbl,bhge->lhe', weight_f, grad_f)
    return (attended, dquery, dkey, dvalue)

def reference(normed, q_raw, key_weight, value_weight, q_gain, k_gain, segment_ids, grad_out):
    feature_rows = D // N_ULY
    key_raw = jnp.zeros((TOKENS, HK * HD), jnp.float32)
    value_raw = jnp.zeros((TOKENS, HK * HD), jnp.float32)
    for slot_index in range(N_ULY):
        lower = slot_index * feature_rows
        rows_in = normed[:, lower:lower + feature_rows]
        key_term = jnp.dot(rows_in, key_weight[lower:lower + feature_rows], preferred_element_type=jnp.float32).astype(jnp.bfloat16)
        value_term = jnp.dot(rows_in, value_weight[lower:lower + feature_rows], preferred_element_type=jnp.float32).astype(jnp.bfloat16)
        key_term, value_term = lax.optimization_barrier((key_term, value_term))
        key_raw = key_raw + key_term.astype(jnp.float32)
        value_raw = value_raw + value_term.astype(jnp.float32)
    query_in = q_raw.astype(jnp.float32).reshape(TOKENS, HK, 2, HD)
    queries = normalize(query_in, q_gain, query_scale).astype(jnp.bfloat16)
    key_in = key_raw.reshape(TOKENS, HK, HD)
    keys_bf = normalize(key_in, k_gain, 1.0).astype(jnp.bfloat16)
    values_bf = value_raw.reshape(TOKENS, HK, HD).astype(jnp.bfloat16)
    grad_heads = grad_out.reshape(TOKENS, HK, 2, HD)
    block_rows = min(512, TOKENS)
    count_blocks = TOKENS // block_rows
    span_rows = block_rows + WINDOW
    key_pad = jnp.concatenate([jnp.zeros((WINDOW, HK, HD), jnp.bfloat16), keys_bf], axis=0)
    value_pad = jnp.concatenate([jnp.zeros((WINDOW, HK, HD), jnp.bfloat16), values_bf], axis=0)
    seg_ids = segment_ids.astype(jnp.int32)
    seg_pad = jnp.concatenate([jnp.full((WINDOW,), -1, jnp.int32), seg_ids])

    def step(carry, block_index):
        key_acc, value_acc = carry
        begin_row = (block_index * block_rows).astype(jnp.int32)
        query_pos = begin_row + jnp.arange(block_rows, dtype=jnp.int32)
        key_pos = begin_row - WINDOW + jnp.arange(span_rows, dtype=jnp.int32)
        attended, dquery, dkey, dvalue = attend_block(lax.dynamic_slice_in_dim(queries, begin_row, block_rows, 0), lax.dynamic_slice_in_dim(key_pad, begin_row, span_rows, 0), lax.dynamic_slice_in_dim(value_pad, begin_row, span_rows, 0), lax.dynamic_slice_in_dim(grad_heads, begin_row, block_rows, 0), query_pos, key_pos, lax.dynamic_slice_in_dim(seg_ids, begin_row, block_rows, 0), lax.dynamic_slice_in_dim(seg_pad, begin_row, span_rows, 0))
        key_acc = lax.dynamic_update_slice_in_dim(key_acc, lax.dynamic_slice_in_dim(key_acc, begin_row, span_rows, 0) + dkey, begin_row, 0)
        value_acc = lax.dynamic_update_slice_in_dim(value_acc, lax.dynamic_slice_in_dim(value_acc, begin_row, span_rows, 0) + dvalue, begin_row, 0)
        return ((key_acc, value_acc), (attended, dquery))
    zero_acc = jnp.zeros((TOKENS + WINDOW, HK, HD), jnp.float32)
    (key_acc, value_acc), (attended, dquery) = lax.scan(step, (zero_acc, zero_acc), jnp.arange(count_blocks, dtype=jnp.int32))
    attention = attended.reshape(TOKENS, HQ * HD)
    _, pull_query = jax.vjp(lambda raw_vals: normalize(raw_vals, q_gain, query_scale), query_in)
    grad_q = pull_query(dquery.reshape(TOKENS, HK, 2, HD))[0].astype(jnp.bfloat16).reshape(TOKENS, HQ * HD)
    _, pull_key = jax.vjp(lambda raw_vals: normalize(raw_vals, k_gain, 1.0), key_in)
    key_grad = pull_key(key_acc[WINDOW:])[0].astype(jnp.bfloat16).reshape(TOKENS, HK * HD)
    value_grad = value_acc[WINDOW:].astype(jnp.bfloat16).reshape(TOKENS, HK * HD)
    grad_normed = (jnp.dot(key_grad, key_weight.T, preferred_element_type=jnp.float32) + jnp.dot(value_grad, value_weight.T, preferred_element_type=jnp.float32)).astype(jnp.bfloat16)

    def weight_step(carry, seq_block):
        begin_row = (seq_block * SPAN).astype(jnp.int32)
        rows_in = lax.dynamic_slice_in_dim(normed, begin_row, SPAN, 0)
        key_term = jnp.dot(rows_in.T, lax.dynamic_slice_in_dim(key_grad, begin_row, SPAN, 0), preferred_element_type=jnp.float32).astype(jnp.bfloat16)
        value_term = jnp.dot(rows_in.T, lax.dynamic_slice_in_dim(value_grad, begin_row, SPAN, 0), preferred_element_type=jnp.float32).astype(jnp.bfloat16)
        key_term, value_term = lax.optimization_barrier((key_term, value_term))
        return ((carry[0] + key_term.astype(jnp.float32), carry[1] + value_term.astype(jnp.float32)), None)
    weight_zero = jnp.zeros((D, HK * HD), jnp.float32)
    (grad_key_weight, grad_value_weight), _ = lax.scan(weight_step, (weight_zero, weight_zero), jnp.arange(N_SEQ, dtype=jnp.int32))
    return (attention, grad_normed, grad_q, grad_key_weight, grad_value_weight)
```

```python
import functools

import jax
import jax.numpy as jnp
from jax import lax
from jax.experimental import pallas as pl
from jax.experimental.pallas import tpu as pltpu
from jax.sharding import PartitionSpec as P

HD = 128
WINDOW = 1024


epsilon = 1e-06
query_scale = 168.0 ** (-0.5)


def from_behind(array, axis, by):
    devices = lax.axis_size(axis)
    pairs = [(i, i + by) for i in range(devices) if 0 <= i + by < devices]
    return lax.ppermute(array, axis, pairs)


def normalize(raw_vals, gain, factor):
    mean_sq = jnp.mean(raw_vals * raw_vals, axis=-1, keepdims=True)
    return raw_vals * lax.rsqrt(mean_sq + epsilon) * gain * factor


def attend_block(
    queries, key_block, value_block, grad_block, query_pos, key_pos, query_seg, key_seg
):
    scores = jnp.einsum("bhge,lhe->hgbl", queries, key_block, preferred_element_type=jnp.float32)
    allowed = (
        (key_pos[None, :] <= query_pos[:, None])
        & (key_pos[None, :] > query_pos[:, None] - WINDOW)
        & (key_seg[None, :] == query_seg[:, None])
    )
    exp_scores = jnp.where(allowed[None, None], jnp.exp(scores), 0.0)
    probs = exp_scores / jnp.sum(exp_scores, axis=-1, keepdims=True)
    weights = probs.astype(jnp.bfloat16)
    attended = jnp.einsum(
        "hgbl,lhe->bhge", weights, value_block, preferred_element_type=jnp.float32
    ).astype(jnp.bfloat16)
    dprob = jnp.einsum(
        "bhge,lhe->hgbl", grad_block, value_block, preferred_element_type=jnp.float32
    )
    delta_row = jnp.sum(probs * dprob, axis=-1, keepdims=True)
    dscore = (probs * (dprob - delta_row)).astype(jnp.bfloat16)
    dquery = jnp.einsum("hgbl,lhe->bhge", dscore, key_block, preferred_element_type=jnp.float32)
    dkey = jnp.einsum("hgbl,bhge->lhe", dscore, queries, preferred_element_type=jnp.float32)
    dvalue = jnp.einsum("hgbl,bhge->lhe", weights, grad_block, preferred_element_type=jnp.float32)
    return (attended, dquery, dkey, dvalue)


def body_general(normed, q_raw, key_weight, value_weight, q_gain, k_gain, segment_ids, grad_out):
    rows_here = normed.shape[0]
    heads_here = q_raw.shape[1] // (2 * HD)
    seq_index = lax.axis_index("seq")
    base_row = seq_index * rows_here
    weight_pair = (
        lax.all_gather(key_weight, "seq", axis=1, tiled=True),
        lax.all_gather(value_weight, "seq", axis=1, tiled=True),
    )
    key_term = jnp.dot(normed, weight_pair[0], preferred_element_type=jnp.float32)
    value_term = jnp.dot(normed, weight_pair[1], preferred_element_type=jnp.float32)
    key_raw, value_raw = (
        lax.psum_scatter(
            key_term.astype(jnp.bfloat16), "uly", scatter_dimension=1, tiled=True
        ).astype(jnp.float32),
        lax.psum_scatter(
            value_term.astype(jnp.bfloat16), "uly", scatter_dimension=1, tiled=True
        ).astype(jnp.float32),
    )
    key_in = key_raw.reshape(rows_here, heads_here, HD)
    keys_bf = normalize(key_in, k_gain, 1.0).astype(jnp.bfloat16)
    values_bf = value_raw.reshape(rows_here, heads_here, HD).astype(jnp.bfloat16)
    query_in = q_raw.astype(jnp.float32).reshape(rows_here, heads_here, 2, HD)
    queries = normalize(query_in, q_gain, query_scale).astype(jnp.bfloat16)
    grad_heads = grad_out.reshape(rows_here, heads_here, 2, HD)
    stacked = jnp.stack([keys_bf, values_bf])
    distance_most = -(-WINDOW // rows_here)
    pieces = []
    for distance in range(distance_most, 0, -1):
        first_row = max(0, distance * rows_here - WINDOW)
        pieces.append(from_behind(stacked, "seq", distance))
    pieces.append(stacked)
    extended = jnp.concatenate(pieces, axis=1)
    block_rows = min(512, rows_here)
    span_rows = block_rows + WINDOW
    count_blocks = rows_here // block_rows
    seg_pad = jnp.concatenate([jnp.full((WINDOW,), -1, jnp.int32), segment_ids])
    query_seg_all = lax.dynamic_slice_in_dim(segment_ids, base_row, rows_here, 0)
    key_seg_all = lax.dynamic_slice_in_dim(seg_pad, base_row, WINDOW + rows_here, 0)

    def step(grad_acc, block_index):
        begin_row = block_index * block_rows
        query_pos = base_row + begin_row + jnp.arange(block_rows, dtype=jnp.int32)
        key_pos = base_row + begin_row - WINDOW + jnp.arange(span_rows, dtype=jnp.int32)
        key_block = lax.dynamic_slice_in_dim(extended, begin_row, span_rows, 1)
        attended, dquery, dkey, dvalue = attend_block(
            lax.dynamic_slice_in_dim(queries, begin_row, block_rows, 0),
            key_block[0],
            key_block[1],
            lax.dynamic_slice_in_dim(grad_heads, begin_row, block_rows, 0),
            query_pos,
            key_pos,
            lax.dynamic_slice_in_dim(query_seg_all, begin_row, block_rows, 0),
            lax.dynamic_slice_in_dim(key_seg_all, begin_row, span_rows, 0),
        )
        update = jnp.stack([dkey, dvalue])
        grad_acc = lax.dynamic_update_slice_in_dim(
            grad_acc,
            lax.dynamic_slice_in_dim(grad_acc, begin_row, span_rows, 1) + update,
            begin_row,
            1,
        )
        return (grad_acc, (attended, dquery))

    zero_acc = jnp.zeros((2, WINDOW + rows_here, heads_here, HD), jnp.float32)
    grad_acc, (attended, dquery) = lax.scan(
        step, zero_acc, jnp.arange(count_blocks, dtype=jnp.int32)
    )
    attention = attended.reshape(rows_here, 2 * heads_here * HD)
    dquery = dquery.reshape(rows_here, heads_here, 2, HD)
    own_grads = grad_acc[:, WINDOW:]
    offset_row = 0
    for distance in range(distance_most, 0, -1):
        first_row = max(0, distance * rows_here - WINDOW)
        piece_rows = rows_here - first_row
        outgoing = grad_acc[:, offset_row : offset_row + piece_rows]
        returned = from_behind(outgoing.astype(jnp.bfloat16), "seq", -distance).astype(
            outgoing.dtype
        )
        own_grads = own_grads.at[:, first_row:].add(returned)
        offset_row = offset_row + piece_rows
    _, pull_query = jax.vjp(lambda raw_vals: normalize(raw_vals, q_gain, query_scale), query_in)
    grad_q = pull_query(dquery)[0].astype(jnp.bfloat16).reshape(rows_here, 2 * heads_here * HD)
    _, pull_key = jax.vjp(lambda raw_vals: normalize(raw_vals, k_gain, 1.0), key_in)
    key_grad = pull_key(own_grads[0])[0].astype(jnp.bfloat16).reshape(rows_here, heads_here * HD)
    value_grad = own_grads[1].astype(jnp.bfloat16).reshape(rows_here, heads_here * HD)
    key_all, value_all = (
        lax.all_gather(key_grad, "uly", axis=1, tiled=True),
        lax.all_gather(value_grad, "uly", axis=1, tiled=True),
    )
    dims_last = (((1,), (1,)), ((), ()))
    total = lax.dot_general(key_all, weight_pair[0], dims_last, preferred_element_type=jnp.float32)
    total = total + lax.dot_general(
        value_all, weight_pair[1], dims_last, preferred_element_type=jnp.float32
    )
    grad_normed = total.astype(jnp.bfloat16)
    dims_first = (((0,), (0,)), ((), ()))
    key_part = lax.dot_general(normed, key_all, dims_first, preferred_element_type=jnp.float32)
    value_part = lax.dot_general(normed, value_all, dims_first, preferred_element_type=jnp.float32)
    grad_key_weight = lax.psum_scatter(
        key_part.astype(jnp.bfloat16), "seq", scatter_dimension=1, tiled=True
    ).astype(jnp.float32)
    grad_value_weight = lax.psum_scatter(
        value_part.astype(jnp.bfloat16), "seq", scatter_dimension=1, tiled=True
    ).astype(jnp.float32)
    return (attention, grad_normed, grad_q, grad_key_weight, grad_value_weight)


MIB = 1 << 20
MASKED = 16384.0
NT = (((1,), (1,)), ((), ()))
ANY = pl.BlockSpec(memory_space=pl.ANY)
SMEM = pl.BlockSpec(memory_space=pltpu.SMEM)
VMEM = pl.BlockSpec(memory_space=pltpu.VMEM)


def at(z, x, c):
    return (z * 2 + x) * 2 + c


def move(array, rule):
    return lax.ppermute(array, "seq", [(at(*a), at(*b)) for a, b in rule])


def along_z(array, hops):
    return move(array, [((z, x, c), (to, x, c)) for z, c, to in hops for x in (0, 1)])


def swap_core(array):
    return move(
        array, [((z, x, c), (z, x, 1 - c)) for z in range(4) for x in (0, 1) for c in (0, 1)]
    )


def swap_x(array):
    return move(
        array, [((z, x, c), (z, 1 - x, c)) for z in range(4) for x in (0, 1) for c in (0, 1)]
    )


def swap_uly(array):
    return lax.ppermute(array, "uly", [(0, 1), (1, 0)])


def call(kernel, out_shape, vmem, flops, bytes_accessed, **rest):
    return pl.pallas_call(
        kernel,
        out_shape=out_shape,
        compiler_params=pltpu.CompilerParams(vmem_limit_bytes=vmem * MIB),
        cost_estimate=pl.CostEstimate(
            flops=flops, bytes_accessed=bytes_accessed, transcendentals=0
        ),
        **rest,
    )


def shaped(shape, dtype=jnp.bfloat16):
    return jax.ShapeDtypeStruct(shape, dtype)


def transpose_in_kernel(key_ref, value_ref, out_ref):
    both = jnp.concatenate([key_ref[...], value_ref[...]], axis=1).astype(jnp.float32)
    out_ref[...] = both.T.astype(jnp.bfloat16)


def transpose_out_kernel(key_ref, value_ref, key_out, value_out):
    width = key_ref.shape[0]
    both = jnp.concatenate([key_ref[...], value_ref[...]], axis=0).T
    key_out[...] = both[:, :width]
    value_out[...] = both[:, width:]


def line_gather(own):
    r1 = along_z(own, [(0, 0, 1), (1, 1, 2), (2, 0, 3)])
    l1 = along_z(own, [(1, 1, 0), (2, 0, 1), (3, 1, 2)])
    r2 = along_z(r1, [(1, 0, 2), (2, 1, 3)])
    l2 = along_z(l1, [(2, 1, 1), (1, 0, 0)])
    r3 = along_z(r2, [(2, 0, 3)])
    l3 = along_z(l2, [(1, 1, 0)])
    return (own, r1, r2, r3, l1, l2, l3)


def line_reduce(far, mid, z):
    f1 = along_z(far, [(3, 0, 2), (0, 1, 1)])
    m1 = along_z(mid, [(3, 1, 2), (0, 0, 1)])
    f2 = along_z(far + f1, [(2, 0, 1), (1, 1, 2)])
    near = along_z(mid, [(0, 1, 1), (3, 0, 2)])
    m2 = along_z(mid + m1, [(2, 1, 1), (1, 0, 2)])
    f3 = along_z(far + f2, [(1, 0, 0), (2, 1, 3)])
    own = jnp.where((z == 0) | (z == 3), far, mid).astype(jnp.float32)
    return own + f3.astype(jnp.float32) + m2.astype(jnp.float32) + near.astype(jnp.float32)


def slot_copies(code, slot_at, refs, buffer, sems, act):
    for k, ref in enumerate(refs):

        @pl.when(slot_at == k)
        def _():
            copy = pltpu.make_async_copy(ref, buffer, sems)
            copy.start() if act else copy.wait()


def project_kernel(code, *refs):
    acts, weights = refs[:4], refs[4:11]
    mine, theirs, acts_v, w_v, acts_sem, w_sem = refs[11:]
    width = mine.shape[1]
    rows = acts[0].shape[0]
    place = code[0]

    def weight_copies(act):
        for slot in range(2):
            slot_copies(
                code, code[1 + slot], weights, w_v.at[pl.ds(slot * width, width)], w_sem.at[slot], act
            )

    weight_copies(True)
    copies = [
        pltpu.make_async_copy(acts[j], acts_v.at[j], acts_sem.at[j]) for j in range(4)
    ]
    for copy in copies:
        copy.start()
    weight_copies(False)
    for j in range(4):
        copies[j].wait()
        both = lax.dot_general(acts_v[j], w_v[...], NT, preferred_element_type=jnp.float32)
        begin = pl.multiple_of((place ^ j) * rows, rows)
        mine[pl.ds(begin, rows), :] = both[:, :width].astype(jnp.bfloat16)
        theirs[pl.ds(begin, rows), :] = both[:, width:].astype(jnp.bfloat16)


def project(code, acts, weights):
    rows, features = acts[0].shape
    width = weights[0].shape[0]
    return call(
        project_kernel,
        [shaped((4 * rows, width)), shaped((4 * rows, width))],
        24,
        2 * 4 * rows * features * 2 * width,
        4 * rows * features * 2 + 2 * width * features * 2,
        in_specs=[SMEM] + [ANY] * 11,
        out_specs=[VMEM, VMEM],
        scratch_shapes=[
            pltpu.VMEM((4, rows, features), jnp.bfloat16),
            pltpu.VMEM((2 * width, features), jnp.bfloat16),
            pltpu.SemaphoreType.DMA((4,)),
            pltpu.SemaphoreType.DMA((2,)),
        ],
        name="project",
    )(code, *acts, *weights)


def normalized(raw, gain, factor):
    inverse = lax.rsqrt(jnp.mean(raw * raw, axis=-1, keepdims=True) + epsilon)
    return raw * inverse * gain * factor


def normalized_pull(raw, gain, factor, cotangent):
    inverse = lax.rsqrt(jnp.mean(raw * raw, axis=-1, keepdims=True) + epsilon)
    scaled = cotangent * gain * factor
    along = jnp.mean(scaled * raw, axis=-1, keepdims=True)
    return inverse * (scaled - raw * (inverse * inverse * along))


def dot(a, b):
    return jnp.dot(a, b, preferred_element_type=jnp.float32)


def scores_kernel(
    code, q_ref, go_ref, own_ref, before_ref, key_mark, query_mark, gain_ref,
    e_ref, stat_ref, dv_own, dv_before, keys_v, acc
):
    block = pl.program_id(0)
    rows = q_ref.shape[1]
    chunks = e_ref.shape[2] // rows
    half = own_ref.shape[0]

    @pl.when(block == 0)
    def _():
        keys_v[:half, :HD] = before_ref[...]
        keys_v[half:, :HD] = own_ref[...]
        keys_v[:, HD:] = key_mark[...]
        acc[...] = jnp.zeros_like(acc)

    key_at = lax.broadcasted_iota(jnp.int32, (rows, rows), 0)
    query_at = lax.broadcasted_iota(jnp.int32, (rows, rows), 1)
    behind = key_at <= query_at
    stats = []
    for g in range(2):
        lanes = slice(g * HD, (g + 1) * HD)
        query = normalized(q_ref[0, :, lanes].astype(jnp.float32), gain_ref[...], query_scale)
        query_t = jnp.concatenate([query.T.astype(jnp.bfloat16), query_mark[...]], axis=0)
        total = jnp.zeros((1, rows), jnp.float32)
        for c in range(chunks):
            begin = pl.multiple_of((block + c) * rows, rows)
            e = jnp.exp(dot(keys_v[pl.ds(begin, rows), :], query_t))
            if c == 0:
                e = jnp.where(behind, 0.0, e)
            if c == chunks - 1:
                e = jnp.where(behind, e, 0.0)
            total = total + jnp.sum(e, axis=0, keepdims=True)
            e_ref[0, g, c * rows : (c + 1) * rows, :] = e.astype(jnp.bfloat16)
        inverse = 1.0 / total
        stats.append(inverse)
        grad = (go_ref[0, :, lanes].astype(jnp.float32).T * inverse).T.astype(jnp.bfloat16)
        span = pl.ds(pl.multiple_of(block * rows, rows), chunks * rows)
        acc[span, :] = acc[span, :] + dot(e_ref[0, g], grad)
    stat_ref[0] = jnp.concatenate(stats + [jnp.zeros((6, rows), jnp.float32)], axis=0)

    @pl.when(block == pl.num_programs(0) - 1)
    def _():
        dv_before[...] = acc[:half, :].astype(jnp.bfloat16)
        dv_own[...] = acc[half:, :]


def whole(shape):
    return pl.BlockSpec(shape, lambda b, code: (0,) * len(shape))


def attend_scores(code, q, go, keys, keys_before, key_mark, query_mark, gain):
    blocks, rows, _ = q.shape
    half = blocks * rows
    span = half + rows
    picked = pl.BlockSpec((1, rows, 2 * HD), lambda b, code: (b ^ code[0], 0, 0))
    return call(
        scores_kernel,
        [
            shaped((blocks, 2, span, rows)),
            shaped((blocks, 8, rows), jnp.float32),
            shaped((half, HD), jnp.float32),
            shaped((half, HD)),
        ],
        40,
        2 * 2 * half * span * 3 * HD,
        2 * half * span * 2 + 8 * half * HD * 2,
        grid_spec=pltpu.PrefetchScalarGridSpec(
            num_scalar_prefetch=1,
            grid=(blocks,),
            in_specs=[
                picked,
                picked,
                whole((half, HD)),
                whole((half, HD)),
                whole((2 * half, HD)),
                pl.BlockSpec((HD, rows), lambda b, code: (0, b)),
                whole((1, HD)),
            ],
            out_specs=[
                pl.BlockSpec((1, 2, span, rows), lambda b, code: (b, 0, 0, 0)),
                pl.BlockSpec((1, 8, rows), lambda b, code: (b, 0, 0)),
                whole((half, HD)),
                whole((half, HD)),
            ],
            scratch_shapes=[
                pltpu.VMEM((2 * half, 2 * HD), jnp.bfloat16),
                pltpu.VMEM((2 * half, HD), jnp.float32),
            ],
        ),
        name="attend_scores",
    )(code, q, go, keys, keys_before, key_mark, query_mark, gain)


def values_kernel(
    code, q_ref, go_ref, own_ref, before_ref, v_own, v_before, gain_ref, e_ref, stat_ref,
    out_ref, gq_ref, dk_own, dk_before, values_v, values_t, keys_t, acc
):
    block = pl.program_id(0)
    rows = q_ref.shape[1]
    span_rows = e_ref.shape[2]
    half = own_ref.shape[0]

    @pl.when(block == 0)
    def _():
        values_v[:half, :] = v_before[...]
        values_v[half:, :] = v_own[...]
        values_t[...] = values_v[...].astype(jnp.float32).T.astype(jnp.bfloat16)
        keys_t[:, :half] = before_ref[...].astype(jnp.float32).T.astype(jnp.bfloat16)
        keys_t[:, half:] = own_ref[...].astype(jnp.float32).T.astype(jnp.bfloat16)
        acc[...] = jnp.zeros_like(acc)

    span = pl.ds(pl.multiple_of(block * rows, rows), span_rows)
    for g in range(2):
        lanes = slice(g * HD, (g + 1) * HD)
        raw = q_ref[0, :, lanes].astype(jnp.float32)
        query = normalized(raw, gain_ref[...], query_scale).astype(jnp.bfloat16)
        inverse = stat_ref[0, g : g + 1, :]
        e = e_ref[0, g]
        out_t = dot(values_t[:, span], e) * inverse
        out_ref[0, :, lanes] = out_t.T.astype(jnp.bfloat16)
        grad_t = go_ref[0, :, lanes].astype(jnp.float32).T
        along = jnp.sum(out_t * grad_t, axis=0, keepdims=True) * inverse
        dprob = dot(values_v[span, :], (grad_t * inverse).astype(jnp.bfloat16))
        dscore = (e.astype(jnp.float32) * (dprob - along)).astype(jnp.bfloat16)
        acc[span, :] = acc[span, :] + dot(dscore, query)
        dquery = dot(keys_t[:, span], dscore).T
        gq_ref[0, :, lanes] = normalized_pull(raw, gain_ref[...], query_scale, dquery).astype(
            jnp.bfloat16
        )

    @pl.when(block == pl.num_programs(0) - 1)
    def _():
        dk_before[...] = acc[:half, :].astype(jnp.bfloat16)
        dk_own[...] = acc[half:, :]


def attend_values(code, q, go, keys, keys_before, values, values_before, gain, e, stat):
    blocks, rows, _ = q.shape
    half = blocks * rows
    span = half + rows
    picked = pl.BlockSpec((1, rows, 2 * HD), lambda b, code: (b ^ code[0], 0, 0))
    return call(
        values_kernel,
        [
            shaped(q.shape),
            shaped(q.shape),
            shaped((half, HD), jnp.float32),
            shaped((half, HD)),
        ],
        40,
        2 * 2 * half * span * 4 * HD,
        2 * half * span * 2 + 8 * half * HD * 2,
        grid_spec=pltpu.PrefetchScalarGridSpec(
            num_scalar_prefetch=1,
            grid=(blocks,),
            in_specs=[picked, picked]
            + [whole((half, HD))] * 4
            + [
                whole((1, HD)),
                pl.BlockSpec((1, 2, span, rows), lambda b, code: (b, 0, 0, 0)),
                pl.BlockSpec((1, 8, rows), lambda b, code: (b, 0, 0)),
            ],
            out_specs=[picked, picked, whole((half, HD)), whole((half, HD))],
            scratch_shapes=[
                pltpu.VMEM((2 * half, HD), jnp.bfloat16),
                pltpu.VMEM((HD, 2 * half), jnp.bfloat16),
                pltpu.VMEM((HD, 2 * half), jnp.bfloat16),
                pltpu.VMEM((2 * half, HD), jnp.float32),
            ],
        ),
        name="attend_values",
    )(code, q, go, keys, keys_before, values, values_before, gain, e, stat)


def weight_grad_kernel(code, mine, theirs, a0, a1, a2, a3, far, mid, acts_v, grad_v, acts_sem):
    acts = (a0, a1, a2, a3)
    rows, features = a0.shape
    width = far.shape[0]
    copies = [
        pltpu.make_async_copy(acts[j], acts_v.at[j], acts_sem.at[j]) for j in range(4)
    ]
    for copy in copies:
        copy.start()
    first = code[3] == 1
    for j in range(4):
        span = pl.ds(pl.multiple_of((code[0] ^ j) * rows, rows), rows)
        own = mine[span, :].astype(jnp.float32).T
        other = theirs[span, :].astype(jnp.float32).T
        grad_v[j, :width, :] = jnp.where(first, own, other).astype(jnp.bfloat16)
        grad_v[j, width:, :] = jnp.where(first, other, own).astype(jnp.bfloat16)
    for copy in copies:
        copy.wait()
    tile = features // 3
    for n in range(3):
        lanes = slice(n * tile, (n + 1) * tile)
        both = dot(grad_v[0], acts_v[0, :, lanes])
        for j in range(1, 4):
            both = both + dot(grad_v[j], acts_v[j, :, lanes])
        far[:, lanes] = both[:width].astype(jnp.bfloat16)
        mid[:, lanes] = both[width:].astype(jnp.bfloat16)


def weight_grad(code, mine, theirs, acts):
    rows, features = acts[0].shape
    width = mine.shape[1]
    return call(
        weight_grad_kernel,
        [shaped((width, features)), shaped((width, features))],
        32,
        2 * 4 * rows * features * 2 * width,
        4 * rows * features * 2 + 2 * width * features * 2,
        in_specs=[SMEM, VMEM, VMEM] + [ANY] * 4,
        out_specs=[VMEM, VMEM],
        scratch_shapes=[
            pltpu.VMEM((4, rows, features), jnp.bfloat16),
            pltpu.VMEM((4, 2 * width, rows), jnp.bfloat16),
            pltpu.SemaphoreType.DMA((4,)),
        ],
        name="weight_grad",
    )(code, mine, theirs, *acts)


def input_grad_kernel(code, *refs):
    grads, key_w, value_w = refs[:4], refs[4:11], refs[11:18]
    kept, sent, w_v, w_sem = refs[18:]
    rows, features = kept.shape[1:]
    width = grads[0].shape[1]

    def weight_copies(act):
        for part, weights in enumerate((key_w, value_w)):
            for slot in range(2):
                row = 2 * part + slot
                slot_copies(
                    code, code[1 + slot], weights, w_v.at[pl.ds(row * width, width)], w_sem.at[row], act
                )

    weight_copies(True)
    weight_copies(False)
    tile = features // 3
    for j in (3, 1, 2, 0):
        span = pl.ds(pl.multiple_of((code[0] ^ j) * rows, rows), rows)
        grad = jnp.concatenate([ref[span, :] for ref in grads], axis=1)
        target = sent if j % 2 else kept
        for n in range(3):
            lanes = slice(n * tile, (n + 1) * tile)
            target[j // 2, :, lanes] = dot(grad, w_v[:, lanes]).astype(jnp.bfloat16)


def input_grad(code, grads, key_weights, value_weights, rows):
    width, features = key_weights[0].shape
    return call(
        input_grad_kernel,
        [shaped((2, rows, features)), shaped((2, rows, features))],
        32,
        2 * 4 * rows * features * 4 * width,
        4 * rows * features * 2 + 4 * width * features * 2,
        in_specs=[SMEM] + [VMEM] * 4 + [ANY] * 14,
        out_specs=[VMEM, VMEM],
        scratch_shapes=[
            pltpu.VMEM((4 * width, features), jnp.bfloat16),
            pltpu.SemaphoreType.DMA((4,)),
        ],
        name="input_grad",
    )(code, *grads, *key_weights, *value_weights)


def body_planes(normed, q_raw, key_weight, value_weight, q_gain, k_gain, segment_ids, grad_out):
    rows, features = normed.shape
    half = 4 * rows
    width = key_weight.shape[1]
    place = lax.axis_index("seq")
    uly = lax.axis_index("uly")
    z, x, c = place // 4, (place // 2) % 2, place % 2

    def slot_code(slot):
        distance = z - (c + 2 * slot)
        return jnp.where(distance >= 0, distance, 3 - distance)

    code = jnp.stack(
        [place % 4, slot_code(uly), slot_code(1 - uly), (c == uly).astype(jnp.int32)]
    ).astype(jnp.int32)
    gain_q = q_gain.reshape(1, HD)

    slabs = call(
        transpose_in_kernel,
        shaped((2 * width, features)),
        16,
        0,
        8 * width * features,
        in_specs=[VMEM, VMEM],
        out_specs=VMEM,
        name="transpose_in",
    )(key_weight, value_weight)
    other = move(
        slabs, [((z, x, 1 - z % 2), (z, x, z % 2)) for z in range(4) for x in (0, 1)]
    )
    first, second = jnp.where(c == 0, slabs, other), jnp.where(c == 0, other, slabs)
    key_weights = line_gather(jnp.concatenate([first[:width], second[:width]], axis=0))
    value_weights = line_gather(jnp.concatenate([first[width:], second[width:]], axis=0))

    normed_x = swap_x(normed)
    acts = (normed, swap_core(normed), normed_x, swap_core(normed_x))

    heads = jnp.stack([q_raw, grad_out]).reshape(2, rows, 2, 2, 2 * HD)

    def pick(array, axis, index):
        return lax.dynamic_index_in_dim(array, index, axis, keepdims=False)

    near = pick(heads, 3, x)
    from_x = swap_x(pick(heads, 3, 1 - x))
    stage = jnp.stack([near, from_x])
    from_core = swap_core(pick(stage, 3, 1 - c))
    stage = pick(stage, 3, c)
    ordered = jnp.stack([stage[0], from_core[0], stage[1], from_core[1]])
    q, go = ordered[:, 0], ordered[:, 1]

    seg_pad = jnp.concatenate([jnp.full((half,), -1, jnp.int32), segment_ids])
    key_seg = lax.dynamic_slice_in_dim(seg_pad, z * half, 2 * half, 0)
    query_seg = lax.dynamic_slice_in_dim(segment_ids, z * half, half, 0)
    lane = lax.broadcasted_iota(jnp.int32, (2 * half, HD), 1)
    key_mark = jnp.where((lane < 2) & (lane != key_seg[:, None]), -MASKED, 0.0).astype(jnp.bfloat16)
    row = lax.broadcasted_iota(jnp.int32, (HD, half), 0)
    query_mark = jnp.where(row == query_seg[None, :], 1.0, 0.0).astype(jnp.bfloat16)

    forward = [(z, c, z + 1) for z in range(3) for c in (0, 1)]
    backward = [(z + 1, c, z) for z in range(3) for c in (0, 1)]

    mine, theirs = project(code, acts, key_weights)
    key_raw = mine.astype(jnp.float32) + swap_uly(theirs).astype(jnp.float32)
    keys = normalized(key_raw, k_gain, 1.0).astype(jnp.bfloat16)
    keys_before = along_z(keys, forward)
    mine, theirs = project(code, acts, value_weights)
    values = (mine.astype(jnp.float32) + swap_uly(theirs).astype(jnp.float32)).astype(jnp.bfloat16)
    values_before = along_z(values, forward)

    e, stat, dv_own, dv_before = attend_scores(
        code, q, go, keys, keys_before, key_mark, query_mark, gain_q
    )
    value_grad = (dv_own + along_z(dv_before, backward).astype(jnp.float32)).astype(jnp.bfloat16)
    value_grad_far = swap_uly(value_grad)
    value_sums = line_reduce(*weight_grad(code, value_grad, value_grad_far, acts), z)

    out, gq, dk_own, dk_before = attend_values(
        code, q, go, keys, keys_before, values, values_before, gain_q, e, stat
    )
    dkey = dk_own + along_z(dk_before, backward).astype(jnp.float32)
    key_grad = normalized_pull(key_raw, k_gain, 1.0, dkey).astype(jnp.bfloat16)
    key_grad_far = swap_uly(key_grad)
    key_sums = line_reduce(*weight_grad(code, key_grad, key_grad_far, acts), z)

    pair = jnp.stack([out, gq], axis=1).reshape(2, 2, 2, rows, 2 * HD)
    from_core = swap_core(pair[:, 1])
    both = jnp.where(
        c == 0, jnp.stack([pair[:, 0], from_core], axis=2), jnp.stack([from_core, pair[:, 0]], axis=2)
    )
    from_x = swap_x(both[1])
    near = both[0]
    both = jnp.where(
        x == 0, jnp.stack([near, from_x], axis=2), jnp.stack([from_x, near], axis=2)
    )
    both = both.transpose(0, 3, 1, 2, 4).reshape(2, rows, 8 * HD)
    attention, grad_q = both[0], both[1]

    kept, sent = input_grad(
        code, (key_grad, key_grad_far, value_grad, value_grad_far), key_weights, value_weights, rows
    )
    away = kept[1].astype(jnp.float32) + swap_core(sent[1]).astype(jnp.float32)
    from_x = swap_x(away.astype(jnp.bfloat16))
    grad_normed = (
        kept[0].astype(jnp.float32)
        + swap_core(sent[0]).astype(jnp.float32)
        + from_x.astype(jnp.float32)
    ).astype(jnp.bfloat16)

    sums = jnp.stack([key_sums, value_sums]).reshape(2, 2, width, features)
    other = move(
        pick(sums, 1, 1 - c).astype(jnp.bfloat16),
        [((z, x, z % 2), (z, x, 1 - z % 2)) for z in range(4) for x in (0, 1)],
    )
    halves = jnp.where(c == z % 2, pick(sums, 1, c), other.astype(jnp.float32))
    grad_key_weight, grad_value_weight = call(
        transpose_out_kernel,
        [shaped((features, width), jnp.float32)] * 2,
        16,
        0,
        16 * width * features,
        in_specs=[VMEM, VMEM],
        out_specs=[VMEM, VMEM],
        name="transpose_out",
    )(halves[0], halves[1])
    return (attention, grad_normed, grad_q, grad_key_weight, grad_value_weight)


def body(normed, q_raw, *rest):
    planes = (
        lax.axis_size("seq") == 16
        and lax.axis_size("uly") == 2
        and 4 * normed.shape[0] == WINDOW
        and q_raw.shape[1] == 8 * HD
    )
    return (body_planes if planes else body_general)(normed, q_raw, *rest)


def solution(mesh):
    return jax.shard_map(
        body,
        mesh=mesh,
        in_specs=(
            P("seq", "uly"),
            P("seq", "uly"),
            P("uly", "seq"),
            P("uly", "seq"),
            P(),
            P(),
            P(),
            P("seq", "uly"),
        ),
        out_specs=(
            P("seq", "uly"),
            P("seq", "uly"),
            P("seq", "uly"),
            P("uly", "seq"),
            P("uly", "seq"),
        ),
        check_vma=False,
    )
```

```python
import functools

import jax
import jax.numpy as jnp
from jax import lax
from jax.experimental import pallas as pl
from jax.experimental.pallas import tpu as pltpu
from jax.sharding import PartitionSpec as P

HD = 128
WINDOW = 1024


epsilon = 1e-06
query_scale = 168.0 ** (-0.5)


def from_behind(array, axis, by):
    devices = lax.axis_size(axis)
    pairs = [(i, i + by) for i in range(devices) if 0 <= i + by < devices]
    return lax.ppermute(array, axis, pairs)


def normalize(raw_vals, gain, factor):
    mean_sq = jnp.mean(raw_vals * raw_vals, axis=-1, keepdims=True)
    return raw_vals * lax.rsqrt(mean_sq + epsilon) * gain * factor


def attend_block(
    queries, key_block, value_block, grad_block, query_pos, key_pos, query_seg, key_seg
):
    scores = jnp.einsum("bhge,lhe->hgbl", queries, key_block, preferred_element_type=jnp.float32)
    allowed = (
        (key_pos[None, :] <= query_pos[:, None])
        & (key_pos[None, :] > query_pos[:, None] - WINDOW)
        & (key_seg[None, :] == query_seg[:, None])
    )
    exp_scores = jnp.where(allowed[None, None], jnp.exp(scores), 0.0)
    probs = exp_scores / jnp.sum(exp_scores, axis=-1, keepdims=True)
    weights = probs.astype(jnp.bfloat16)
    attended = jnp.einsum(
        "hgbl,lhe->bhge", weights, value_block, preferred_element_type=jnp.float32
    ).astype(jnp.bfloat16)
    dprob = jnp.einsum(
        "bhge,lhe->hgbl", grad_block, value_block, preferred_element_type=jnp.float32
    )
    delta_row = jnp.sum(probs * dprob, axis=-1, keepdims=True)
    dscore = (probs * (dprob - delta_row)).astype(jnp.bfloat16)
    dquery = jnp.einsum("hgbl,lhe->bhge", dscore, key_block, preferred_element_type=jnp.float32)
    dkey = jnp.einsum("hgbl,bhge->lhe", dscore, queries, preferred_element_type=jnp.float32)
    dvalue = jnp.einsum("hgbl,bhge->lhe", weights, grad_block, preferred_element_type=jnp.float32)
    return (attended, dquery, dkey, dvalue)


def body_general(normed, q_raw, key_weight, value_weight, q_gain, k_gain, segment_ids, grad_out):
    rows_here = normed.shape[0]
    heads_here = q_raw.shape[1] // (2 * HD)
    seq_index = lax.axis_index("seq")
    base_row = seq_index * rows_here
    weight_pair = (
        lax.all_gather(key_weight, "seq", axis=1, tiled=True),
        lax.all_gather(value_weight, "seq", axis=1, tiled=True),
    )
    key_term = jnp.dot(normed, weight_pair[0], preferred_element_type=jnp.float32)
    value_term = jnp.dot(normed, weight_pair[1], preferred_element_type=jnp.float32)
    key_raw, value_raw = (
        lax.psum_scatter(
            key_term.astype(jnp.bfloat16), "uly", scatter_dimension=1, tiled=True
        ).astype(jnp.float32),
        lax.psum_scatter(
            value_term.astype(jnp.bfloat16), "uly", scatter_dimension=1, tiled=True
        ).astype(jnp.float32),
    )
    key_in = key_raw.reshape(rows_here, heads_here, HD)
    keys_bf = normalize(key_in, k_gain, 1.0).astype(jnp.bfloat16)
    values_bf = value_raw.reshape(rows_here, heads_here, HD).astype(jnp.bfloat16)
    query_in = q_raw.astype(jnp.float32).reshape(rows_here, heads_here, 2, HD)
    queries = normalize(query_in, q_gain, query_scale).astype(jnp.bfloat16)
    grad_heads = grad_out.reshape(rows_here, heads_here, 2, HD)
    stacked = jnp.stack([keys_bf, values_bf])
    distance_most = -(-WINDOW // rows_here)
    pieces = []
    for distance in range(distance_most, 0, -1):
        first_row = max(0, distance * rows_here - WINDOW)
        pieces.append(from_behind(stacked, "seq", distance))
    pieces.append(stacked)
    extended = jnp.concatenate(pieces, axis=1)
    block_rows = min(512, rows_here)
    span_rows = block_rows + WINDOW
    count_blocks = rows_here // block_rows
    seg_pad = jnp.concatenate([jnp.full((WINDOW,), -1, jnp.int32), segment_ids])
    query_seg_all = lax.dynamic_slice_in_dim(segment_ids, base_row, rows_here, 0)
    key_seg_all = lax.dynamic_slice_in_dim(seg_pad, base_row, WINDOW + rows_here, 0)

    def step(grad_acc, block_index):
        begin_row = block_index * block_rows
        query_pos = base_row + begin_row + jnp.arange(block_rows, dtype=jnp.int32)
        key_pos = base_row + begin_row - WINDOW + jnp.arange(span_rows, dtype=jnp.int32)
        key_block = lax.dynamic_slice_in_dim(extended, begin_row, span_rows, 1)
        attended, dquery, dkey, dvalue = attend_block(
            lax.dynamic_slice_in_dim(queries, begin_row, block_rows, 0),
            key_block[0],
            key_block[1],
            lax.dynamic_slice_in_dim(grad_heads, begin_row, block_rows, 0),
            query_pos,
            key_pos,
            lax.dynamic_slice_in_dim(query_seg_all, begin_row, block_rows, 0),
            lax.dynamic_slice_in_dim(key_seg_all, begin_row, span_rows, 0),
        )
        update = jnp.stack([dkey, dvalue])
        grad_acc = lax.dynamic_update_slice_in_dim(
            grad_acc,
            lax.dynamic_slice_in_dim(grad_acc, begin_row, span_rows, 1) + update,
            begin_row,
            1,
        )
        return (grad_acc, (attended, dquery))

    zero_acc = jnp.zeros((2, WINDOW + rows_here, heads_here, HD), jnp.float32)
    grad_acc, (attended, dquery) = lax.scan(
        step, zero_acc, jnp.arange(count_blocks, dtype=jnp.int32)
    )
    attention = attended.reshape(rows_here, 2 * heads_here * HD)
    dquery = dquery.reshape(rows_here, heads_here, 2, HD)
    own_grads = grad_acc[:, WINDOW:]
    offset_row = 0
    for distance in range(distance_most, 0, -1):
        first_row = max(0, distance * rows_here - WINDOW)
        piece_rows = rows_here - first_row
        outgoing = grad_acc[:, offset_row : offset_row + piece_rows]
        returned = from_behind(outgoing.astype(jnp.bfloat16), "seq", -distance).astype(
            outgoing.dtype
        )
        own_grads = own_grads.at[:, first_row:].add(returned)
        offset_row = offset_row + piece_rows
    _, pull_query = jax.vjp(lambda raw_vals: normalize(raw_vals, q_gain, query_scale), query_in)
    grad_q = pull_query(dquery)[0].astype(jnp.bfloat16).reshape(rows_here, 2 * heads_here * HD)
    _, pull_key = jax.vjp(lambda raw_vals: normalize(raw_vals, k_gain, 1.0), key_in)
    key_grad = pull_key(own_grads[0])[0].astype(jnp.bfloat16).reshape(rows_here, heads_here * HD)
    value_grad = own_grads[1].astype(jnp.bfloat16).reshape(rows_here, heads_here * HD)
    key_all, value_all = (
        lax.all_gather(key_grad, "uly", axis=1, tiled=True),
        lax.all_gather(value_grad, "uly", axis=1, tiled=True),
    )
    dims_last = (((1,), (1,)), ((), ()))
    total = lax.dot_general(key_all, weight_pair[0], dims_last, preferred_element_type=jnp.float32)
    total = total + lax.dot_general(
        value_all, weight_pair[1], dims_last, preferred_element_type=jnp.float32
    )
    grad_normed = total.astype(jnp.bfloat16)
    dims_first = (((0,), (0,)), ((), ()))
    key_part = lax.dot_general(normed, key_all, dims_first, preferred_element_type=jnp.float32)
    value_part = lax.dot_general(normed, value_all, dims_first, preferred_element_type=jnp.float32)
    grad_key_weight = lax.psum_scatter(
        key_part.astype(jnp.bfloat16), "seq", scatter_dimension=1, tiled=True
    ).astype(jnp.float32)
    grad_value_weight = lax.psum_scatter(
        value_part.astype(jnp.bfloat16), "seq", scatter_dimension=1, tiled=True
    ).astype(jnp.float32)
    return (attention, grad_normed, grad_q, grad_key_weight, grad_value_weight)


MIB = 1 << 20
MASKED = 16384.0
NT = (((1,), (1,)), ((), ()))
HBM = pl.BlockSpec(memory_space=pltpu.HBM)
SMEM = pl.BlockSpec(memory_space=pltpu.SMEM)
VMEM = pl.BlockSpec(memory_space=pltpu.VMEM)


def at(z, x, c):
    return (z * 2 + x) * 2 + c


def move(array, rule):
    return lax.ppermute(array, "seq", [(at(*a), at(*b)) for a, b in rule])


def along_z(array, hops):
    return move(array, [((z, x, c), (to, x, c)) for z, c, to in hops for x in (0, 1)])


def swap_core(array):
    return move(
        array, [((z, x, c), (z, x, 1 - c)) for z in range(4) for x in (0, 1) for c in (0, 1)]
    )


def swap_x(array):
    return move(
        array, [((z, x, c), (z, 1 - x, c)) for z in range(4) for x in (0, 1) for c in (0, 1)]
    )


def swap_uly(array):
    return lax.ppermute(array, "uly", [(0, 1), (1, 0)])


def call(kernel, out_shape, vmem, flops, bytes_accessed, **rest):
    return pl.pallas_call(
        kernel,
        out_shape=out_shape,
        compiler_params=pltpu.CompilerParams(vmem_limit_bytes=vmem * MIB),
        cost_estimate=pl.CostEstimate(
            flops=flops, bytes_accessed=bytes_accessed, transcendentals=0
        ),
        **rest,
    )


def shaped(shape, dtype=jnp.bfloat16):
    return jax.ShapeDtypeStruct(shape, dtype)


def after_all(arrays, *earlier):
    return lax.optimization_barrier(tuple(arrays) + earlier)[: len(arrays)]


def after(array, *earlier):
    return after_all((array,), *earlier)[0]


HOP_ONE = [(0, 0, 1), (3, 1, 2), (1, 1, 0), (2, 0, 3)]
HOP_INNER = [(1, 1, 2), (2, 0, 1)]
HOP_SECOND = [(1, 0, 2), (2, 1, 1)]
HOP_OUTER = [(1, 0, 0), (2, 1, 3)]
HOP_THIRD = [(2, 0, 3), (1, 1, 0)]
BACK_THIRD, BACK_OUTER, BACK_MID, BACK_INNER, BACK_ONE = (
    [(to, c, z) for z, c, to in hops]
    for hops in (HOP_THIRD, HOP_OUTER, HOP_SECOND, HOP_INNER, HOP_ONE)
)

CHAIN = ((0, 1, 1, 0, 3, 2, 5, 4), (4, 5, 2, 3, 0, 1, 1, 0))


def summed(parts):
    return functools.reduce(jnp.add, [part.astype(jnp.float32) for part in parts])


def slot_copies(code, slot_at, refs, buffer, sems, act):
    for k, ref in enumerate(refs):

        @pl.when(slot_at == k)
        def _():
            copy = pltpu.make_async_copy(ref, buffer, sems)
            copy.start() if act else copy.wait()


def project_kernel(code, *refs):
    acts, weights = refs[:4], refs[4:-6]
    mine, theirs, acts_v, w_v, acts_sem, w_sem = refs[-6:]
    width = mine.shape[1]
    rows, features = acts[0].shape
    place = code[0]

    def weight_copies(act):
        for slot in range(2):
            slot_copies(
                code,
                code[1 + slot],
                weights,
                w_v.at[pl.ds(slot * width, width)],
                w_sem.at[slot],
                act,
            )

    weight_copies(True)
    tile = features // 3
    copies = []
    for n in range(3):
        lanes = pl.ds(n * tile, tile)
        for j in range(4):
            to = pl.ds(pl.multiple_of((place ^ j) * rows, rows), rows)
            copies.append(
                pltpu.make_async_copy(
                    acts[j].at[:, lanes], acts_v.at[to, lanes], acts_sem.at[4 * n + j]
                )
            )
    for copy in copies:
        copy.start()
    weight_copies(False)
    both = 0.0
    for n in range(3):
        lanes = slice(n * tile, (n + 1) * tile)
        for copy in copies[4 * n : 4 * n + 4]:
            copy.wait()
        both = both + lax.dot_general(
            acts_v[:, lanes], w_v[:, lanes], NT, preferred_element_type=jnp.float32
        )
    mine[...] = both[:, :width].astype(jnp.bfloat16)
    theirs[...] = both[:, width:].astype(jnp.bfloat16)


def project(code, acts, weights):
    rows, features = acts[0].shape
    width = weights[0].shape[0]
    return call(
        project_kernel,
        [shaped((4 * rows, width)), shaped((4 * rows, width))],
        12,
        2 * 4 * rows * features * 2 * width,
        4 * rows * features * 2 + 2 * width * features * 2,
        in_specs=[SMEM] + [HBM] * (4 + len(weights)),
        out_specs=[VMEM, VMEM],
        scratch_shapes=[
            pltpu.VMEM((4 * rows, features), jnp.bfloat16),
            pltpu.VMEM((2 * width, features), jnp.bfloat16),
            pltpu.SemaphoreType.DMA((12,)),
            pltpu.SemaphoreType.DMA((2,)),
        ],
        name="project",
    )(code, *acts, *weights)


def normalized(raw, gain, factor):
    inverse = lax.rsqrt(jnp.mean(raw * raw, axis=-1, keepdims=True) + epsilon)
    return raw * inverse * gain * factor


def normalized_pull(raw, gain, factor, cotangent):
    inverse = lax.rsqrt(jnp.mean(raw * raw, axis=-1, keepdims=True) + epsilon)
    scaled = cotangent * gain * factor
    along = jnp.mean(scaled * raw, axis=-1, keepdims=True)
    return inverse * (scaled - raw * (inverse * inverse * along))


def dot(a, b):
    return jnp.dot(a, b, preferred_element_type=jnp.float32)


def scores_kernel(
    code, q_ref, go_ref, own_ref, before_ref, key_mark, query_mark, gain_ref,
    e_ref, stat_ref, dv_own, dv_before, keys_v, acc
):
    block = pl.program_id(0)
    rows = q_ref.shape[1]
    chunks = e_ref.shape[2] // rows
    half = own_ref.shape[0]

    @pl.when(block == 0)
    def _():
        keys_v[:half, :HD] = before_ref[...]
        keys_v[half:, :HD] = own_ref[...]
        keys_v[:, HD:] = key_mark[...]
        acc[...] = jnp.zeros_like(acc)

    key_at = lax.broadcasted_iota(jnp.int32, (rows, rows), 0)
    query_at = lax.broadcasted_iota(jnp.int32, (rows, rows), 1)
    behind = key_at <= query_at
    stats = []
    for g in range(2):
        lanes = slice(g * HD, (g + 1) * HD)
        query = normalized(q_ref[0, :, lanes].astype(jnp.float32), gain_ref[...], query_scale)
        query_t = jnp.concatenate([query.T.astype(jnp.bfloat16), query_mark[...]], axis=0)
        total = jnp.zeros((1, rows), jnp.float32)
        for c in range(chunks):
            begin = pl.multiple_of((block + c) * rows, rows)
            e = jnp.exp(dot(keys_v[pl.ds(begin, rows), :], query_t))
            if c == 0:
                e = jnp.where(behind, 0.0, e)
            if c == chunks - 1:
                e = jnp.where(behind, e, 0.0)
            total = total + jnp.sum(e, axis=0, keepdims=True)
            e_ref[0, g, c * rows : (c + 1) * rows, :] = e.astype(jnp.bfloat16)
        inverse = 1.0 / total
        stats.append(inverse)
        grad = (go_ref[0, :, lanes].astype(jnp.float32).T * inverse).T.astype(jnp.bfloat16)
        span = pl.ds(pl.multiple_of(block * rows, rows), chunks * rows)
        acc[span, :] = acc[span, :] + dot(e_ref[0, g], grad)
    stat_ref[0] = jnp.concatenate(stats + [jnp.zeros((6, rows), jnp.float32)], axis=0)

    @pl.when(block == pl.num_programs(0) - 1)
    def _():
        dv_before[...] = acc[:half, :].astype(jnp.bfloat16)
        dv_own[...] = acc[half:, :]


def whole(shape):
    return pl.BlockSpec(shape, lambda b, code: (0,) * len(shape))


def attend_scores(code, q, go, keys, keys_before, key_mark, query_mark, gain):
    blocks, rows, _ = q.shape
    half = blocks * rows
    span = half + rows
    picked = pl.BlockSpec((1, rows, 2 * HD), lambda b, code: (b ^ code[0], 0, 0))
    return call(
        scores_kernel,
        [
            shaped((blocks, 2, span, rows)),
            shaped((blocks, 8, rows), jnp.float32),
            shaped((half, HD), jnp.float32),
            shaped((half, HD)),
        ],
        14,
        2 * 2 * half * span * 3 * HD,
        2 * half * span * 2 + 8 * half * HD * 2,
        grid_spec=pltpu.PrefetchScalarGridSpec(
            num_scalar_prefetch=1,
            grid=(blocks,),
            in_specs=[
                picked,
                picked,
                whole((half, HD)),
                whole((half, HD)),
                whole((2 * half, HD)),
                pl.BlockSpec((HD, rows), lambda b, code: (0, b)),
                whole((1, HD)),
            ],
            out_specs=[
                pl.BlockSpec((1, 2, span, rows), lambda b, code: (b, 0, 0, 0)),
                pl.BlockSpec((1, 8, rows), lambda b, code: (b, 0, 0)),
                whole((half, HD)),
                whole((half, HD)),
            ],
            scratch_shapes=[
                pltpu.VMEM((2 * half, 2 * HD), jnp.bfloat16),
                pltpu.VMEM((2 * half, HD), jnp.float32),
            ],
        ),
        name="attend_scores",
    )(code, q, go, keys, keys_before, key_mark, query_mark, gain)


def values_kernel(
    code, q_ref, go_ref, own_ref, before_ref, v_own, v_before, gain_ref, e_ref, stat_ref,
    out_ref, gq_ref, dk_own, dk_before, values_v, values_t, keys_t, acc
):
    block = pl.program_id(0)
    rows = q_ref.shape[1]
    span_rows = e_ref.shape[2]
    half = own_ref.shape[0]

    @pl.when(block == 0)
    def _():
        values_v[:half, :] = v_before[...]
        values_v[half:, :] = v_own[...]
        values_t[...] = values_v[...].astype(jnp.float32).T.astype(jnp.bfloat16)
        keys_t[:, :half] = before_ref[...].astype(jnp.float32).T.astype(jnp.bfloat16)
        keys_t[:, half:] = own_ref[...].astype(jnp.float32).T.astype(jnp.bfloat16)
        acc[...] = jnp.zeros_like(acc)

    span = pl.ds(pl.multiple_of(block * rows, rows), span_rows)
    for g in range(2):
        lanes = slice(g * HD, (g + 1) * HD)
        raw = q_ref[0, :, lanes].astype(jnp.float32)
        query = normalized(raw, gain_ref[...], query_scale).astype(jnp.bfloat16)
        inverse = stat_ref[0, g : g + 1, :]
        e = e_ref[0, g]
        out_t = dot(values_t[:, span], e) * inverse
        out_ref[0, :, lanes] = out_t.T.astype(jnp.bfloat16)
        grad_t = go_ref[0, :, lanes].astype(jnp.float32).T
        along = jnp.sum(out_t * grad_t, axis=0, keepdims=True) * inverse
        dprob = dot(values_v[span, :], (grad_t * inverse).astype(jnp.bfloat16))
        dscore = (e.astype(jnp.float32) * (dprob - along)).astype(jnp.bfloat16)
        acc[span, :] = acc[span, :] + dot(dscore, query)
        dquery = dot(keys_t[:, span], dscore).T
        gq_ref[0, :, lanes] = normalized_pull(raw, gain_ref[...], query_scale, dquery).astype(
            jnp.bfloat16
        )

    @pl.when(block == pl.num_programs(0) - 1)
    def _():
        dk_before[...] = acc[:half, :].astype(jnp.bfloat16)
        dk_own[...] = acc[half:, :]


def attend_values(code, q, go, keys, keys_before, values, values_before, gain, e, stat):
    blocks, rows, _ = q.shape
    half = blocks * rows
    span = half + rows
    picked = pl.BlockSpec((1, rows, 2 * HD), lambda b, code: (b ^ code[0], 0, 0))
    return call(
        values_kernel,
        [
            shaped(q.shape),
            shaped(q.shape),
            shaped((half, HD), jnp.float32),
            shaped((half, HD)),
        ],
        16,
        2 * 2 * half * span * 4 * HD,
        2 * half * span * 2 + 8 * half * HD * 2,
        grid_spec=pltpu.PrefetchScalarGridSpec(
            num_scalar_prefetch=1,
            grid=(blocks,),
            in_specs=[picked, picked]
            + [whole((half, HD))] * 4
            + [
                whole((1, HD)),
                pl.BlockSpec((1, 2, span, rows), lambda b, code: (b, 0, 0, 0)),
                pl.BlockSpec((1, 8, rows), lambda b, code: (b, 0, 0)),
            ],
            out_specs=[picked, picked, whole((half, HD)), whole((half, HD))],
            scratch_shapes=[
                pltpu.VMEM((2 * half, HD), jnp.bfloat16),
                pltpu.VMEM((HD, 2 * half), jnp.bfloat16),
                pltpu.VMEM((HD, 2 * half), jnp.bfloat16),
                pltpu.VMEM((2 * half, HD), jnp.float32),
            ],
        ),
        name="attend_values",
    )(code, q, go, keys, keys_before, values, values_before, gain, e, stat)


def weight_grad_kernel(code, mine, theirs, a0, a1, a2, a3, far, mid, acts_v, grad_v, acts_sem):
    acts = (a0, a1, a2, a3)
    rows, features = a0.shape
    width = far.shape[0]
    copies = [
        pltpu.make_async_copy(acts[j], acts_v.at[j], acts_sem.at[j]) for j in range(4)
    ]
    for copy in copies:
        copy.start()
    first = code[3] == 1
    for j in range(4):
        span = pl.ds(pl.multiple_of((code[0] ^ j) * rows, rows), rows)
        own = mine[span, :].astype(jnp.float32).T
        other = theirs[span, :].astype(jnp.float32).T
        grad_v[j, :width, :] = jnp.where(first, own, other).astype(jnp.bfloat16)
        grad_v[j, width:, :] = jnp.where(first, other, own).astype(jnp.bfloat16)
    for copy in copies:
        copy.wait()
    tile = features // 3
    for n in range(3):
        lanes = slice(n * tile, (n + 1) * tile)
        both = dot(grad_v[0], acts_v[0, :, lanes])
        for j in range(1, 4):
            both = both + dot(grad_v[j], acts_v[j, :, lanes])
        far[:, lanes] = both[:width].astype(jnp.bfloat16)
        mid[:, lanes] = both[width:].astype(jnp.bfloat16)


def weight_grad(code, mine, theirs, acts):
    rows, features = acts[0].shape
    width = mine.shape[1]
    return call(
        weight_grad_kernel,
        [shaped((width, features)), shaped((width, features))],
        12,
        0,
        0,
        in_specs=[SMEM, VMEM, VMEM] + [HBM] * 4,
        out_specs=[VMEM, VMEM],
        scratch_shapes=[
            pltpu.VMEM((4, rows, features), jnp.bfloat16),
            pltpu.VMEM((4, 2 * width, rows), jnp.bfloat16),
            pltpu.SemaphoreType.DMA((4,)),
        ],
        name="weight_grad",
    )(code, mine, theirs, *acts)


def input_grad_kernel(code, *refs):
    grads, key_w, value_w = refs[:4], refs[4:10], refs[10:16]
    kept, sent, w_v, w_sem = refs[16:]
    rows, features = kept.shape[1:]
    width = grads[0].shape[1]

    def weight_copies(act):
        for part, weights in enumerate((key_w, value_w)):
            for slot in range(2):
                row = 2 * part + slot
                slot_copies(
                    code, code[1 + slot], weights, w_v.at[pl.ds(row * width, width)], w_sem.at[row], act
                )

    weight_copies(True)
    weight_copies(False)
    tile = features // 3
    for j in (3, 1, 2, 0):
        span = pl.ds(pl.multiple_of((code[0] ^ j) * rows, rows), rows)
        grad = jnp.concatenate([ref[span, :] for ref in grads], axis=1)
        target = sent if j % 2 else kept
        for n in range(3):
            lanes = slice(n * tile, (n + 1) * tile)
            target[j // 2, :, lanes] = dot(grad, w_v[:, lanes]).astype(jnp.bfloat16)


def input_grad(code, grads, key_weights, value_weights, rows):
    width, features = key_weights[0].shape
    return call(
        input_grad_kernel,
        [shaped((2, rows, features)), shaped((2, rows, features))],
        16,
        2 * 4 * rows * features * 4 * width,
        4 * rows * features * 2 + 4 * width * features * 2,
        in_specs=[SMEM] + [VMEM] * 4 + [HBM] * 12,
        out_specs=[VMEM, VMEM],
        scratch_shapes=[
            pltpu.VMEM((4 * width, features), jnp.bfloat16),
            pltpu.SemaphoreType.DMA((4,)),
        ],
        name="input_grad",
    )(code, *grads, *key_weights, *value_weights)


def body_planes(normed, q_raw, key_weight, value_weight, q_gain, k_gain, segment_ids, grad_out):
    rows, features = normed.shape
    half = 4 * rows
    width = key_weight.shape[1]
    place = lax.axis_index("seq")
    uly = lax.axis_index("uly")
    z, x, c = place // 4, (place // 2) % 2, place % 2

    on_line = z * 2 + c
    chosen = [
        jnp.asarray(CHAIN, jnp.int32)[slot, on_line] for slot in (uly, 1 - uly)
    ]
    inner = (z == 1) | (z == 2)
    first_is_own = jnp.where(inner, c, 1 - c) == uly
    code = jnp.stack([place % 4, *chosen, first_is_own]).astype(jnp.int32)
    gain_q = q_gain.reshape(1, HD)

    def picked(first_is_low, low, high):
        return jnp.where(first_is_low, low, high)

    normed_x = swap_x(normed)

    def slab(weight):
        other = move(
            weight.T, [((z, x, 1 - z % 2), (z, x, z % 2)) for z in range(4) for x in (0, 1)]
        )
        both = (picked(c == 0, weight.T, other), picked(c == 0, other, weight.T))
        return jnp.concatenate(both, axis=0)

    key_slab = slab(key_weight)
    value_slab = slab(value_weight)

    k_one, k_inner = along_z(key_slab, HOP_ONE), along_z(key_slab, HOP_INNER)
    v_one, v_inner = along_z(value_slab, HOP_ONE), along_z(value_slab, HOP_INNER)
    normed_c = swap_core(after(normed, key_slab))
    k_second, k_outer = along_z(k_one, HOP_SECOND), along_z(k_inner, HOP_OUTER)
    v_one, v_inner = after_all((v_one, v_inner), k_one, k_inner)
    v_second, v_outer = along_z(v_one, HOP_SECOND), along_z(v_inner, HOP_OUTER)
    k_second, k_outer = after_all((k_second, k_outer), v_one, v_inner)
    k_third = along_z(k_second, HOP_THIRD)
    normed_x = after(normed_x, k_second, k_outer)
    normed_xc = swap_core(normed_x)

    def head(array, index):
        return array[:, index * 2 * HD : (index + 1) * 2 * HD]

    sources = after_all((q_raw, grad_out), normed_x)
    from_x = swap_x(
        jnp.stack([picked(x == 1, head(a, 2 * k), head(a, 2 * k + 1)) for a in sources for k in (0, 1)])
    )
    near = [picked(x == 0, head(a, 2 * k), head(a, 2 * k + 1)) for a in sources for k in (0, 1)]
    v_second, v_outer = after_all((v_second, v_outer), normed_x, k_second)
    v_third = along_z(v_second, HOP_THIRD)

    segments = after(segment_ids, v_second, v_outer)
    seg_pad = jnp.concatenate([jnp.full((half,), -1, jnp.int32), segments])
    key_seg = lax.dynamic_slice_in_dim(seg_pad, z * half, 2 * half, 0)
    query_seg = lax.dynamic_slice_in_dim(segments, z * half, half, 0)
    lane = lax.broadcasted_iota(jnp.int32, (2 * half, HD), 1)
    key_mark = jnp.where((lane < 2) & (lane != key_seg[:, None]), -MASKED, 0.0).astype(jnp.bfloat16)
    row = lax.broadcasted_iota(jnp.int32, (HD, half), 0)
    query_mark = jnp.where(row == query_seg[None, :], 1.0, 0.0).astype(jnp.bfloat16)

    forward = [(z, c, z + 1) for z in range(3) for c in (0, 1)]
    backward = [(z + 1, c, z) for z in range(3) for c in (0, 1)]

    acts = (normed, normed_c, normed_x, normed_xc)
    k_third = after(k_third, v_second, v_outer)
    key_weights = (key_slab, k_one, k_inner, k_second, k_outer, k_third)
    mine, theirs = project(code, acts, key_weights)
    key_far = swap_uly(theirs)
    from_x = after(from_x, theirs)
    arrays = [near[0], near[1], near[2], near[3], from_x[0], from_x[1], from_x[2], from_x[3]]
    from_core = swap_core(
        jnp.stack([picked(c == 1, arrays[2 * k], arrays[2 * k + 1]) for k in range(4)])
    )
    kept = [picked(c == 0, arrays[2 * k], arrays[2 * k + 1]) for k in range(4)]

    value_weights = (value_slab, v_one, v_inner, v_second, v_outer, after(v_third, theirs))
    value_mine, value_theirs = project(code, acts, value_weights)
    value_far = swap_uly(value_theirs)
    key_far = after(key_far, value_theirs)
    key_raw = mine.astype(jnp.float32) + key_far.astype(jnp.float32)
    keys = normalized(key_raw, k_gain, 1.0).astype(jnp.bfloat16)
    keys_before = along_z(keys, forward)
    value_far, from_core = after_all((value_far, from_core), keys)
    values = (value_mine.astype(jnp.float32) + value_far.astype(jnp.float32)).astype(jnp.bfloat16)
    values_before = along_z(values, forward)
    q = jnp.stack([kept[0], from_core[0], kept[2], from_core[2]])
    go = jnp.stack([kept[1], from_core[1], kept[3], from_core[3]])

    keys_before = after(keys_before, values)
    e, stat, dv_own, dv_before = attend_scores(
        code, q, go, keys, keys_before, key_mark, query_mark, gain_q
    )
    dv_back = along_z(dv_before, backward)
    values_before = after(values_before, e)
    out, gq, dk_own, dk_before = attend_values(
        code, q, go, keys, keys_before, values, values_before, gain_q, e, stat
    )
    dk_back = along_z(dk_before, backward)
    value_grad = (dv_own + after(dv_back, dk_own).astype(jnp.float32)).astype(jnp.bfloat16)
    value_grad_far = swap_uly(value_grad)

    out, gq = after_all((out, gq), value_grad)
    from_core = swap_core(jnp.stack([out[1], out[3], gq[1], gq[3]]))
    own_pairs = ((out[0], from_core[0]), (gq[0], from_core[2]))
    far_pairs = ((out[2], from_core[1]), (gq[2], from_core[3]))

    def by_core(pairs):
        return [picked((c == 0) == (k == 0), a, b) for a, b in pairs for k in (0, 1)]

    back_payload = jnp.stack(by_core(far_pairs))
    back_x = swap_x(back_payload)
    own_heads = by_core(own_pairs)

    dkey = dk_own + after(dk_back, back_payload).astype(jnp.float32)
    key_grad = normalized_pull(key_raw, k_gain, 1.0, dkey).astype(jnp.bfloat16)
    key_grad_far = swap_uly(key_grad)
    value_grad_far = after(value_grad_far, key_grad)

    v_first, v_second = weight_grad(code, value_grad, value_grad_far, acts)
    v_third, v_outer = along_z(v_second, BACK_THIRD), along_z(v_first, BACK_OUTER)
    key_grad_far = after(key_grad_far, v_first, back_x)
    grads = (key_grad, key_grad_far, value_grad, value_grad_far)
    kept, sent = input_grad(code, grads, key_weights, value_weights, rows)
    sent = swap_core(sent)
    key_grad_far = after(key_grad_far, kept)
    k_first, k_second = weight_grad(code, key_grad, key_grad_far, acts)
    k_third, k_outer = along_z(k_second, BACK_THIRD), along_z(k_first, BACK_OUTER)
    v_third, v_outer = after_all((v_third, v_outer), k_first)
    v_mid_payload, v_inner_payload = v_first + v_third, v_second + v_outer
    v_mid, v_inner = along_z(v_mid_payload, BACK_MID), along_z(v_inner_payload, BACK_INNER)
    sent = after(sent, v_mid_payload, v_inner_payload)
    away = (kept[1].astype(jnp.float32) + sent[1].astype(jnp.float32)).astype(jnp.bfloat16)
    from_x = swap_x(away)
    own_sum = kept[0].astype(jnp.float32) + sent[0].astype(jnp.float32)
    k_third, k_outer = after_all((k_third, k_outer), away)
    k_mid_payload, k_inner_payload = k_first + k_third, k_second + k_outer
    k_mid, k_inner = along_z(k_mid_payload, BACK_MID), along_z(k_inner_payload, BACK_INNER)
    v_mid, v_inner, own_sum, back_x = after_all(
        (v_mid, v_inner, own_sum, back_x), k_mid_payload, k_inner_payload
    )
    v_one_payload = v_first + v_mid
    v_one = along_z(v_one_payload, BACK_ONE)
    k_mid, k_inner = after_all((k_mid, k_inner), v_one_payload)
    k_one_payload = k_first + k_mid
    k_one = along_z(k_one_payload, BACK_ONE)

    def by_x(own, far, k):
        return [picked(x == 0, own[k], far[k]), picked(x == 0, far[k], own[k])]

    attention, grad_q = (
        jnp.concatenate(by_x(own_heads, back_x, k) + by_x(own_heads, back_x, k + 1), axis=1)
        for k in (0, 2)
    )
    def halves(total):
        own, away = (picked(c == k, total[:width], total[width:]) for k in (0, 1))
        other = move(
            away.astype(jnp.bfloat16),
            [((z, x, z % 2), (z, x, 1 - z % 2)) for z in range(4) for x in (0, 1)],
        )
        return own, other

    def owned(own, other):
        return jnp.where(c == z % 2, own, other.astype(jnp.float32)).T

    v_one, from_x = after_all((v_one, from_x), k_one_payload)
    value_sum, value_other = halves(summed((v_second, v_inner, v_one)))
    grad_normed = (own_sum + from_x.astype(jnp.float32)).astype(jnp.bfloat16)
    grad_value_weight = owned(value_sum, after(value_other, grad_normed))
    k_one = after(k_one, grad_value_weight, grad_normed, attention, grad_q)
    grad_key_weight = owned(*halves(summed((k_second, k_inner, k_one))))
    return (attention, grad_normed, grad_q, grad_key_weight, grad_value_weight)


def body(normed, q_raw, *rest):
    planes = (
        lax.axis_size("seq") == 16
        and lax.axis_size("uly") == 2
        and 4 * normed.shape[0] == WINDOW
        and q_raw.shape[1] == 8 * HD
    )
    return (body_planes if planes else body_general)(normed, q_raw, *rest)


def solution(mesh):
    return jax.shard_map(
        body,
        mesh=mesh,
        in_specs=(
            P("seq", "uly"),
            P("seq", "uly"),
            P("uly", "seq"),
            P("uly", "seq"),
            P(),
            P(),
            P(),
            P("seq", "uly"),
        ),
        out_specs=(
            P("seq", "uly"),
            P("seq", "uly"),
            P("seq", "uly"),
            P("uly", "seq"),
            P("uly", "seq"),
        ),
        check_vma=False,
    )
```

```python
import functools

import jax
import jax.numpy as jnp
from jax import lax
from jax.experimental import pallas as pl
from jax.experimental.pallas import tpu as pltpu
from jax.sharding import PartitionSpec as P

HD = 128
WINDOW = 1024


epsilon = 1e-06
query_scale = 168.0 ** (-0.5)


def from_behind(array, axis, by):
    devices = lax.axis_size(axis)
    pairs = [(i, i + by) for i in range(devices) if 0 <= i + by < devices]
    return lax.ppermute(array, axis, pairs)


def normalize(raw_vals, gain, factor):
    mean_sq = jnp.mean(raw_vals * raw_vals, axis=-1, keepdims=True)
    return raw_vals * lax.rsqrt(mean_sq + epsilon) * gain * factor


def attend_block(
    queries, key_block, value_block, grad_block, query_pos, key_pos, query_seg, key_seg
):
    scores = jnp.einsum("bhge,lhe->hgbl", queries, key_block, preferred_element_type=jnp.float32)
    allowed = (
        (key_pos[None, :] <= query_pos[:, None])
        & (key_pos[None, :] > query_pos[:, None] - WINDOW)
        & (key_seg[None, :] == query_seg[:, None])
    )
    exp_scores = jnp.where(allowed[None, None], jnp.exp(scores), 0.0)
    probs = exp_scores / jnp.sum(exp_scores, axis=-1, keepdims=True)
    weights = probs.astype(jnp.bfloat16)
    attended = jnp.einsum(
        "hgbl,lhe->bhge", weights, value_block, preferred_element_type=jnp.float32
    ).astype(jnp.bfloat16)
    dprob = jnp.einsum(
        "bhge,lhe->hgbl", grad_block, value_block, preferred_element_type=jnp.float32
    )
    delta_row = jnp.sum(probs * dprob, axis=-1, keepdims=True)
    dscore = (probs * (dprob - delta_row)).astype(jnp.bfloat16)
    dquery = jnp.einsum("hgbl,lhe->bhge", dscore, key_block, preferred_element_type=jnp.float32)
    dkey = jnp.einsum("hgbl,bhge->lhe", dscore, queries, preferred_element_type=jnp.float32)
    dvalue = jnp.einsum("hgbl,bhge->lhe", weights, grad_block, preferred_element_type=jnp.float32)
    return (attended, dquery, dkey, dvalue)


def body_general(normed, q_raw, key_weight, value_weight, q_gain, k_gain, segment_ids, grad_out):
    rows_here = normed.shape[0]
    heads_here = q_raw.shape[1] // (2 * HD)
    seq_index = lax.axis_index("seq")
    base_row = seq_index * rows_here
    weight_pair = (
        lax.all_gather(key_weight, "seq", axis=1, tiled=True),
        lax.all_gather(value_weight, "seq", axis=1, tiled=True),
    )
    key_term = jnp.dot(normed, weight_pair[0], preferred_element_type=jnp.float32)
    value_term = jnp.dot(normed, weight_pair[1], preferred_element_type=jnp.float32)
    key_raw, value_raw = (
        lax.psum_scatter(
            key_term.astype(jnp.bfloat16), "uly", scatter_dimension=1, tiled=True
        ).astype(jnp.float32),
        lax.psum_scatter(
            value_term.astype(jnp.bfloat16), "uly", scatter_dimension=1, tiled=True
        ).astype(jnp.float32),
    )
    key_in = key_raw.reshape(rows_here, heads_here, HD)
    keys_bf = normalize(key_in, k_gain, 1.0).astype(jnp.bfloat16)
    values_bf = value_raw.reshape(rows_here, heads_here, HD).astype(jnp.bfloat16)
    query_in = q_raw.astype(jnp.float32).reshape(rows_here, heads_here, 2, HD)
    queries = normalize(query_in, q_gain, query_scale).astype(jnp.bfloat16)
    grad_heads = grad_out.reshape(rows_here, heads_here, 2, HD)
    stacked = jnp.stack([keys_bf, values_bf])
    distance_most = -(-WINDOW // rows_here)
    pieces = []
    for distance in range(distance_most, 0, -1):
        first_row = max(0, distance * rows_here - WINDOW)
        pieces.append(from_behind(stacked, "seq", distance))
    pieces.append(stacked)
    extended = jnp.concatenate(pieces, axis=1)
    block_rows = min(512, rows_here)
    span_rows = block_rows + WINDOW
    count_blocks = rows_here // block_rows
    seg_pad = jnp.concatenate([jnp.full((WINDOW,), -1, jnp.int32), segment_ids])
    query_seg_all = lax.dynamic_slice_in_dim(segment_ids, base_row, rows_here, 0)
    key_seg_all = lax.dynamic_slice_in_dim(seg_pad, base_row, WINDOW + rows_here, 0)

    def step(grad_acc, block_index):
        begin_row = block_index * block_rows
        query_pos = base_row + begin_row + jnp.arange(block_rows, dtype=jnp.int32)
        key_pos = base_row + begin_row - WINDOW + jnp.arange(span_rows, dtype=jnp.int32)
        key_block = lax.dynamic_slice_in_dim(extended, begin_row, span_rows, 1)
        attended, dquery, dkey, dvalue = attend_block(
            lax.dynamic_slice_in_dim(queries, begin_row, block_rows, 0),
            key_block[0],
            key_block[1],
            lax.dynamic_slice_in_dim(grad_heads, begin_row, block_rows, 0),
            query_pos,
            key_pos,
            lax.dynamic_slice_in_dim(query_seg_all, begin_row, block_rows, 0),
            lax.dynamic_slice_in_dim(key_seg_all, begin_row, span_rows, 0),
        )
        update = jnp.stack([dkey, dvalue])
        grad_acc = lax.dynamic_update_slice_in_dim(
            grad_acc,
            lax.dynamic_slice_in_dim(grad_acc, begin_row, span_rows, 1) + update,
            begin_row,
            1,
        )
        return (grad_acc, (attended, dquery))

    zero_acc = jnp.zeros((2, WINDOW + rows_here, heads_here, HD), jnp.float32)
    grad_acc, (attended, dquery) = lax.scan(
        step, zero_acc, jnp.arange(count_blocks, dtype=jnp.int32)
    )
    attention = attended.reshape(rows_here, 2 * heads_here * HD)
    dquery = dquery.reshape(rows_here, heads_here, 2, HD)
    own_grads = grad_acc[:, WINDOW:]
    offset_row = 0
    for distance in range(distance_most, 0, -1):
        first_row = max(0, distance * rows_here - WINDOW)
        piece_rows = rows_here - first_row
        outgoing = grad_acc[:, offset_row : offset_row + piece_rows]
        returned = from_behind(outgoing.astype(jnp.bfloat16), "seq", -distance).astype(
            outgoing.dtype
        )
        own_grads = own_grads.at[:, first_row:].add(returned)
        offset_row = offset_row + piece_rows
    _, pull_query = jax.vjp(lambda raw_vals: normalize(raw_vals, q_gain, query_scale), query_in)
    grad_q = pull_query(dquery)[0].astype(jnp.bfloat16).reshape(rows_here, 2 * heads_here * HD)
    _, pull_key = jax.vjp(lambda raw_vals: normalize(raw_vals, k_gain, 1.0), key_in)
    key_grad = pull_key(own_grads[0])[0].astype(jnp.bfloat16).reshape(rows_here, heads_here * HD)
    value_grad = own_grads[1].astype(jnp.bfloat16).reshape(rows_here, heads_here * HD)
    key_all, value_all = (
        lax.all_gather(key_grad, "uly", axis=1, tiled=True),
        lax.all_gather(value_grad, "uly", axis=1, tiled=True),
    )
    dims_last = (((1,), (1,)), ((), ()))
    total = lax.dot_general(key_all, weight_pair[0], dims_last, preferred_element_type=jnp.float32)
    total = total + lax.dot_general(
        value_all, weight_pair[1], dims_last, preferred_element_type=jnp.float32
    )
    grad_normed = total.astype(jnp.bfloat16)
    dims_first = (((0,), (0,)), ((), ()))
    key_part = lax.dot_general(normed, key_all, dims_first, preferred_element_type=jnp.float32)
    value_part = lax.dot_general(normed, value_all, dims_first, preferred_element_type=jnp.float32)
    grad_key_weight = lax.psum_scatter(
        key_part.astype(jnp.bfloat16), "seq", scatter_dimension=1, tiled=True
    ).astype(jnp.float32)
    grad_value_weight = lax.psum_scatter(
        value_part.astype(jnp.bfloat16), "seq", scatter_dimension=1, tiled=True
    ).astype(jnp.float32)
    return (attention, grad_normed, grad_q, grad_key_weight, grad_value_weight)


MIB = 1 << 20
MASKED = 16384.0
NT = (((1,), (1,)), ((), ()))
HBM = pl.BlockSpec(memory_space=pltpu.HBM)
SMEM = pl.BlockSpec(memory_space=pltpu.SMEM)
VMEM = pl.BlockSpec(memory_space=pltpu.VMEM)


def at(z, x, c):
    return (z * 2 + x) * 2 + c


def move(array, rule):
    return lax.ppermute(array, "seq", [(at(*a), at(*b)) for a, b in rule])


def along_z(array, hops):
    return move(array, [((z, x, c), (to, x, c)) for z, c, to in hops for x in (0, 1)])


def swap_core(array):
    return move(
        array, [((z, x, c), (z, x, 1 - c)) for z in range(4) for x in (0, 1) for c in (0, 1)]
    )


def swap_x(array):
    return move(
        array, [((z, x, c), (z, 1 - x, c)) for z in range(4) for x in (0, 1) for c in (0, 1)]
    )


def swap_uly(array):
    return lax.ppermute(array, "uly", [(0, 1), (1, 0)])


def call(kernel, out_shape, vmem, flops=0, accessed=0, **rest):
    return pl.pallas_call(
        kernel,
        out_shape=out_shape,
        compiler_params=pltpu.CompilerParams(vmem_limit_bytes=vmem * MIB),
        cost_estimate=pl.CostEstimate(flops=flops, bytes_accessed=accessed, transcendentals=0),
        **rest,
    )


def shaped(shape, dtype=jnp.bfloat16):
    return jax.ShapeDtypeStruct(shape, dtype)


def after_all(arrays, *earlier):
    return lax.optimization_barrier(tuple(arrays) + earlier)[: len(arrays)]


def after(array, *earlier):
    return after_all((array,), *earlier)[0]


HOP_ONE = [(0, 0, 1), (3, 1, 2), (1, 1, 0), (2, 0, 3)]
HOP_INNER = [(1, 1, 2), (2, 0, 1)]
HOP_SECOND = [(1, 0, 2), (2, 1, 1)]
HOP_OUTER = [(1, 0, 0), (2, 1, 3)]
HOP_THIRD = [(2, 0, 3), (1, 1, 0)]
BACK_THIRD, BACK_OUTER, BACK_MID, BACK_INNER, BACK_ONE = (
    [(to, c, z) for z, c, to in hops]
    for hops in (HOP_THIRD, HOP_OUTER, HOP_SECOND, HOP_INNER, HOP_ONE)
)

CHAIN = ((0, 1, 1, 0, 3, 2, 5, 4), (4, 5, 2, 3, 0, 1, 1, 0))


def sums_kernel(counts, *refs):
    terms, outs = refs[: sum(counts)], refs[sum(counts) :]
    for out, count in zip(outs, counts):
        total = terms[0][...].astype(jnp.float32)
        for term in terms[1:count]:
            total = total + term[...].astype(jnp.float32)
        out[...] = total.astype(out.dtype)
        terms = terms[count:]


def sums(*groups):
    terms = [term for group in groups for term in group]
    return call(
        functools.partial(sums_kernel, [len(group) for group in groups]),
        [shaped(group[0].shape) for group in groups],
        12,
        in_specs=[VMEM] * len(terms),
        out_specs=[VMEM] * len(groups),
        name="sums",
    )(*terms)


def halves_kernel(code, a, b, c, own, away):
    width = own.shape[0]
    total = a[...].astype(jnp.float32) + b[...].astype(jnp.float32) + c[...].astype(jnp.float32)
    low = code[4] == 0
    own[...] = jnp.where(low, total[:width], total[width:])
    away[...] = jnp.where(low, total[width:], total[:width]).astype(jnp.bfloat16)


def halves(code, parts):
    width, features = parts[0].shape
    return call(
        halves_kernel,
        [shaped((width // 2, features), jnp.float32), shaped((width // 2, features))],
        12,
        in_specs=[SMEM] + [VMEM] * 3,
        out_specs=[VMEM] * 2,
        name="halves",
    )(code, *parts)


def owned_kernel(code, own, other, out):
    out[...] = jnp.where(code[6] == 1, own[...], other[...].astype(jnp.float32))


def owned(code, own, other):
    return call(
        owned_kernel,
        shaped(own.shape, jnp.float32),
        12,
        in_specs=[SMEM] + [VMEM] * 2,
        out_specs=VMEM,
        name="owned",
    )(code, own, other).T


def pack_kernel(first, second, out):
    out[0] = first[1]
    out[1] = second[1]


def pack(first, second):
    return call(
        pack_kernel, shaped(second.shape), 12, in_specs=[VMEM] * 2, out_specs=VMEM, name="pack"
    )(first, second)


def by_head_kernel(code, near, near_other, far, attention, grad_q):
    lanes = near.shape[3]
    core, x = code[4], code[5]
    for which, out in enumerate((attention, grad_q)):
        for k, side, source in (
            (core, x, near.at[0, which]),
            (1 - core, x, near_other.at[0, which]),
            (core, 1 - x, far.at[0, which]),
            (1 - core, 1 - x, far.at[1, which]),
        ):
            out[:, pl.ds(pl.multiple_of((2 * k + side) * lanes, lanes), lanes)] = source[...]


def by_head(code, near, near_other, far):
    _, _, rows, lanes = near.shape
    return call(
        by_head_kernel,
        [shaped((rows, 4 * lanes))] * 2,
        12,
        in_specs=[SMEM] + [VMEM] * 3,
        out_specs=[VMEM] * 2,
        name="by_head",
    )(code, near, near_other, far)


def slot_copies(code, slot_at, refs, buffer, sems, act):
    for k, ref in enumerate(refs):

        @pl.when(slot_at == k)
        def _():
            copy = pltpu.make_async_copy(ref, buffer, sems)
            copy.start() if act else copy.wait()


def project_kernel(code, *refs):
    acts, weights = refs[:4], refs[4:-6]
    mine, theirs, w_v, acts_v, acts_sem, w_sem = refs[-6:]
    width = mine.shape[1]
    rows, features = acts[0].shape
    place = code[0]

    def weight_copies(act):
        for slot in range(2):
            slot_copies(
                code,
                code[1 + slot],
                weights,
                w_v.at[pl.ds(slot * width, width)],
                w_sem.at[slot],
                act,
            )

    weight_copies(True)
    tile = features // 3
    copies = []
    for n in range(3):
        lanes = pl.ds(n * tile, tile)
        for j in range(4):
            to = pl.ds(pl.multiple_of((place ^ j) * rows, rows), rows)
            copies.append(
                pltpu.make_async_copy(
                    acts[j].at[:, lanes], acts_v.at[to, lanes], acts_sem.at[4 * n + j]
                )
            )
    for copy in copies:
        copy.start()
    weight_copies(False)
    both = 0.0
    for n in range(3):
        lanes = slice(n * tile, (n + 1) * tile)
        for copy in copies[4 * n : 4 * n + 4]:
            copy.wait()
        both = both + lax.dot_general(
            acts_v[:, lanes], w_v[:, lanes], NT, preferred_element_type=jnp.float32
        )
    mine[...] = both[:, :width].astype(jnp.bfloat16)
    theirs[...] = both[:, width:].astype(jnp.bfloat16)


def project(code, acts, weights):
    rows, features = acts[0].shape
    width = weights[0].shape[0]
    return call(
        project_kernel,
        [shaped((4 * rows, width)), shaped((4 * rows, width)), shaped((2 * width, features))],
        12,
        in_specs=[SMEM] + [HBM] * (4 + len(weights)),
        out_specs=[VMEM, VMEM, VMEM],
        scratch_shapes=[
            pltpu.VMEM((4 * rows, features), jnp.bfloat16),
            pltpu.SemaphoreType.DMA((12,)),
            pltpu.SemaphoreType.DMA((2,)),
        ],
        name="project",
    )(code, *acts, *weights)


def normalized(raw, gain, factor):
    inverse = lax.rsqrt(jnp.mean(raw * raw, axis=-1, keepdims=True) + epsilon)
    return raw * inverse * gain * factor


def normalized_pull(raw, gain, factor, cotangent):
    inverse = lax.rsqrt(jnp.mean(raw * raw, axis=-1, keepdims=True) + epsilon)
    scaled = cotangent * gain * factor
    along = jnp.mean(scaled * raw, axis=-1, keepdims=True)
    return inverse * (scaled - raw * (inverse * inverse * along))


def dot(a, b):
    return jnp.dot(a, b, preferred_element_type=jnp.float32)


def scores_kernel(
    code, q_ref, go_ref, own_ref, before_ref, key_mark, query_mark, gain_ref,
    e_ref, stat_ref, dv_own, dv_before, keys_v, acc
):
    block = pl.program_id(0)
    rows = q_ref.shape[1]
    chunks = e_ref.shape[2] // rows
    half = own_ref.shape[0]

    @pl.when(block == 0)
    def _():
        keys_v[:half, :HD] = before_ref[...]
        keys_v[half:, :HD] = own_ref[...]
        keys_v[:, HD:] = key_mark[...]
        acc[...] = jnp.zeros_like(acc)

    key_at = lax.broadcasted_iota(jnp.int32, (rows, rows), 0)
    query_at = lax.broadcasted_iota(jnp.int32, (rows, rows), 1)
    behind = key_at <= query_at
    stats = []
    for g in range(2):
        lanes = slice(g * HD, (g + 1) * HD)
        query = normalized(q_ref[0, :, lanes].astype(jnp.float32), gain_ref[...], query_scale)
        query_t = jnp.concatenate([query.T.astype(jnp.bfloat16), query_mark[...]], axis=0)
        total = jnp.zeros((1, rows), jnp.float32)
        for c in range(chunks):
            begin = pl.multiple_of((block + c) * rows, rows)
            e = jnp.exp(dot(keys_v[pl.ds(begin, rows), :], query_t))
            if c == 0:
                e = jnp.where(behind, 0.0, e)
            if c == chunks - 1:
                e = jnp.where(behind, e, 0.0)
            total = total + jnp.sum(e, axis=0, keepdims=True)
            e_ref[0, g, c * rows : (c + 1) * rows, :] = e.astype(jnp.bfloat16)
        inverse = 1.0 / total
        stats.append(inverse)
        grad = (go_ref[0, :, lanes].astype(jnp.float32).T * inverse).T.astype(jnp.bfloat16)
        span = pl.ds(pl.multiple_of(block * rows, rows), chunks * rows)
        acc[span, :] = acc[span, :] + dot(e_ref[0, g], grad)
    stat_ref[0] = jnp.concatenate(stats + [jnp.zeros((6, rows), jnp.float32)], axis=0)

    @pl.when(block == pl.num_programs(0) - 1)
    def _():
        dv_before[...] = acc[:half, :].astype(jnp.bfloat16)
        dv_own[...] = acc[half:, :]


def whole(shape):
    return pl.BlockSpec(shape, lambda b, code: (0,) * len(shape))


def attend_scores(code, q, go, keys, keys_before, key_mark, query_mark, gain):
    blocks, rows, _ = q.shape
    half = blocks * rows
    span = half + rows
    picked = pl.BlockSpec((1, rows, 2 * HD), lambda b, code: (b ^ code[0], 0, 0))
    return call(
        scores_kernel,
        [
            shaped((blocks, 2, span, rows)),
            shaped((blocks, 8, rows), jnp.float32),
            shaped((half, HD), jnp.float32),
            shaped((half, HD)),
        ],
        14,
        grid_spec=pltpu.PrefetchScalarGridSpec(
            num_scalar_prefetch=1,
            grid=(blocks,),
            in_specs=[
                picked,
                picked,
                whole((half, HD)),
                whole((half, HD)),
                whole((2 * half, HD)),
                pl.BlockSpec((HD, rows), lambda b, code: (0, b)),
                whole((1, HD)),
            ],
            out_specs=[
                pl.BlockSpec((1, 2, span, rows), lambda b, code: (b, 0, 0, 0)),
                pl.BlockSpec((1, 8, rows), lambda b, code: (b, 0, 0)),
                whole((half, HD)),
                whole((half, HD)),
            ],
            scratch_shapes=[
                pltpu.VMEM((2 * half, 2 * HD), jnp.bfloat16),
                pltpu.VMEM((2 * half, HD), jnp.float32),
            ],
        ),
        name="attend_scores",
    )(code, q, go, keys, keys_before, key_mark, query_mark, gain)


def values_kernel(
    code, q_ref, go_ref, own_ref, before_ref, v_own, v_before, gain_ref, e_ref, stat_ref,
    kept, sent, dk_own, dk_before, values_v, values_t, keys_t, acc
):
    block = pl.program_id(0)
    rows = q_ref.shape[1]
    span_rows = e_ref.shape[2]
    half = own_ref.shape[0]

    @pl.when(block == 0)
    def _():
        values_v[:half, :] = v_before[...]
        values_v[half:, :] = v_own[...]
        values_t[...] = values_v[...].astype(jnp.float32).T.astype(jnp.bfloat16)
        keys_t[:, :half] = before_ref[...].astype(jnp.float32).T.astype(jnp.bfloat16)
        keys_t[:, half:] = own_ref[...].astype(jnp.float32).T.astype(jnp.bfloat16)
        acc[...] = jnp.zeros_like(acc)

    piece = block ^ code[0]
    odd = (piece % 2 == 1) & jnp.ones((rows, HD), jnp.bool_)

    def put(which, lanes, result):
        for target, here in ((kept, ~odd), (sent, odd)):
            at_piece = target.at[piece // 2, which, :, lanes]
            at_piece[...] = jnp.where(here, result, at_piece[...])

    span = pl.ds(pl.multiple_of(block * rows, rows), span_rows)
    for g in range(2):
        lanes = slice(g * HD, (g + 1) * HD)
        raw = q_ref[0, :, lanes].astype(jnp.float32)
        query = normalized(raw, gain_ref[...], query_scale).astype(jnp.bfloat16)
        inverse = stat_ref[0, g : g + 1, :]
        e = e_ref[0, g]
        out_t = dot(values_t[:, span], e) * inverse
        put(0, lanes, out_t.T.astype(jnp.bfloat16))
        grad_t = go_ref[0, :, lanes].astype(jnp.float32).T
        along = jnp.sum(out_t * grad_t, axis=0, keepdims=True) * inverse
        dprob = dot(values_v[span, :], (grad_t * inverse).astype(jnp.bfloat16))
        dscore = (e.astype(jnp.float32) * (dprob - along)).astype(jnp.bfloat16)
        acc[span, :] = acc[span, :] + dot(dscore, query)
        dquery = dot(keys_t[:, span], dscore).T
        pulled = normalized_pull(raw, gain_ref[...], query_scale, dquery)
        put(1, lanes, pulled.astype(jnp.bfloat16))

    @pl.when(block == pl.num_programs(0) - 1)
    def _():
        dk_before[...] = acc[:half, :].astype(jnp.bfloat16)
        dk_own[...] = acc[half:, :]


def attend_values(code, q, go, keys, keys_before, values, values_before, gain, e, stat):
    blocks, rows, _ = q.shape
    half = blocks * rows
    span = half + rows
    picked = pl.BlockSpec((1, rows, 2 * HD), lambda b, code: (b ^ code[0], 0, 0))
    return call(
        values_kernel,
        [
            shaped((2, 2, rows, 2 * HD)),
            shaped((2, 2, rows, 2 * HD)),
            shaped((half, HD), jnp.float32),
            shaped((half, HD)),
        ],
        16,
        grid_spec=pltpu.PrefetchScalarGridSpec(
            num_scalar_prefetch=1,
            grid=(blocks,),
            in_specs=[picked, picked]
            + [whole((half, HD))] * 4
            + [
                whole((1, HD)),
                pl.BlockSpec((1, 2, span, rows), lambda b, code: (b, 0, 0, 0)),
                pl.BlockSpec((1, 8, rows), lambda b, code: (b, 0, 0)),
            ],
            out_specs=[
                whole((2, 2, rows, 2 * HD)),
                whole((2, 2, rows, 2 * HD)),
                whole((half, HD)),
                whole((half, HD)),
            ],
            scratch_shapes=[
                pltpu.VMEM((2 * half, HD), jnp.bfloat16),
                pltpu.VMEM((HD, 2 * half), jnp.bfloat16),
                pltpu.VMEM((HD, 2 * half), jnp.bfloat16),
                pltpu.VMEM((2 * half, HD), jnp.float32),
            ],
        ),
        name="attend_values",
    )(code, q, go, keys, keys_before, values, values_before, gain, e, stat)


def weight_grad_kernel(code, mine, theirs, a0, a1, a2, a3, far, mid, acts_v, grad_v, acts_sem):
    acts = (a0, a1, a2, a3)
    rows, features = a0.shape
    width = far.shape[0]
    copies = [
        pltpu.make_async_copy(acts[j], acts_v.at[j], acts_sem.at[j]) for j in range(4)
    ]
    for copy in copies:
        copy.start()
    first = code[3] == 1
    for j in range(4):
        span = pl.ds(pl.multiple_of((code[0] ^ j) * rows, rows), rows)
        own = mine[span, :].astype(jnp.float32).T
        other = theirs[span, :].astype(jnp.float32).T
        grad_v[j, :width, :] = jnp.where(first, own, other).astype(jnp.bfloat16)
        grad_v[j, width:, :] = jnp.where(first, other, own).astype(jnp.bfloat16)
    for copy in copies:
        copy.wait()
    tile = features // 3
    for n in range(3):
        lanes = slice(n * tile, (n + 1) * tile)
        both = dot(grad_v[0], acts_v[0, :, lanes])
        for j in range(1, 4):
            both = both + dot(grad_v[j], acts_v[j, :, lanes])
        far[:, lanes] = both[:width].astype(jnp.bfloat16)
        mid[:, lanes] = both[width:].astype(jnp.bfloat16)


def weight_grad(code, mine, theirs, acts):
    rows, features = acts[0].shape
    width = mine.shape[1]
    return call(
        weight_grad_kernel,
        [shaped((width, features)), shaped((width, features))],
        12,
        2 * 4 * rows * features * 2 * width,
        4 * rows * features * 2 + 2 * width * features * 2,
        in_specs=[SMEM, VMEM, VMEM] + [HBM] * 4,
        out_specs=[VMEM, VMEM],
        scratch_shapes=[
            pltpu.VMEM((4, rows, features), jnp.bfloat16),
            pltpu.VMEM((4, 2 * width, rows), jnp.bfloat16),
            pltpu.SemaphoreType.DMA((4,)),
        ],
        name="weight_grad",
    )(code, mine, theirs, *acts)


def input_grad_kernel(piece, code, *refs):
    grads, weights, out = refs[:8], refs[8:12], refs[12]
    rows = out.shape[0]
    span = pl.ds(pl.multiple_of((code[0] ^ piece) * rows, rows), rows)
    total = 0.0
    for k, weight in enumerate(weights):
        grad = jnp.concatenate([ref[span, :] for ref in grads[2 * k : 2 * k + 2]], axis=1)
        total = total + dot(grad, weight[...])
    out[...] = total.astype(jnp.bfloat16)


def input_grad(code, piece, grads, weights, rows):
    width, features = weights[0].shape
    tile = features // 3
    return call(
        functools.partial(input_grad_kernel, piece),
        shaped((rows, features)),
        16,
        grid=(3,),
        in_specs=[SMEM]
        + [pl.BlockSpec(grad.shape, lambda n: (0, 0)) for grad in grads]
        + [pl.BlockSpec((width, tile), lambda n: (0, n))] * 4,
        out_specs=pl.BlockSpec((rows, tile), lambda n: (0, n)),
        name="input_grad",
    )(code, *grads, *weights)


def body_planes(normed, q_raw, key_weight, value_weight, q_gain, k_gain, segment_ids, grad_out):
    rows, features = normed.shape
    half = 4 * rows
    width = key_weight.shape[1]
    place = lax.axis_index("seq")
    uly = lax.axis_index("uly")
    z, x, c = place // 4, (place // 2) % 2, place % 2

    on_line = z * 2 + c
    chosen = [
        jnp.asarray(CHAIN, jnp.int32)[slot, on_line] for slot in (uly, 1 - uly)
    ]
    inner = (z == 1) | (z == 2)
    first_is_own = jnp.where(inner, c, 1 - c) == uly
    code = jnp.stack([place % 4, *chosen, first_is_own, c, x, c == z % 2]).astype(jnp.int32)
    gain_q = q_gain.reshape(1, HD)

    def picked(first_is_low, low, high):
        return jnp.where(first_is_low, low, high)

    normed_x = swap_x(normed)

    def slab(weight):
        other = move(
            weight.T, [((z, x, 1 - z % 2), (z, x, z % 2)) for z in range(4) for x in (0, 1)]
        )
        both = (picked(c == 0, weight.T, other), picked(c == 0, other, weight.T))
        return jnp.concatenate(both, axis=0)

    key_slab = slab(key_weight)
    value_slab = slab(value_weight)

    k_one, k_inner = along_z(key_slab, HOP_ONE), along_z(key_slab, HOP_INNER)
    v_one, v_inner = along_z(value_slab, HOP_ONE), along_z(value_slab, HOP_INNER)
    normed_c = swap_core(after(normed, key_slab))
    k_second, k_outer = along_z(k_one, HOP_SECOND), along_z(k_inner, HOP_OUTER)
    v_one, v_inner = after_all((v_one, v_inner), k_one, k_inner)
    v_second, v_outer = along_z(v_one, HOP_SECOND), along_z(v_inner, HOP_OUTER)
    k_second, k_outer = after_all((k_second, k_outer), v_one, v_inner)
    k_third = along_z(k_second, HOP_THIRD)
    normed_x = after(normed_x, k_second, k_outer)
    normed_xc = swap_core(normed_x)

    def head(array, index):
        return array[:, index * 2 * HD : (index + 1) * 2 * HD]

    sources = after_all((q_raw, grad_out), normed_x)
    from_x = swap_x(
        jnp.stack([picked(x == 1, head(a, 2 * k), head(a, 2 * k + 1)) for a in sources for k in (0, 1)])
    )
    near = [picked(x == 0, head(a, 2 * k), head(a, 2 * k + 1)) for a in sources for k in (0, 1)]
    v_second, v_outer = after_all((v_second, v_outer), normed_x, k_second)
    v_third = along_z(v_second, HOP_THIRD)

    segments = after(segment_ids, v_second, v_outer)
    seg_pad = jnp.concatenate([jnp.full((half,), -1, jnp.int32), segments])
    key_seg = lax.dynamic_slice_in_dim(seg_pad, z * half, 2 * half, 0)
    query_seg = lax.dynamic_slice_in_dim(segments, z * half, half, 0)
    lane = lax.broadcasted_iota(jnp.int32, (2 * half, HD), 1)
    key_mark = jnp.where((lane < 2) & (lane != key_seg[:, None]), -MASKED, 0.0).astype(jnp.bfloat16)
    row = lax.broadcasted_iota(jnp.int32, (HD, half), 0)
    query_mark = jnp.where(row == query_seg[None, :], 1.0, 0.0).astype(jnp.bfloat16)

    forward = [(z, c, z + 1) for z in range(3) for c in (0, 1)]
    backward = [(z + 1, c, z) for z in range(3) for c in (0, 1)]

    acts = (normed, normed_c, normed_x, normed_xc)
    k_third = after(k_third, v_second, v_outer)
    key_weights = (key_slab, k_one, k_inner, k_second, k_outer, k_third)
    mine, theirs, key_w = project(code, acts, key_weights)
    key_far = swap_uly(theirs)
    from_x = after(from_x, theirs)
    arrays = [near[0], near[1], near[2], near[3], from_x[0], from_x[1], from_x[2], from_x[3]]
    from_core = swap_core(
        jnp.stack([picked(c == 1, arrays[2 * k], arrays[2 * k + 1]) for k in range(4)])
    )
    kept = [picked(c == 0, arrays[2 * k], arrays[2 * k + 1]) for k in range(4)]

    value_weights = (value_slab, v_one, v_inner, v_second, v_outer, after(v_third, theirs))
    value_mine, value_theirs, value_w = project(code, acts, value_weights)
    value_far = swap_uly(value_theirs)
    key_far = after(key_far, value_theirs)
    key_raw = mine.astype(jnp.float32) + key_far.astype(jnp.float32)
    keys = normalized(key_raw, k_gain, 1.0).astype(jnp.bfloat16)
    keys_before = along_z(keys, forward)
    value_far, from_core = after_all((value_far, from_core), keys)
    values = (value_mine.astype(jnp.float32) + value_far.astype(jnp.float32)).astype(jnp.bfloat16)
    values_before = along_z(values, forward)
    q = jnp.stack([kept[0], from_core[0], kept[2], from_core[2]])
    go = jnp.stack([kept[1], from_core[1], kept[3], from_core[3]])

    keys_before = after(keys_before, values)
    key_w_core, value_w_core = swap_core(key_w), swap_core(value_w)
    e, stat, dv_own, dv_before = attend_scores(
        code, q, go, keys, keys_before, key_mark, query_mark, gain_q
    )
    dv_back = along_z(dv_before, backward)
    values_before = after(values_before, e, key_w_core, value_w_core)
    near, sent_back, dk_own, dk_before = attend_values(
        code, q, go, keys, keys_before, values, values_before, gain_q, e, stat
    )
    dk_back = along_z(dk_before, backward)
    value_grad = (dv_own + after(dv_back, dk_own).astype(jnp.float32)).astype(jnp.bfloat16)
    value_grad_far = swap_uly(value_grad)

    near_other = swap_core(sent_back)
    far = pack(near, near_other)
    back_x = swap_x(far)

    v_first, v_second = weight_grad(code, value_grad, after(value_grad_far, far), acts)
    v_third, v_outer = along_z(v_second, BACK_THIRD), along_z(v_first, BACK_OUTER)
    dkey = dk_own + after(dk_back, v_first).astype(jnp.float32)
    key_grad = normalized_pull(key_raw, k_gain, 1.0, dkey).astype(jnp.bfloat16)
    key_grad_far = swap_uly(key_grad)
    grads = (key_grad, key_grad_far, value_grad, value_grad_far)
    grads_core = tuple(swap_core(grad) for grad in grads)
    k_first, k_second = weight_grad(code, key_grad, key_grad_far, acts)
    k_third = along_z(k_second, BACK_THIRD)
    back_x = after(back_x, k_first)
    grads = grads[:2] + after_all(grads_core[:2], back_x) + grads[2:] + grads_core[2:]
    weights = (key_w, key_w_core, value_w, value_w_core)
    away = input_grad(code, 2, grads, weights, rows)
    from_x = swap_x(away)
    v_third, v_outer = after_all((v_third, v_outer), away)
    v_mid_payload, v_inner_payload = sums((v_first, v_third), (v_second, v_outer))
    v_mid, v_inner = along_z(v_mid_payload, BACK_MID), along_z(v_inner_payload, BACK_INNER)
    key_grad_far = after(key_grad_far, v_mid_payload)
    kept = input_grad(code, 0, (key_grad, key_grad_far) + grads[2:], weights, rows)
    k_third = after(k_third, kept)
    (k_mid_payload,) = sums((k_first, k_third))
    k_mid, k_outer = along_z(k_mid_payload, BACK_MID), along_z(after(k_first, k_third), BACK_OUTER)
    v_mid, v_inner = after_all((v_mid, v_inner), k_mid_payload)
    (v_one_payload,) = sums((v_first, v_mid))
    v_one = along_z(v_one_payload, BACK_ONE)
    attention, grad_q = by_head(code, near, near_other, after(back_x, v_one_payload, v_inner))
    k_mid, k_outer = after_all((k_mid, k_outer), attention)
    k_one_payload, k_inner_payload = sums((k_first, k_mid), (k_second, k_outer))
    k_one, k_inner = along_z(k_one_payload, BACK_ONE), along_z(k_inner_payload, BACK_INNER)

    def to_core(away):
        return move(
            away, [((z, x, z % 2), (z, x, 1 - z % 2)) for z in range(4) for x in (0, 1)]
        )

    from_x = after(from_x, k_inner_payload)
    (grad_normed,) = sums((kept, from_x))
    v_one = after(v_one, grad_normed)
    value_own, value_away = halves(code, (v_second, v_inner, v_one))
    value_other = to_core(value_away)
    k_one, k_inner = after_all((k_one, k_inner), value_own)
    key_own, key_away = halves(code, (k_second, k_inner, k_one))
    key_other = to_core(key_away)
    grad_value_weight = owned(code, value_own, after(value_other, key_own))
    grad_key_weight = owned(code, key_own, after(key_other, grad_value_weight))
    return (attention, grad_normed, grad_q, grad_key_weight, grad_value_weight)


def body(normed, q_raw, *rest):
    planes = (
        lax.axis_size("seq") == 16
        and lax.axis_size("uly") == 2
        and 4 * normed.shape[0] == WINDOW
        and q_raw.shape[1] == 8 * HD
    )
    return (body_planes if planes else body_general)(normed, q_raw, *rest)


def solution(mesh):
    return jax.shard_map(
        body,
        mesh=mesh,
        in_specs=(
            P("seq", "uly"),
            P("seq", "uly"),
            P("uly", "seq"),
            P("uly", "seq"),
            P(),
            P(),
            P(),
            P("seq", "uly"),
        ),
        out_specs=(
            P("seq", "uly"),
            P("seq", "uly"),
            P("seq", "uly"),
            P("uly", "seq"),
            P("uly", "seq"),
        ),
        check_vma=False,
    )
```

```python
import functools

import jax
import jax.numpy as jnp
from jax import lax
from jax.experimental import pallas as pl
from jax.experimental.pallas import tpu as pltpu
from jax.sharding import PartitionSpec as P

HD = 128
WINDOW = 1024


epsilon = 1e-06
query_scale = 168.0 ** (-0.5)


def from_behind(array, axis, by):
    devices = lax.axis_size(axis)
    pairs = [(i, i + by) for i in range(devices) if 0 <= i + by < devices]
    return lax.ppermute(array, axis, pairs)


def normalize(raw_vals, gain, factor):
    mean_sq = jnp.mean(raw_vals * raw_vals, axis=-1, keepdims=True)
    return raw_vals * lax.rsqrt(mean_sq + epsilon) * gain * factor


def attend_block(
    queries, key_block, value_block, grad_block, query_pos, key_pos, query_seg, key_seg
):
    scores = jnp.einsum("bhge,lhe->hgbl", queries, key_block, preferred_element_type=jnp.float32)
    allowed = (
        (key_pos[None, :] <= query_pos[:, None])
        & (key_pos[None, :] > query_pos[:, None] - WINDOW)
        & (key_seg[None, :] == query_seg[:, None])
    )
    exp_scores = jnp.where(allowed[None, None], jnp.exp(scores), 0.0)
    probs = exp_scores / jnp.sum(exp_scores, axis=-1, keepdims=True)
    weights = probs.astype(jnp.bfloat16)
    attended = jnp.einsum(
        "hgbl,lhe->bhge", weights, value_block, preferred_element_type=jnp.float32
    ).astype(jnp.bfloat16)
    dprob = jnp.einsum(
        "bhge,lhe->hgbl", grad_block, value_block, preferred_element_type=jnp.float32
    )
    delta_row = jnp.sum(probs * dprob, axis=-1, keepdims=True)
    dscore = (probs * (dprob - delta_row)).astype(jnp.bfloat16)
    dquery = jnp.einsum("hgbl,lhe->bhge", dscore, key_block, preferred_element_type=jnp.float32)
    dkey = jnp.einsum("hgbl,bhge->lhe", dscore, queries, preferred_element_type=jnp.float32)
    dvalue = jnp.einsum("hgbl,bhge->lhe", weights, grad_block, preferred_element_type=jnp.float32)
    return (attended, dquery, dkey, dvalue)


def body_general(normed, q_raw, key_weight, value_weight, q_gain, k_gain, segment_ids, grad_out):
    rows_here = normed.shape[0]
    heads_here = q_raw.shape[1] // (2 * HD)
    seq_index = lax.axis_index("seq")
    base_row = seq_index * rows_here
    weight_pair = (
        lax.all_gather(key_weight, "seq", axis=1, tiled=True),
        lax.all_gather(value_weight, "seq", axis=1, tiled=True),
    )
    key_term = jnp.dot(normed, weight_pair[0], preferred_element_type=jnp.float32)
    value_term = jnp.dot(normed, weight_pair[1], preferred_element_type=jnp.float32)
    key_raw, value_raw = (
        lax.psum_scatter(
            key_term.astype(jnp.bfloat16), "uly", scatter_dimension=1, tiled=True
        ).astype(jnp.float32),
        lax.psum_scatter(
            value_term.astype(jnp.bfloat16), "uly", scatter_dimension=1, tiled=True
        ).astype(jnp.float32),
    )
    key_in = key_raw.reshape(rows_here, heads_here, HD)
    keys_bf = normalize(key_in, k_gain, 1.0).astype(jnp.bfloat16)
    values_bf = value_raw.reshape(rows_here, heads_here, HD).astype(jnp.bfloat16)
    query_in = q_raw.astype(jnp.float32).reshape(rows_here, heads_here, 2, HD)
    queries = normalize(query_in, q_gain, query_scale).astype(jnp.bfloat16)
    grad_heads = grad_out.reshape(rows_here, heads_here, 2, HD)
    stacked = jnp.stack([keys_bf, values_bf])
    distance_most = -(-WINDOW // rows_here)
    pieces = []
    for distance in range(distance_most, 0, -1):
        first_row = max(0, distance * rows_here - WINDOW)
        pieces.append(from_behind(stacked, "seq", distance))
    pieces.append(stacked)
    extended = jnp.concatenate(pieces, axis=1)
    block_rows = min(512, rows_here)
    span_rows = block_rows + WINDOW
    count_blocks = rows_here // block_rows
    seg_pad = jnp.concatenate([jnp.full((WINDOW,), -1, jnp.int32), segment_ids])
    query_seg_all = lax.dynamic_slice_in_dim(segment_ids, base_row, rows_here, 0)
    key_seg_all = lax.dynamic_slice_in_dim(seg_pad, base_row, WINDOW + rows_here, 0)

    def step(grad_acc, block_index):
        begin_row = block_index * block_rows
        query_pos = base_row + begin_row + jnp.arange(block_rows, dtype=jnp.int32)
        key_pos = base_row + begin_row - WINDOW + jnp.arange(span_rows, dtype=jnp.int32)
        key_block = lax.dynamic_slice_in_dim(extended, begin_row, span_rows, 1)
        attended, dquery, dkey, dvalue = attend_block(
            lax.dynamic_slice_in_dim(queries, begin_row, block_rows, 0),
            key_block[0],
            key_block[1],
            lax.dynamic_slice_in_dim(grad_heads, begin_row, block_rows, 0),
            query_pos,
            key_pos,
            lax.dynamic_slice_in_dim(query_seg_all, begin_row, block_rows, 0),
            lax.dynamic_slice_in_dim(key_seg_all, begin_row, span_rows, 0),
        )
        update = jnp.stack([dkey, dvalue])
        grad_acc = lax.dynamic_update_slice_in_dim(
            grad_acc,
            lax.dynamic_slice_in_dim(grad_acc, begin_row, span_rows, 1) + update,
            begin_row,
            1,
        )
        return (grad_acc, (attended, dquery))

    zero_acc = jnp.zeros((2, WINDOW + rows_here, heads_here, HD), jnp.float32)
    grad_acc, (attended, dquery) = lax.scan(
        step, zero_acc, jnp.arange(count_blocks, dtype=jnp.int32)
    )
    attention = attended.reshape(rows_here, 2 * heads_here * HD)
    dquery = dquery.reshape(rows_here, heads_here, 2, HD)
    own_grads = grad_acc[:, WINDOW:]
    offset_row = 0
    for distance in range(distance_most, 0, -1):
        first_row = max(0, distance * rows_here - WINDOW)
        piece_rows = rows_here - first_row
        outgoing = grad_acc[:, offset_row : offset_row + piece_rows]
        returned = from_behind(outgoing.astype(jnp.bfloat16), "seq", -distance).astype(
            outgoing.dtype
        )
        own_grads = own_grads.at[:, first_row:].add(returned)
        offset_row = offset_row + piece_rows
    _, pull_query = jax.vjp(lambda raw_vals: normalize(raw_vals, q_gain, query_scale), query_in)
    grad_q = pull_query(dquery)[0].astype(jnp.bfloat16).reshape(rows_here, 2 * heads_here * HD)
    _, pull_key = jax.vjp(lambda raw_vals: normalize(raw_vals, k_gain, 1.0), key_in)
    key_grad = pull_key(own_grads[0])[0].astype(jnp.bfloat16).reshape(rows_here, heads_here * HD)
    value_grad = own_grads[1].astype(jnp.bfloat16).reshape(rows_here, heads_here * HD)
    key_all, value_all = (
        lax.all_gather(key_grad, "uly", axis=1, tiled=True),
        lax.all_gather(value_grad, "uly", axis=1, tiled=True),
    )
    dims_last = (((1,), (1,)), ((), ()))
    total = lax.dot_general(key_all, weight_pair[0], dims_last, preferred_element_type=jnp.float32)
    total = total + lax.dot_general(
        value_all, weight_pair[1], dims_last, preferred_element_type=jnp.float32
    )
    grad_normed = total.astype(jnp.bfloat16)
    dims_first = (((0,), (0,)), ((), ()))
    key_part = lax.dot_general(normed, key_all, dims_first, preferred_element_type=jnp.float32)
    value_part = lax.dot_general(normed, value_all, dims_first, preferred_element_type=jnp.float32)
    grad_key_weight = lax.psum_scatter(
        key_part.astype(jnp.bfloat16), "seq", scatter_dimension=1, tiled=True
    ).astype(jnp.float32)
    grad_value_weight = lax.psum_scatter(
        value_part.astype(jnp.bfloat16), "seq", scatter_dimension=1, tiled=True
    ).astype(jnp.float32)
    return (attention, grad_normed, grad_q, grad_key_weight, grad_value_weight)


MIB = 1 << 20
MASKED = 16384.0
NT = (((1,), (1,)), ((), ()))
HBM = pl.BlockSpec(memory_space=pltpu.HBM)
SMEM = pl.BlockSpec(memory_space=pltpu.SMEM)
VMEM = pl.BlockSpec(memory_space=pltpu.VMEM)


def at(z, x, c):
    return (z * 2 + x) * 2 + c


def move(array, rule):
    return lax.ppermute(array, "seq", [(at(*a), at(*b)) for a, b in rule])


def along_z(array, hops):
    return move(array, [((z, x, c), (to, x, c)) for z, c, to in hops for x in (0, 1)])


def swap_core(array):
    return move(
        array, [((z, x, c), (z, x, 1 - c)) for z in range(4) for x in (0, 1) for c in (0, 1)]
    )


def swap_x(array):
    return move(
        array, [((z, x, c), (z, 1 - x, c)) for z in range(4) for x in (0, 1) for c in (0, 1)]
    )


def swap_uly(array):
    return lax.ppermute(array, "uly", [(0, 1), (1, 0)])


def call(kernel, out_shape, vmem, flops=0, accessed=0, **rest):
    return pl.pallas_call(
        kernel,
        out_shape=out_shape,
        compiler_params=pltpu.CompilerParams(vmem_limit_bytes=vmem * MIB),
        cost_estimate=pl.CostEstimate(flops=flops, bytes_accessed=accessed, transcendentals=0),
        **rest,
    )


def shaped(shape, dtype=jnp.bfloat16):
    return jax.ShapeDtypeStruct(shape, dtype)


def after_all(arrays, *earlier):
    return lax.optimization_barrier(tuple(arrays) + earlier)[: len(arrays)]


def after(array, *earlier):
    return after_all((array,), *earlier)[0]


HOP_ONE = [(0, 0, 1), (3, 1, 2), (1, 1, 0), (2, 0, 3)]
HOP_INNER = [(1, 1, 2), (2, 0, 1)]
HOP_SECOND = [(1, 0, 2), (2, 1, 1)]
HOP_OUTER = [(1, 0, 0), (2, 1, 3)]
HOP_THIRD = [(2, 0, 3), (1, 1, 0)]
BACK_THIRD, BACK_OUTER, BACK_MID, BACK_INNER, BACK_ONE = (
    [(to, c, z) for z, c, to in hops]
    for hops in (HOP_THIRD, HOP_OUTER, HOP_SECOND, HOP_INNER, HOP_ONE)
)

CHAIN = ((0, 1, 1, 0, 3, 2, 5, 4), (4, 5, 2, 3, 0, 1, 1, 0))


def sums_kernel(counts, *refs):
    terms, outs = refs[: sum(counts)], refs[sum(counts) :]
    for out, count in zip(outs, counts):
        total = terms[0][...].astype(jnp.float32)
        for term in terms[1:count]:
            total = total + term[...].astype(jnp.float32)
        out[...] = total.astype(out.dtype)
        terms = terms[count:]


def sums(*groups):
    terms = [term for group in groups for term in group]
    return call(
        functools.partial(sums_kernel, [len(group) for group in groups]),
        [shaped(group[0].shape) for group in groups],
        12,
        in_specs=[VMEM] * len(terms),
        out_specs=[VMEM] * len(groups),
        name="sums",
    )(*terms)


def halves_kernel(code, a, b, c, own, away):
    width = own.shape[0]
    total = a[...].astype(jnp.float32) + b[...].astype(jnp.float32) + c[...].astype(jnp.float32)
    low = code[4] == 0
    own[...] = jnp.where(low, total[:width], total[width:])
    away[...] = jnp.where(low, total[width:], total[:width]).astype(jnp.bfloat16)


def halves(code, parts):
    width, features = parts[0].shape
    return call(
        halves_kernel,
        [shaped((width // 2, features), jnp.float32), shaped((width // 2, features))],
        12,
        in_specs=[SMEM] + [VMEM] * 3,
        out_specs=[VMEM] * 2,
        name="halves",
    )(code, *parts)


def owned_kernel(code, own, other, out):
    out[...] = jnp.where(code[6] == 1, own[...], other[...].astype(jnp.float32))


def owned(code, own, other):
    return call(
        owned_kernel,
        shaped(own.shape, jnp.float32),
        12,
        in_specs=[SMEM] + [VMEM] * 2,
        out_specs=VMEM,
        name="owned",
    )(code, own, other).T


def pack_kernel(first, second, out):
    out[0] = first[1]
    out[1] = second[1]


def pack(first, second):
    return call(
        pack_kernel, shaped(second.shape), 12, in_specs=[VMEM] * 2, out_specs=VMEM, name="pack"
    )(first, second)


def by_head_kernel(code, near, near_other, far, attention, grad_q):
    lanes = near.shape[3]
    core, x = code[4], code[5]
    for which, out in enumerate((attention, grad_q)):
        for k, side, source in (
            (core, x, near.at[0, which]),
            (1 - core, x, near_other.at[0, which]),
            (core, 1 - x, far.at[0, which]),
            (1 - core, 1 - x, far.at[1, which]),
        ):
            out[:, pl.ds(pl.multiple_of((2 * k + side) * lanes, lanes), lanes)] = source[...]


def by_head(code, near, near_other, far):
    _, _, rows, lanes = near.shape
    return call(
        by_head_kernel,
        [shaped((rows, 4 * lanes))] * 2,
        12,
        in_specs=[SMEM] + [VMEM] * 3,
        out_specs=[VMEM] * 2,
        name="by_head",
    )(code, near, near_other, far)


def slot_copies(code, slot_at, refs, buffer, sems, act):
    for k, ref in enumerate(refs):

        @pl.when(slot_at == k)
        def _():
            copy = pltpu.make_async_copy(ref, buffer, sems)
            copy.start() if act else copy.wait()


def project_kernel(code, *refs):
    acts, weights = refs[:4], refs[4:-4]
    mine, theirs, w_v, w_sem = refs[-4:]
    width = mine.shape[1]
    rows = acts[0].shape[0]

    def weight_copies(act):
        for slot in range(2):
            slot_copies(
                code, code[1 + slot], weights, w_v.at[pl.ds(slot * width, width)], w_sem.at[slot], act
            )

    weight_copies(True)
    weight_copies(False)
    for j in range(4):
        here = pl.ds(pl.multiple_of((code[0] ^ j) * rows, rows), rows)
        both = lax.dot_general(acts[j][...], w_v[...], NT, preferred_element_type=jnp.float32)
        mine[here, :] = both[:, :width].astype(jnp.bfloat16)
        theirs[here, :] = both[:, width:].astype(jnp.bfloat16)


def project(code, acts, weights):
    rows, features = acts[0].shape
    width = weights[0].shape[0]
    return call(
        project_kernel,
        [shaped((4 * rows, width)), shaped((4 * rows, width)), shaped((2 * width, features))],
        12,
        in_specs=[SMEM] + [VMEM] * 4 + [HBM] * len(weights),
        out_specs=[VMEM, VMEM, VMEM],
        scratch_shapes=[
            pltpu.SemaphoreType.DMA((2,)),
        ],
        name="project",
    )(code, *acts, *weights)


def normalized(raw, gain, factor):
    inverse = lax.rsqrt(jnp.mean(raw * raw, axis=-1, keepdims=True) + epsilon)
    return raw * inverse * gain * factor


def normalized_pull(raw, gain, factor, cotangent):
    inverse = lax.rsqrt(jnp.mean(raw * raw, axis=-1, keepdims=True) + epsilon)
    scaled = cotangent * gain * factor
    along = jnp.mean(scaled * raw, axis=-1, keepdims=True)
    return inverse * (scaled - raw * (inverse * inverse * along))


def dot(a, b):
    return jnp.dot(a, b, preferred_element_type=jnp.float32)


def scores_kernel(
    code, q_ref, go_ref, own_ref, before_ref, key_mark, query_mark, gain_ref,
    e_ref, stat_ref, dv_own, dv_before, keys_v, acc
):
    block = pl.program_id(0)
    rows = q_ref.shape[1]
    chunks = e_ref.shape[1] // rows
    half = own_ref.shape[0]

    @pl.when(block == 0)
    def _():
        keys_v[:half, :HD] = before_ref[...]
        keys_v[half:, :HD] = own_ref[...]
        keys_v[:, HD:] = key_mark[...]
        acc[...] = jnp.zeros_like(acc)

    key_at = lax.broadcasted_iota(jnp.int32, (rows, 2 * rows), 0)
    query_at = lax.broadcasted_iota(jnp.int32, (rows, 2 * rows), 1)
    behind = key_at <= jnp.where(query_at >= rows, query_at - rows, query_at)
    heads, grads = [], []
    for g in range(2):
        lanes = slice(g * HD, (g + 1) * HD)
        query = normalized(q_ref[0, :, lanes].astype(jnp.float32), gain_ref[...], query_scale)
        heads.append(jnp.concatenate([query.T.astype(jnp.bfloat16), query_mark[...]], axis=0))
        grads.append(go_ref[0, :, lanes].astype(jnp.float32).T)
    query_t = jnp.concatenate(heads, axis=1)
    total = jnp.zeros((1, 2 * rows), jnp.float32)
    es = []
    for c in range(chunks):
        begin = pl.multiple_of((block + c) * rows, rows)
        e = jnp.exp(dot(keys_v[pl.ds(begin, rows), :], query_t))
        if c == 0:
            e = jnp.where(behind, 0.0, e)
        if c == chunks - 1:
            e = jnp.where(behind, e, 0.0)
        total = total + jnp.sum(e, axis=0, keepdims=True)
        es.append(e.astype(jnp.bfloat16))
        e_ref[0, c * rows : (c + 1) * rows, :] = es[-1]
    inverse = 1.0 / total
    stat_ref[0] = jnp.broadcast_to(inverse, stat_ref.shape[1:])
    grad = (jnp.concatenate(grads, axis=1) * inverse).T.astype(jnp.bfloat16)
    for c in range(chunks):
        span = pl.ds(pl.multiple_of((block + c) * rows, rows), rows)
        acc[span, :] = acc[span, :] + dot(es[c], grad)

    @pl.when(block == pl.num_programs(0) - 1)
    def _():
        dv_before[...] = acc[:half, :].astype(jnp.bfloat16)
        dv_own[...] = acc[half:, :]


def whole(shape):
    return pl.BlockSpec(shape, lambda b, code: (0,) * len(shape))


def attend_scores(code, q, go, keys, keys_before, key_mark, query_mark, gain):
    blocks, rows, _ = q.shape
    half = blocks * rows
    span = half + rows
    picked = pl.BlockSpec((1, rows, 2 * HD), lambda b, code: (b ^ code[0], 0, 0))
    return call(
        scores_kernel,
        [
            shaped((blocks, span, 2 * rows)),
            shaped((blocks, 8, 2 * rows), jnp.float32),
            shaped((half, HD), jnp.float32),
            shaped((half, HD)),
        ],
        14,
        grid_spec=pltpu.PrefetchScalarGridSpec(
            num_scalar_prefetch=1,
            grid=(blocks,),
            in_specs=[
                picked,
                picked,
                whole((half, HD)),
                whole((half, HD)),
                whole((2 * half, HD)),
                pl.BlockSpec((HD, rows), lambda b, code: (0, b)),
                whole((1, HD)),
            ],
            out_specs=[
                pl.BlockSpec((1, span, 2 * rows), lambda b, code: (b, 0, 0)),
                pl.BlockSpec((1, 8, 2 * rows), lambda b, code: (b, 0, 0)),
                whole((half, HD)),
                whole((half, HD)),
            ],
            scratch_shapes=[
                pltpu.VMEM((2 * half, 2 * HD), jnp.bfloat16),
                pltpu.VMEM((2 * half, HD), jnp.float32),
            ],
        ),
        name="attend_scores",
    )(code, q, go, keys, keys_before, key_mark, query_mark, gain)


def values_kernel(
    code, q_ref, go_ref, own_ref, before_ref, v_own, v_before, gain_ref, e_ref, stat_ref,
    kept, sent, dk_own, dk_before, values_v, values_t, keys_t, acc
):
    block = pl.program_id(0)
    rows = q_ref.shape[1]
    span_rows = e_ref.shape[1]
    half = own_ref.shape[0]

    @pl.when(block == 0)
    def _():
        values_v[:half, :] = v_before[...]
        values_v[half:, :] = v_own[...]
        values_t[...] = values_v[...].astype(jnp.float32).T.astype(jnp.bfloat16)
        keys_t[:, :half] = before_ref[...].astype(jnp.float32).T.astype(jnp.bfloat16)
        keys_t[:, half:] = own_ref[...].astype(jnp.float32).T.astype(jnp.bfloat16)
        acc[...] = jnp.zeros_like(acc)

    piece = block ^ code[0]
    odd = (piece % 2 == 1) & jnp.ones((rows, HD), jnp.bool_)

    def put(which, lanes, result):
        for target, here in ((kept, ~odd), (sent, odd)):
            at_piece = target.at[piece // 2, which, :, lanes]
            at_piece[...] = jnp.where(here, result, at_piece[...])

    span = pl.ds(pl.multiple_of(block * rows, rows), span_rows)
    raws = [q_ref[0, :, g * HD : (g + 1) * HD].astype(jnp.float32) for g in range(2)]
    queries = jnp.concatenate(
        [normalized(raw, gain_ref[...], query_scale).astype(jnp.bfloat16) for raw in raws], axis=0
    )
    grad_t = jnp.concatenate(
        [go_ref[0, :, g * HD : (g + 1) * HD].astype(jnp.float32).T for g in range(2)], axis=1
    )
    inverse = stat_ref[0, :1, :]
    e = e_ref[0]
    out_t = dot(values_t[:, span], e) * inverse
    along = jnp.sum(out_t * grad_t, axis=0, keepdims=True) * inverse
    scaled = (grad_t * inverse).astype(jnp.bfloat16)
    parts = []
    for c in range(span_rows // rows):
        here = pl.ds(pl.multiple_of((block + c) * rows, rows), rows)
        dprob = dot(values_v[here, :], scaled)
        dscore = e[c * rows : (c + 1) * rows] * (dprob - along).astype(jnp.bfloat16)
        acc[here, :] = acc[here, :] + dot(dscore, queries)
        parts.append(dscore)
    dquery_t = dot(keys_t[:, span], jnp.concatenate(parts, axis=0))
    for g in range(2):
        lanes = slice(g * HD, (g + 1) * HD)
        across = slice(g * rows, (g + 1) * rows)
        put(0, lanes, out_t[:, across].T.astype(jnp.bfloat16))
        pulled = normalized_pull(raws[g], gain_ref[...], query_scale, dquery_t[:, across].T)
        put(1, lanes, pulled.astype(jnp.bfloat16))

    @pl.when(block == pl.num_programs(0) - 1)
    def _():
        dk_before[...] = acc[:half, :].astype(jnp.bfloat16)
        dk_own[...] = acc[half:, :]


def attend_values(code, q, go, keys, keys_before, values, values_before, gain, e, stat):
    blocks, rows, _ = q.shape
    half = blocks * rows
    span = half + rows
    picked = pl.BlockSpec((1, rows, 2 * HD), lambda b, code: (b ^ code[0], 0, 0))
    return call(
        values_kernel,
        [
            shaped((2, 2, rows, 2 * HD)),
            shaped((2, 2, rows, 2 * HD)),
            shaped((half, HD), jnp.float32),
            shaped((half, HD)),
        ],
        16,
        grid_spec=pltpu.PrefetchScalarGridSpec(
            num_scalar_prefetch=1,
            grid=(blocks,),
            in_specs=[picked, picked]
            + [whole((half, HD))] * 4
            + [
                whole((1, HD)),
                pl.BlockSpec((1, span, 2 * rows), lambda b, code: (b, 0, 0)),
                pl.BlockSpec((1, 8, 2 * rows), lambda b, code: (b, 0, 0)),
            ],
            out_specs=[
                whole((2, 2, rows, 2 * HD)),
                whole((2, 2, rows, 2 * HD)),
                whole((half, HD)),
                whole((half, HD)),
            ],
            scratch_shapes=[
                pltpu.VMEM((2 * half, HD), jnp.bfloat16),
                pltpu.VMEM((HD, 2 * half), jnp.bfloat16),
                pltpu.VMEM((HD, 2 * half), jnp.bfloat16),
                pltpu.VMEM((2 * half, HD), jnp.float32),
            ],
        ),
        name="attend_values",
    )(code, q, go, keys, keys_before, values, values_before, gain, e, stat)


def weight_grad_kernel(code, mine, theirs, a0, a1, a2, a3, far, mid):
    acts = (a0, a1, a2, a3)
    rows, features = a0.shape
    width = far.shape[0]
    first = code[3] == 1
    grads = []
    for j in range(4):
        span = pl.ds(pl.multiple_of((code[0] ^ j) * rows, rows), rows)
        own = mine[span, :].astype(jnp.float32).T
        other = theirs[span, :].astype(jnp.float32).T
        both = (jnp.where(first, own, other), jnp.where(first, other, own))
        grads.append(jnp.concatenate(both, axis=0).astype(jnp.bfloat16))
    tile = features // 3
    for n in range(3):
        lanes = slice(n * tile, (n + 1) * tile)
        both = dot(grads[0], acts[0][:, lanes])
        for j in range(1, 4):
            both = both + dot(grads[j], acts[j][:, lanes])
        far[:, lanes] = both[:width].astype(jnp.bfloat16)
        mid[:, lanes] = both[width:].astype(jnp.bfloat16)


def weight_grad(code, mine, theirs, acts):
    rows, features = acts[0].shape
    width = mine.shape[1]
    return call(
        weight_grad_kernel,
        [shaped((width, features)), shaped((width, features))],
        12,
        2 * 4 * rows * features * 2 * width,
        4 * rows * features * 2 + 2 * width * features * 2,
        in_specs=[SMEM] + [VMEM] * 6,
        out_specs=[VMEM, VMEM],
        name="weight_grad",
    )(code, mine, theirs, *acts)


def input_grad_kernel(piece, code, *refs):
    grads, weights, out = refs[:8], refs[8:12], refs[12]
    rows, features = out.shape
    span = pl.ds(pl.multiple_of((code[0] ^ piece) * rows, rows), rows)
    parts = [
        jnp.concatenate([ref[span, :] for ref in grads[2 * k : 2 * k + 2]], axis=1) for k in range(4)
    ]
    tile = features // 3
    for n in range(3):
        lanes = slice(n * tile, (n + 1) * tile)
        total = dot(parts[0], weights[0][:, lanes])
        for k in range(1, 4):
            total = total + dot(parts[k], weights[k][:, lanes])
        out[:, lanes] = total.astype(jnp.bfloat16)


def input_grad(code, piece, grads, weights, rows):
    features = weights[0].shape[1]
    return call(
        functools.partial(input_grad_kernel, piece),
        shaped((rows, features)),
        16,
        in_specs=[SMEM] + [VMEM] * 12,
        out_specs=VMEM,
        name="input_grad",
    )(code, *grads, *weights)


def body_planes(normed, q_raw, key_weight, value_weight, q_gain, k_gain, segment_ids, grad_out):
    rows, features = normed.shape
    half = 4 * rows
    width = key_weight.shape[1]
    place = lax.axis_index("seq")
    uly = lax.axis_index("uly")
    z, x, c = place // 4, (place // 2) % 2, place % 2

    on_line = z * 2 + c
    chosen = [
        jnp.asarray(CHAIN, jnp.int32)[slot, on_line] for slot in (uly, 1 - uly)
    ]
    inner = (z == 1) | (z == 2)
    first_is_own = jnp.where(inner, c, 1 - c) == uly
    code = jnp.stack([place % 4, *chosen, first_is_own, c, x, c == z % 2]).astype(jnp.int32)
    gain_q = q_gain.reshape(1, HD)

    def picked(first_is_low, low, high):
        return jnp.where(first_is_low, low, high)

    normed_x = swap_x(normed)

    def slab(weight):
        other = move(
            weight.T, [((z, x, 1 - z % 2), (z, x, z % 2)) for z in range(4) for x in (0, 1)]
        )
        both = (picked(c == 0, weight.T, other), picked(c == 0, other, weight.T))
        return jnp.concatenate(both, axis=0)

    key_slab = slab(key_weight)
    value_slab = slab(value_weight)

    k_one, k_inner = along_z(key_slab, HOP_ONE), along_z(key_slab, HOP_INNER)
    v_one, v_inner = along_z(value_slab, HOP_ONE), along_z(value_slab, HOP_INNER)
    normed_c = swap_core(after(normed, key_slab))
    k_one, k_inner = after_all((k_one, k_inner), code)
    k_second, k_outer = along_z(k_one, HOP_SECOND), along_z(k_inner, HOP_OUTER)
    v_one, v_inner = after_all((v_one, v_inner), k_one, k_inner)
    v_second, v_outer = along_z(v_one, HOP_SECOND), along_z(v_inner, HOP_OUTER)
    k_second, k_outer = after_all((k_second, k_outer), v_one, v_inner)
    k_third = along_z(k_second, HOP_THIRD)
    normed_x = after(normed_x, k_second, k_outer)
    normed_xc = swap_core(normed_x)

    def head(array, index):
        return array[:, index * 2 * HD : (index + 1) * 2 * HD]

    sources = after_all((q_raw, grad_out), normed_x)
    from_x = swap_x(
        jnp.stack([picked(x == 1, head(a, 2 * k), head(a, 2 * k + 1)) for a in sources for k in (0, 1)])
    )
    near = [picked(x == 0, head(a, 2 * k), head(a, 2 * k + 1)) for a in sources for k in (0, 1)]
    v_second, v_outer = after_all((v_second, v_outer), normed_x, k_second)
    v_third = along_z(v_second, HOP_THIRD)

    segments = after(segment_ids, v_second, v_outer)
    seg_pad = jnp.concatenate([jnp.full((half,), -1, jnp.int32), segments])
    key_seg = lax.dynamic_slice_in_dim(seg_pad, z * half, 2 * half, 0)
    query_seg = lax.dynamic_slice_in_dim(segments, z * half, half, 0)
    lane = lax.broadcasted_iota(jnp.int32, (2 * half, HD), 1)
    key_mark = jnp.where((lane < 2) & (lane != key_seg[:, None]), -MASKED, 0.0).astype(jnp.bfloat16)
    row = lax.broadcasted_iota(jnp.int32, (HD, half), 0)
    query_mark = jnp.where(row == query_seg[None, :], 1.0, 0.0).astype(jnp.bfloat16)

    forward = [(z, c, z + 1) for z in range(3) for c in (0, 1)]
    backward = [(z + 1, c, z) for z in range(3) for c in (0, 1)]

    acts = (normed, normed_c, normed_x, normed_xc)
    k_third = after(k_third, v_second, v_outer)
    key_weights = (key_slab, k_one, k_inner, k_second, k_outer, k_third)
    mine, theirs, key_w = project(code, acts, key_weights)
    key_far = swap_uly(theirs)
    from_x = after(from_x, theirs)
    arrays = [near[0], near[1], near[2], near[3], from_x[0], from_x[1], from_x[2], from_x[3]]
    from_core = swap_core(
        jnp.stack([picked(c == 1, arrays[2 * k], arrays[2 * k + 1]) for k in range(4)])
    )
    kept = [picked(c == 0, arrays[2 * k], arrays[2 * k + 1]) for k in range(4)]

    value_weights = (value_slab, v_one, v_inner, v_second, v_outer, after(v_third, theirs))
    value_mine, value_theirs, value_w = project(code, acts, value_weights)
    value_far = swap_uly(value_theirs)
    key_far = after(key_far, value_theirs)
    key_raw = mine.astype(jnp.float32) + key_far.astype(jnp.float32)
    keys = normalized(key_raw, k_gain, 1.0).astype(jnp.bfloat16)
    keys_before = along_z(keys, forward)
    value_far, from_core = after_all((value_far, from_core), keys)
    values = (value_mine.astype(jnp.float32) + value_far.astype(jnp.float32)).astype(jnp.bfloat16)
    values_before = along_z(values, forward)
    q = jnp.stack([kept[0], from_core[0], kept[2], from_core[2]])
    go = jnp.stack([kept[1], from_core[1], kept[3], from_core[3]])

    keys_before = after(keys_before, values)
    key_w_core, value_w_core = swap_core(key_w), swap_core(value_w)
    e, stat, dv_own, dv_before = attend_scores(
        code, q, go, keys, keys_before, key_mark, query_mark, gain_q
    )
    dv_back = along_z(dv_before, backward)
    values_before = after(values_before, e, key_w_core, value_w_core)
    near, sent_back, dk_own, dk_before = attend_values(
        code, q, go, keys, keys_before, values, values_before, gain_q, e, stat
    )
    dk_back = along_z(dk_before, backward)
    value_grad = (dv_own + after(dv_back, dk_own).astype(jnp.float32)).astype(jnp.bfloat16)
    value_grad_far = swap_uly(value_grad)

    near_other = swap_core(sent_back)
    far = pack(near, near_other)
    back_x = swap_x(far)

    v_first, v_second = weight_grad(code, value_grad, after(value_grad_far, far), acts)
    v_third, v_outer = along_z(v_second, BACK_THIRD), along_z(v_first, BACK_OUTER)
    dkey = dk_own + after(dk_back, v_first).astype(jnp.float32)
    key_grad = normalized_pull(key_raw, k_gain, 1.0, dkey).astype(jnp.bfloat16)
    key_grad_far = swap_uly(key_grad)
    grads = (key_grad, key_grad_far, value_grad, value_grad_far)
    grads_core = tuple(swap_core(grad) for grad in grads)
    k_first, k_second = weight_grad(code, key_grad, key_grad_far, acts)
    k_third = along_z(k_second, BACK_THIRD)
    back_x = after(back_x, k_first)
    grads = grads[:2] + after_all(grads_core[:2], back_x) + grads[2:] + grads_core[2:]
    weights = (key_w, key_w_core, value_w, value_w_core)
    away = input_grad(code, 2, grads, weights, rows)
    from_x = swap_x(away)
    v_third, v_outer = after_all((v_third, v_outer), away)
    v_mid_payload, v_inner_payload = sums((v_first, v_third), (v_second, v_outer))
    v_mid, v_inner = along_z(v_mid_payload, BACK_MID), along_z(v_inner_payload, BACK_INNER)
    k_third = after(k_third, v_mid_payload)
    (k_mid_payload,) = sums((k_first, k_third))
    key_grad_far = after(key_grad_far, k_mid_payload)
    kept = input_grad(code, 0, (key_grad, key_grad_far) + grads[2:], weights, rows)
    k_mid, k_outer = along_z(k_mid_payload, BACK_MID), along_z(after(k_first, k_third), BACK_OUTER)
    v_mid, v_inner = after_all((v_mid, v_inner), kept)
    (v_one_payload,) = sums((v_first, v_mid))
    v_one = along_z(v_one_payload, BACK_ONE)
    attention, grad_q = by_head(code, near, near_other, after(back_x, v_one_payload, v_inner))
    k_mid, k_outer = after_all((k_mid, k_outer), attention)
    k_one_payload, k_inner_payload = sums((k_first, k_mid), (k_second, k_outer))
    k_one, k_inner = along_z(k_one_payload, BACK_ONE), along_z(k_inner_payload, BACK_INNER)

    def to_core(away):
        return move(
            away, [((z, x, z % 2), (z, x, 1 - z % 2)) for z in range(4) for x in (0, 1)]
        )

    from_x = after(from_x, k_inner_payload)
    (grad_normed,) = sums((kept, from_x))
    v_one = after(v_one, grad_normed)
    value_own, value_away = halves(code, (v_second, v_inner, v_one))
    grad_value_weight = owned(code, value_own, to_core(value_away))
    k_one, k_inner = after_all((k_one, k_inner), grad_value_weight)
    key_own, key_away = halves(code, (k_second, k_inner, k_one))
    grad_key_weight = owned(code, key_own, to_core(key_away))
    return (attention, grad_normed, grad_q, grad_key_weight, grad_value_weight)


def body(normed, q_raw, *rest):
    planes = (
        lax.axis_size("seq") == 16
        and lax.axis_size("uly") == 2
        and 4 * normed.shape[0] == WINDOW
        and q_raw.shape[1] == 8 * HD
    )
    return (body_planes if planes else body_general)(normed, q_raw, *rest)


def solution(mesh):
    return jax.shard_map(
        body,
        mesh=mesh,
        in_specs=(
            P("seq", "uly"),
            P("seq", "uly"),
            P("uly", "seq"),
            P("uly", "seq"),
            P(),
            P(),
            P(),
            P("seq", "uly"),
        ),
        out_specs=(
            P("seq", "uly"),
            P("seq", "uly"),
            P("seq", "uly"),
            P("uly", "seq"),
            P("uly", "seq"),
        ),
        check_vma=False,
    )
```

```python
import functools

import jax
import jax.numpy as jnp
from jax import lax
from jax.experimental import pallas as pl
from jax.experimental.pallas import tpu as pltpu
from jax.sharding import PartitionSpec as P

HD = 128
WINDOW = 1024


epsilon = 1e-06
query_scale = 168.0 ** (-0.5)


def from_behind(array, axis, by):
    devices = lax.axis_size(axis)
    pairs = [(i, i + by) for i in range(devices) if 0 <= i + by < devices]
    return lax.ppermute(array, axis, pairs)


def normalize(raw_vals, gain, factor):
    mean_sq = jnp.mean(raw_vals * raw_vals, axis=-1, keepdims=True)
    return raw_vals * lax.rsqrt(mean_sq + epsilon) * gain * factor


def attend_block(
    queries, key_block, value_block, grad_block, query_pos, key_pos, query_seg, key_seg
):
    scores = jnp.einsum("bhge,lhe->hgbl", queries, key_block, preferred_element_type=jnp.float32)
    allowed = (
        (key_pos[None, :] <= query_pos[:, None])
        & (key_pos[None, :] > query_pos[:, None] - WINDOW)
        & (key_seg[None, :] == query_seg[:, None])
    )
    exp_scores = jnp.where(allowed[None, None], jnp.exp(scores), 0.0)
    probs = exp_scores / jnp.sum(exp_scores, axis=-1, keepdims=True)
    weights = probs.astype(jnp.bfloat16)
    attended = jnp.einsum(
        "hgbl,lhe->bhge", weights, value_block, preferred_element_type=jnp.float32
    ).astype(jnp.bfloat16)
    dprob = jnp.einsum(
        "bhge,lhe->hgbl", grad_block, value_block, preferred_element_type=jnp.float32
    )
    delta_row = jnp.sum(probs * dprob, axis=-1, keepdims=True)
    dscore = (probs * (dprob - delta_row)).astype(jnp.bfloat16)
    dquery = jnp.einsum("hgbl,lhe->bhge", dscore, key_block, preferred_element_type=jnp.float32)
    dkey = jnp.einsum("hgbl,bhge->lhe", dscore, queries, preferred_element_type=jnp.float32)
    dvalue = jnp.einsum("hgbl,bhge->lhe", weights, grad_block, preferred_element_type=jnp.float32)
    return (attended, dquery, dkey, dvalue)


def body_general(normed, q_raw, key_weight, value_weight, q_gain, k_gain, segment_ids, grad_out):
    rows_here = normed.shape[0]
    heads_here = q_raw.shape[1] // (2 * HD)
    seq_index = lax.axis_index("seq")
    base_row = seq_index * rows_here
    weight_pair = (
        lax.all_gather(key_weight, "seq", axis=1, tiled=True),
        lax.all_gather(value_weight, "seq", axis=1, tiled=True),
    )
    key_term = jnp.dot(normed, weight_pair[0], preferred_element_type=jnp.float32)
    value_term = jnp.dot(normed, weight_pair[1], preferred_element_type=jnp.float32)
    key_raw, value_raw = (
        lax.psum_scatter(
            key_term.astype(jnp.bfloat16), "uly", scatter_dimension=1, tiled=True
        ).astype(jnp.float32),
        lax.psum_scatter(
            value_term.astype(jnp.bfloat16), "uly", scatter_dimension=1, tiled=True
        ).astype(jnp.float32),
    )
    key_in = key_raw.reshape(rows_here, heads_here, HD)
    keys_bf = normalize(key_in, k_gain, 1.0).astype(jnp.bfloat16)
    values_bf = value_raw.reshape(rows_here, heads_here, HD).astype(jnp.bfloat16)
    query_in = q_raw.astype(jnp.float32).reshape(rows_here, heads_here, 2, HD)
    queries = normalize(query_in, q_gain, query_scale).astype(jnp.bfloat16)
    grad_heads = grad_out.reshape(rows_here, heads_here, 2, HD)
    stacked = jnp.stack([keys_bf, values_bf])
    distance_most = -(-WINDOW // rows_here)
    pieces = []
    for distance in range(distance_most, 0, -1):
        first_row = max(0, distance * rows_here - WINDOW)
        pieces.append(from_behind(stacked, "seq", distance))
    pieces.append(stacked)
    extended = jnp.concatenate(pieces, axis=1)
    block_rows = min(512, rows_here)
    span_rows = block_rows + WINDOW
    count_blocks = rows_here // block_rows
    seg_pad = jnp.concatenate([jnp.full((WINDOW,), -1, jnp.int32), segment_ids])
    query_seg_all = lax.dynamic_slice_in_dim(segment_ids, base_row, rows_here, 0)
    key_seg_all = lax.dynamic_slice_in_dim(seg_pad, base_row, WINDOW + rows_here, 0)

    def step(grad_acc, block_index):
        begin_row = block_index * block_rows
        query_pos = base_row + begin_row + jnp.arange(block_rows, dtype=jnp.int32)
        key_pos = base_row + begin_row - WINDOW + jnp.arange(span_rows, dtype=jnp.int32)
        key_block = lax.dynamic_slice_in_dim(extended, begin_row, span_rows, 1)
        attended, dquery, dkey, dvalue = attend_block(
            lax.dynamic_slice_in_dim(queries, begin_row, block_rows, 0),
            key_block[0],
            key_block[1],
            lax.dynamic_slice_in_dim(grad_heads, begin_row, block_rows, 0),
            query_pos,
            key_pos,
            lax.dynamic_slice_in_dim(query_seg_all, begin_row, block_rows, 0),
            lax.dynamic_slice_in_dim(key_seg_all, begin_row, span_rows, 0),
        )
        update = jnp.stack([dkey, dvalue])
        grad_acc = lax.dynamic_update_slice_in_dim(
            grad_acc,
            lax.dynamic_slice_in_dim(grad_acc, begin_row, span_rows, 1) + update,
            begin_row,
            1,
        )
        return (grad_acc, (attended, dquery))

    zero_acc = jnp.zeros((2, WINDOW + rows_here, heads_here, HD), jnp.float32)
    grad_acc, (attended, dquery) = lax.scan(
        step, zero_acc, jnp.arange(count_blocks, dtype=jnp.int32)
    )
    attention = attended.reshape(rows_here, 2 * heads_here * HD)
    dquery = dquery.reshape(rows_here, heads_here, 2, HD)
    own_grads = grad_acc[:, WINDOW:]
    offset_row = 0
    for distance in range(distance_most, 0, -1):
        first_row = max(0, distance * rows_here - WINDOW)
        piece_rows = rows_here - first_row
        outgoing = grad_acc[:, offset_row : offset_row + piece_rows]
        returned = from_behind(outgoing.astype(jnp.bfloat16), "seq", -distance).astype(
            outgoing.dtype
        )
        own_grads = own_grads.at[:, first_row:].add(returned)
        offset_row = offset_row + piece_rows
    _, pull_query = jax.vjp(lambda raw_vals: normalize(raw_vals, q_gain, query_scale), query_in)
    grad_q = pull_query(dquery)[0].astype(jnp.bfloat16).reshape(rows_here, 2 * heads_here * HD)
    _, pull_key = jax.vjp(lambda raw_vals: normalize(raw_vals, k_gain, 1.0), key_in)
    key_grad = pull_key(own_grads[0])[0].astype(jnp.bfloat16).reshape(rows_here, heads_here * HD)
    value_grad = own_grads[1].astype(jnp.bfloat16).reshape(rows_here, heads_here * HD)
    key_all, value_all = (
        lax.all_gather(key_grad, "uly", axis=1, tiled=True),
        lax.all_gather(value_grad, "uly", axis=1, tiled=True),
    )
    dims_last = (((1,), (1,)), ((), ()))
    total = lax.dot_general(key_all, weight_pair[0], dims_last, preferred_element_type=jnp.float32)
    total = total + lax.dot_general(
        value_all, weight_pair[1], dims_last, preferred_element_type=jnp.float32
    )
    grad_normed = total.astype(jnp.bfloat16)
    dims_first = (((0,), (0,)), ((), ()))
    key_part = lax.dot_general(normed, key_all, dims_first, preferred_element_type=jnp.float32)
    value_part = lax.dot_general(normed, value_all, dims_first, preferred_element_type=jnp.float32)
    grad_key_weight = lax.psum_scatter(
        key_part.astype(jnp.bfloat16), "seq", scatter_dimension=1, tiled=True
    ).astype(jnp.float32)
    grad_value_weight = lax.psum_scatter(
        value_part.astype(jnp.bfloat16), "seq", scatter_dimension=1, tiled=True
    ).astype(jnp.float32)
    return (attention, grad_normed, grad_q, grad_key_weight, grad_value_weight)


MIB = 1 << 20
MASKED = 16384.0
NT = (((1,), (1,)), ((), ()))
HBM = pl.BlockSpec(memory_space=pltpu.HBM)
SMEM = pl.BlockSpec(memory_space=pltpu.SMEM)
VMEM = pl.BlockSpec(memory_space=pltpu.VMEM)


def at(z, x, c):
    return (z * 2 + x) * 2 + c


def move(array, rule):
    return lax.ppermute(array, "seq", [(at(*a), at(*b)) for a, b in rule])


def along_z(array, hops):
    return move(array, [((z, x, c), (to, x, c)) for z, c, to in hops for x in (0, 1)])


def swap_core(array):
    return move(
        array, [((z, x, c), (z, x, 1 - c)) for z in range(4) for x in (0, 1) for c in (0, 1)]
    )


def swap_x(array):
    return move(
        array, [((z, x, c), (z, 1 - x, c)) for z in range(4) for x in (0, 1) for c in (0, 1)]
    )


def swap_uly(array):
    return lax.ppermute(array, "uly", [(0, 1), (1, 0)])


def call(kernel, out_shape, vmem, flops=0, accessed=0, **rest):
    return pl.pallas_call(
        kernel,
        out_shape=out_shape,
        compiler_params=pltpu.CompilerParams(vmem_limit_bytes=vmem * MIB),
        cost_estimate=pl.CostEstimate(flops=flops, bytes_accessed=accessed, transcendentals=0),
        **rest,
    )


def shaped(shape, dtype=jnp.bfloat16):
    return jax.ShapeDtypeStruct(shape, dtype)


def after_all(arrays, *earlier):
    return lax.optimization_barrier(tuple(arrays) + earlier)[: len(arrays)]


def after(array, *earlier):
    return after_all((array,), *earlier)[0]


HOP_ONE = [(0, 0, 1), (3, 1, 2), (1, 1, 0), (2, 0, 3)]
HOP_INNER = [(1, 1, 2), (2, 0, 1)]
HOP_SECOND = [(1, 0, 2), (2, 1, 1)]
HOP_OUTER = [(1, 0, 0), (2, 1, 3)]
HOP_THIRD = [(2, 0, 3), (1, 1, 0)]
BACK_THIRD, BACK_OUTER, BACK_MID, BACK_INNER, BACK_ONE = (
    [(to, c, z) for z, c, to in hops]
    for hops in (HOP_THIRD, HOP_OUTER, HOP_SECOND, HOP_INNER, HOP_ONE)
)

CHAIN = ((0, 1, 1, 0, 3, 2, 5, 4), (4, 5, 2, 3, 0, 1, 1, 0))


def sums_kernel(counts, *refs):
    terms, outs = refs[: sum(counts)], refs[sum(counts) :]
    for out, count in zip(outs, counts):
        total = terms[0][...].astype(jnp.float32)
        for term in terms[1:count]:
            total = total + term[...].astype(jnp.float32)
        out[...] = total.astype(out.dtype)
        terms = terms[count:]


def sums(*groups):
    terms = [term for group in groups for term in group]
    return call(
        functools.partial(sums_kernel, [len(group) for group in groups]),
        [shaped(group[0].shape) for group in groups],
        12,
        in_specs=[VMEM] * len(terms),
        out_specs=[VMEM] * len(groups),
        name="sums",
    )(*terms)


def halves_kernel(code, a, b, c, own, away):
    width = own.shape[0]
    total = a[...].astype(jnp.float32) + b[...].astype(jnp.float32) + c[...].astype(jnp.float32)
    low = code[4] == 0
    own[...] = jnp.where(low, total[:width], total[width:])
    away[...] = jnp.where(low, total[width:], total[:width]).astype(jnp.bfloat16)


def halves(code, parts):
    width, features = parts[0].shape
    return call(
        halves_kernel,
        [shaped((width // 2, features), jnp.float32), shaped((width // 2, features))],
        12,
        in_specs=[SMEM] + [VMEM] * 3,
        out_specs=[VMEM] * 2,
        name="halves",
    )(code, *parts)


def owned_kernel(code, own, other, out):
    out[...] = jnp.where(code[6] == 1, own[...], other[...].astype(jnp.float32))


def owned(code, own, other):
    return call(
        owned_kernel,
        shaped(own.shape, jnp.float32),
        12,
        in_specs=[SMEM] + [VMEM] * 2,
        out_specs=VMEM,
        name="owned",
    )(code, own, other).T


def pack_kernel(first, second, out):
    out[0] = first[1]
    out[1] = second[1]


def pack(first, second):
    return call(
        pack_kernel, shaped(second.shape), 12, in_specs=[VMEM] * 2, out_specs=VMEM, name="pack"
    )(first, second)


def by_head_kernel(code, near, near_other, far, attention, grad_q):
    lanes = near.shape[3]
    core, x = code[4], code[5]
    for which, out in enumerate((attention, grad_q)):
        for k, side, source in (
            (core, x, near.at[0, which]),
            (1 - core, x, near_other.at[0, which]),
            (core, 1 - x, far.at[0, which]),
            (1 - core, 1 - x, far.at[1, which]),
        ):
            out[:, pl.ds(pl.multiple_of((2 * k + side) * lanes, lanes), lanes)] = source[...]


def by_head(code, near, near_other, far):
    _, _, rows, lanes = near.shape
    return call(
        by_head_kernel,
        [shaped((rows, 4 * lanes))] * 2,
        12,
        in_specs=[SMEM] + [VMEM] * 3,
        out_specs=[VMEM] * 2,
        name="by_head",
    )(code, near, near_other, far)


def slot_copies(code, slot_at, refs, buffer, sems, act):
    for k, ref in enumerate(refs):

        @pl.when(slot_at == k)
        def _():
            copy = pltpu.make_async_copy(ref, buffer, sems)
            copy.start() if act else copy.wait()


def project_kernel(code, *refs):
    acts, weights = refs[:4], refs[4:-4]
    mine, theirs, w_v, w_sem = refs[-4:]
    width = mine.shape[1]
    rows = acts[0].shape[0]

    def weight_copies(act):
        for slot in range(2):
            slot_copies(
                code, code[1 + slot], weights, w_v.at[pl.ds(slot * width, width)], w_sem.at[slot], act
            )

    weight_copies(True)
    weight_copies(False)
    for j in range(4):
        here = pl.ds(pl.multiple_of((code[0] ^ j) * rows, rows), rows)
        both = lax.dot_general(acts[j][...], w_v[...], NT, preferred_element_type=jnp.float32)
        mine[here, :] = both[:, :width].astype(jnp.bfloat16)
        theirs[here, :] = both[:, width:].astype(jnp.bfloat16)


def project(code, acts, weights):
    rows, features = acts[0].shape
    width = weights[0].shape[0]
    return call(
        project_kernel,
        [shaped((4 * rows, width)), shaped((4 * rows, width)), shaped((2 * width, features))],
        12,
        in_specs=[SMEM] + [VMEM] * 4 + [HBM] * len(weights),
        out_specs=[VMEM, VMEM, VMEM],
        scratch_shapes=[
            pltpu.SemaphoreType.DMA((2,)),
        ],
        name="project",
    )(code, *acts, *weights)


def normalized(raw, gain, factor):
    inverse = lax.rsqrt(jnp.mean(raw * raw, axis=-1, keepdims=True) + epsilon)
    return raw * inverse * gain * factor


def normalized_pull(raw, gain, factor, cotangent):
    inverse = lax.rsqrt(jnp.mean(raw * raw, axis=-1, keepdims=True) + epsilon)
    scaled = cotangent * gain * factor
    along = jnp.mean(scaled * raw, axis=-1, keepdims=True)
    return inverse * (scaled - raw * (inverse * inverse * along))


def dot(a, b):
    return jnp.dot(a, b, preferred_element_type=jnp.float32)


def scores_kernel(
    code, q_ref, go_ref, own_ref, before_ref, key_mark, query_mark, gain_ref,
    e_ref, stat_ref, dv_own, dv_before, keys_v, acc
):
    block = pl.program_id(0)
    rows = q_ref.shape[1]
    chunks = e_ref.shape[1] // rows
    half = own_ref.shape[0]

    @pl.when(block == 0)
    def _():
        keys_v[:half, :HD] = before_ref[...]
        keys_v[half:, :HD] = own_ref[...]
        keys_v[:, HD:] = key_mark[...]
        acc[...] = jnp.zeros_like(acc)

    key_at = lax.broadcasted_iota(jnp.int32, (rows, 2 * rows), 0)
    query_at = lax.broadcasted_iota(jnp.int32, (rows, 2 * rows), 1)
    behind = key_at <= jnp.where(query_at >= rows, query_at - rows, query_at)
    heads, grads = [], []
    for g in range(2):
        lanes = slice(g * HD, (g + 1) * HD)
        query = normalized(q_ref[0, :, lanes].astype(jnp.float32), gain_ref[...], query_scale)
        heads.append(jnp.concatenate([query.T.astype(jnp.bfloat16), query_mark[...]], axis=0))
        grads.append(go_ref[0, :, lanes].astype(jnp.float32).T)
    query_t = jnp.concatenate(heads, axis=1)
    span = pl.ds(pl.multiple_of(block * rows, rows), chunks * rows)
    e = jnp.exp(dot(keys_v[span, :], query_t))
    e = jnp.concatenate(
        [
            jnp.where(behind, 0.0, e[:rows]),
            e[rows:-rows],
            jnp.where(behind, e[-rows:], 0.0),
        ],
        axis=0,
    )
    total = jnp.sum(e, axis=0, keepdims=True)
    e = e.astype(jnp.bfloat16)
    e_ref[0] = e
    inverse = 1.0 / total
    stat_ref[0] = jnp.broadcast_to(inverse, stat_ref.shape[1:])
    grad = (jnp.concatenate(grads, axis=1) * inverse).T.astype(jnp.bfloat16)
    acc[span, :] = acc[span, :] + dot(e, grad)

    @pl.when(block == pl.num_programs(0) - 1)
    def _():
        dv_before[...] = acc[:half, :].astype(jnp.bfloat16)
        dv_own[...] = acc[half:, :]


def whole(shape):
    return pl.BlockSpec(shape, lambda b, code: (0,) * len(shape))


def attend_scores(code, q, go, keys, keys_before, key_mark, query_mark, gain):
    blocks, rows, _ = q.shape
    half = blocks * rows
    span = half + rows
    picked = pl.BlockSpec((1, rows, 2 * HD), lambda b, code: (b ^ code[0], 0, 0))
    return call(
        scores_kernel,
        [
            shaped((blocks, span, 2 * rows)),
            shaped((blocks, 8, 2 * rows), jnp.float32),
            shaped((half, HD), jnp.float32),
            shaped((half, HD)),
        ],
        14,
        grid_spec=pltpu.PrefetchScalarGridSpec(
            num_scalar_prefetch=1,
            grid=(blocks,),
            in_specs=[
                picked,
                picked,
                whole((half, HD)),
                whole((half, HD)),
                whole((2 * half, HD)),
                pl.BlockSpec((HD, rows), lambda b, code: (0, b)),
                whole((1, HD)),
            ],
            out_specs=[
                pl.BlockSpec((1, span, 2 * rows), lambda b, code: (b, 0, 0)),
                pl.BlockSpec((1, 8, 2 * rows), lambda b, code: (b, 0, 0)),
                whole((half, HD)),
                whole((half, HD)),
            ],
            scratch_shapes=[
                pltpu.VMEM((2 * half, 2 * HD), jnp.bfloat16),
                pltpu.VMEM((2 * half, HD), jnp.float32),
            ],
        ),
        name="attend_scores",
    )(code, q, go, keys, keys_before, key_mark, query_mark, gain)


def values_kernel(
    code, q_ref, go_ref, own_ref, before_ref, v_own, v_before, gain_ref, e_ref, stat_ref,
    kept, sent, dk_own, dk_before, values_v, values_t, keys_t, acc
):
    block = pl.program_id(0)
    rows = q_ref.shape[1]
    span_rows = e_ref.shape[1]
    half = own_ref.shape[0]

    @pl.when(block == 0)
    def _():
        values_v[:half, :] = v_before[...]
        values_v[half:, :] = v_own[...]
        values_t[...] = values_v[...].astype(jnp.float32).T.astype(jnp.bfloat16)
        keys_t[:, :half] = before_ref[...].astype(jnp.float32).T.astype(jnp.bfloat16)
        keys_t[:, half:] = own_ref[...].astype(jnp.float32).T.astype(jnp.bfloat16)
        acc[...] = jnp.zeros_like(acc)

    piece = block ^ code[0]
    odd = (piece % 2 == 1) & jnp.ones((rows, HD), jnp.bool_)

    def put(which, lanes, result):
        for target, here in ((kept, ~odd), (sent, odd)):
            at_piece = target.at[piece // 2, which, :, lanes]
            at_piece[...] = jnp.where(here, result, at_piece[...])

    span = pl.ds(pl.multiple_of(block * rows, rows), span_rows)
    raws = [q_ref[0, :, g * HD : (g + 1) * HD].astype(jnp.float32) for g in range(2)]
    queries = jnp.concatenate(
        [normalized(raw, gain_ref[...], query_scale).astype(jnp.bfloat16) for raw in raws], axis=0
    )
    grad_t = jnp.concatenate(
        [go_ref[0, :, g * HD : (g + 1) * HD].astype(jnp.float32).T for g in range(2)], axis=1
    )
    inverse = stat_ref[0, :1, :]
    e = e_ref[0]
    out_t = dot(values_t[:, span], e) * inverse
    along = jnp.sum(out_t * grad_t, axis=0, keepdims=True) * inverse
    scaled = (grad_t * inverse).astype(jnp.bfloat16)
    dprob = dot(values_v[span, :], scaled)
    dscore = e * (dprob - along).astype(jnp.bfloat16)
    acc[span, :] = acc[span, :] + dot(dscore, queries)
    dquery_t = dot(keys_t[:, span], dscore)
    for g in range(2):
        lanes = slice(g * HD, (g + 1) * HD)
        across = slice(g * rows, (g + 1) * rows)
        put(0, lanes, out_t[:, across].T.astype(jnp.bfloat16))
        pulled = normalized_pull(raws[g], gain_ref[...], query_scale, dquery_t[:, across].T)
        put(1, lanes, pulled.astype(jnp.bfloat16))

    @pl.when(block == pl.num_programs(0) - 1)
    def _():
        dk_before[...] = acc[:half, :].astype(jnp.bfloat16)
        dk_own[...] = acc[half:, :]


def attend_values(code, q, go, keys, keys_before, values, values_before, gain, e, stat):
    blocks, rows, _ = q.shape
    half = blocks * rows
    span = half + rows
    picked = pl.BlockSpec((1, rows, 2 * HD), lambda b, code: (b ^ code[0], 0, 0))
    return call(
        values_kernel,
        [
            shaped((2, 2, rows, 2 * HD)),
            shaped((2, 2, rows, 2 * HD)),
            shaped((half, HD), jnp.float32),
            shaped((half, HD)),
        ],
        16,
        grid_spec=pltpu.PrefetchScalarGridSpec(
            num_scalar_prefetch=1,
            grid=(blocks,),
            in_specs=[picked, picked]
            + [whole((half, HD))] * 4
            + [
                whole((1, HD)),
                pl.BlockSpec((1, span, 2 * rows), lambda b, code: (b, 0, 0)),
                pl.BlockSpec((1, 8, 2 * rows), lambda b, code: (b, 0, 0)),
            ],
            out_specs=[
                whole((2, 2, rows, 2 * HD)),
                whole((2, 2, rows, 2 * HD)),
                whole((half, HD)),
                whole((half, HD)),
            ],
            scratch_shapes=[
                pltpu.VMEM((2 * half, HD), jnp.bfloat16),
                pltpu.VMEM((HD, 2 * half), jnp.bfloat16),
                pltpu.VMEM((HD, 2 * half), jnp.bfloat16),
                pltpu.VMEM((2 * half, HD), jnp.float32),
            ],
        ),
        name="attend_values",
    )(code, q, go, keys, keys_before, values, values_before, gain, e, stat)


def weight_grad_kernel(code, mine, theirs, a0, a1, a2, a3, far, mid):
    acts = (a0, a1, a2, a3)
    rows, features = a0.shape
    width = far.shape[0]
    first = code[3] == 1
    grads = []
    for j in range(4):
        span = pl.ds(pl.multiple_of((code[0] ^ j) * rows, rows), rows)
        own = mine[span, :].astype(jnp.float32).T
        other = theirs[span, :].astype(jnp.float32).T
        both = (jnp.where(first, own, other), jnp.where(first, other, own))
        grads.append(jnp.concatenate(both, axis=0).astype(jnp.bfloat16))
    tile = features // 3
    for n in range(3):
        lanes = slice(n * tile, (n + 1) * tile)
        both = dot(grads[0], acts[0][:, lanes])
        for j in range(1, 4):
            both = both + dot(grads[j], acts[j][:, lanes])
        far[:, lanes] = both[:width].astype(jnp.bfloat16)
        mid[:, lanes] = both[width:].astype(jnp.bfloat16)


def weight_grad(code, mine, theirs, acts):
    rows, features = acts[0].shape
    width = mine.shape[1]
    return call(
        weight_grad_kernel,
        [shaped((width, features)), shaped((width, features))],
        12,
        2 * 4 * rows * features * 2 * width,
        4 * rows * features * 2 + 2 * width * features * 2,
        in_specs=[SMEM] + [VMEM] * 6,
        out_specs=[VMEM, VMEM],
        name="weight_grad",
    )(code, mine, theirs, *acts)


def input_grad_kernel(piece, code, *refs):
    grads, weights, out = refs[:8], refs[8:12], refs[12]
    rows, features = out.shape
    span = pl.ds(pl.multiple_of((code[0] ^ piece) * rows, rows), rows)
    parts = [
        jnp.concatenate([ref[span, :] for ref in grads[2 * k : 2 * k + 2]], axis=1) for k in range(4)
    ]
    tile = features // 3
    for n in range(3):
        lanes = slice(n * tile, (n + 1) * tile)
        total = dot(parts[0], weights[0][:, lanes])
        for k in range(1, 4):
            total = total + dot(parts[k], weights[k][:, lanes])
        out[:, lanes] = total.astype(jnp.bfloat16)


def input_grad(code, piece, grads, weights, rows):
    features = weights[0].shape[1]
    return call(
        functools.partial(input_grad_kernel, piece),
        shaped((rows, features)),
        16,
        in_specs=[SMEM] + [VMEM] * 12,
        out_specs=VMEM,
        name="input_grad",
    )(code, *grads, *weights)


def body_planes(normed, q_raw, key_weight, value_weight, q_gain, k_gain, segment_ids, grad_out):
    rows, features = normed.shape
    half = 4 * rows
    width = key_weight.shape[1]
    place = lax.axis_index("seq")
    uly = lax.axis_index("uly")
    z, x, c = place // 4, (place // 2) % 2, place % 2

    on_line = z * 2 + c
    chosen = [
        jnp.asarray(CHAIN, jnp.int32)[slot, on_line] for slot in (uly, 1 - uly)
    ]
    inner = (z == 1) | (z == 2)
    first_is_own = jnp.where(inner, c, 1 - c) == uly
    code = jnp.stack([place % 4, *chosen, first_is_own, c, x, c == z % 2]).astype(jnp.int32)
    gain_q = q_gain.reshape(1, HD)

    def picked(first_is_low, low, high):
        return jnp.where(first_is_low, low, high)

    normed_x = swap_x(normed)

    def slab(weight):
        other = move(
            weight.T, [((z, x, 1 - z % 2), (z, x, z % 2)) for z in range(4) for x in (0, 1)]
        )
        both = (picked(c == 0, weight.T, other), picked(c == 0, other, weight.T))
        return jnp.concatenate(both, axis=0)

    key_slab = slab(key_weight)
    value_slab = slab(value_weight)

    k_one, k_inner = along_z(key_slab, HOP_ONE), along_z(key_slab, HOP_INNER)
    v_one, v_inner = along_z(value_slab, HOP_ONE), along_z(value_slab, HOP_INNER)
    normed_c = swap_core(after(normed, key_slab))
    k_one, k_inner = after_all((k_one, k_inner), code)
    k_second, k_outer = along_z(k_one, HOP_SECOND), along_z(k_inner, HOP_OUTER)
    v_one, v_inner = after_all((v_one, v_inner), k_one, k_inner)
    v_second, v_outer = along_z(v_one, HOP_SECOND), along_z(v_inner, HOP_OUTER)
    k_second, k_outer = after_all((k_second, k_outer), v_one, v_inner)
    k_third = along_z(k_second, HOP_THIRD)
    normed_x = after(normed_x, k_second, k_outer)
    normed_xc = swap_core(normed_x)

    def head(array, index):
        return array[:, index * 2 * HD : (index + 1) * 2 * HD]

    sources = after_all((q_raw, grad_out), normed_x)
    from_x = swap_x(
        jnp.stack([picked(x == 1, head(a, 2 * k), head(a, 2 * k + 1)) for a in sources for k in (0, 1)])
    )
    near = [picked(x == 0, head(a, 2 * k), head(a, 2 * k + 1)) for a in sources for k in (0, 1)]
    v_second, v_outer = after_all((v_second, v_outer), normed_x, k_second)
    v_third = along_z(v_second, HOP_THIRD)

    segments = after(segment_ids, v_second, v_outer)
    seg_pad = jnp.concatenate([jnp.full((half,), -1, jnp.int32), segments])
    key_seg = lax.dynamic_slice_in_dim(seg_pad, z * half, 2 * half, 0)
    query_seg = lax.dynamic_slice_in_dim(segments, z * half, half, 0)
    lane = lax.broadcasted_iota(jnp.int32, (2 * half, HD), 1)
    key_mark = jnp.where((lane < 2) & (lane != key_seg[:, None]), -MASKED, 0.0).astype(jnp.bfloat16)
    row = lax.broadcasted_iota(jnp.int32, (HD, half), 0)
    query_mark = jnp.where(row == query_seg[None, :], 1.0, 0.0).astype(jnp.bfloat16)

    forward = [(z, c, z + 1) for z in range(3) for c in (0, 1)]
    backward = [(z + 1, c, z) for z in range(3) for c in (0, 1)]

    acts = (normed, normed_c, normed_x, normed_xc)
    k_third = after(k_third, v_second, v_outer)
    key_weights = (key_slab, k_one, k_inner, k_second, k_outer, k_third)
    mine, theirs, key_w = project(code, acts, key_weights)
    key_far = swap_uly(theirs)
    from_x = after(from_x, theirs)
    arrays = [near[0], near[1], near[2], near[3], from_x[0], from_x[1], from_x[2], from_x[3]]
    from_core = swap_core(
        jnp.stack([picked(c == 1, arrays[2 * k], arrays[2 * k + 1]) for k in range(4)])
    )
    kept = [picked(c == 0, arrays[2 * k], arrays[2 * k + 1]) for k in range(4)]

    value_weights = (value_slab, v_one, v_inner, v_second, v_outer, after(v_third, theirs))
    value_mine, value_theirs, value_w = project(code, acts, value_weights)
    value_far = swap_uly(value_theirs)
    key_far = after(key_far, value_theirs)
    key_raw = mine.astype(jnp.float32) + key_far.astype(jnp.float32)
    keys = normalized(key_raw, k_gain, 1.0).astype(jnp.bfloat16)
    keys_before = along_z(keys, forward)
    value_far, from_core = after_all((value_far, from_core), keys)
    values = (value_mine.astype(jnp.float32) + value_far.astype(jnp.float32)).astype(jnp.bfloat16)
    values_before = along_z(values, forward)
    q = jnp.stack([kept[0], from_core[0], kept[2], from_core[2]])
    go = jnp.stack([kept[1], from_core[1], kept[3], from_core[3]])

    keys_before = after(keys_before, values)
    key_w_core, value_w_core = swap_core(key_w), swap_core(value_w)
    e, stat, dv_own, dv_before = attend_scores(
        code, q, go, keys, keys_before, key_mark, query_mark, gain_q
    )
    dv_back = along_z(dv_before, backward)
    values_before = after(values_before, e, key_w_core, value_w_core)
    near, sent_back, dk_own, dk_before = attend_values(
        code, q, go, keys, keys_before, values, values_before, gain_q, e, stat
    )
    dk_back = along_z(dk_before, backward)
    value_grad = (dv_own + after(dv_back, dk_own).astype(jnp.float32)).astype(jnp.bfloat16)
    value_grad_far = swap_uly(value_grad)

    near_other = swap_core(sent_back)
    far = pack(near, near_other)
    back_x = swap_x(far)

    v_first, v_second = weight_grad(code, value_grad, after(value_grad_far, far), acts)
    v_third, v_outer = along_z(v_second, BACK_THIRD), along_z(v_first, BACK_OUTER)
    dkey = dk_own + after(dk_back, v_first).astype(jnp.float32)
    key_grad = normalized_pull(key_raw, k_gain, 1.0, dkey).astype(jnp.bfloat16)
    key_grad_far = swap_uly(key_grad)
    grads = (key_grad, key_grad_far, value_grad, value_grad_far)
    grads_core = tuple(swap_core(grad) for grad in grads)
    k_first, k_second = weight_grad(code, key_grad, key_grad_far, acts)
    k_third = along_z(k_second, BACK_THIRD)
    back_x = after(back_x, k_first)
    grads = grads[:2] + after_all(grads_core[:2], back_x) + grads[2:] + grads_core[2:]
    weights = (key_w, key_w_core, value_w, value_w_core)
    away = input_grad(code, 2, grads, weights, rows)
    from_x = swap_x(away)
    v_third, v_outer = after_all((v_third, v_outer), away)
    v_mid_payload, v_inner_payload = sums((v_first, v_third), (v_second, v_outer))
    v_mid, v_inner = along_z(v_mid_payload, BACK_MID), along_z(v_inner_payload, BACK_INNER)
    k_third = after(k_third, v_mid_payload)
    (k_mid_payload,) = sums((k_first, k_third))
    key_grad_far = after(key_grad_far, k_mid_payload)
    kept = input_grad(code, 0, (key_grad, key_grad_far) + grads[2:], weights, rows)
    k_mid, k_outer = along_z(k_mid_payload, BACK_MID), along_z(after(k_first, k_third), BACK_OUTER)
    v_mid, v_inner = after_all((v_mid, v_inner), kept)
    (v_one_payload,) = sums((v_first, v_mid))
    v_one = along_z(v_one_payload, BACK_ONE)
    attention, grad_q = by_head(code, near, near_other, after(back_x, v_one_payload, v_inner))
    k_mid, k_outer = after_all((k_mid, k_outer), attention)
    k_one_payload, k_inner_payload = sums((k_first, k_mid), (k_second, k_outer))
    k_one, k_inner = along_z(k_one_payload, BACK_ONE), along_z(k_inner_payload, BACK_INNER)

    def to_core(away):
        return move(
            away, [((z, x, z % 2), (z, x, 1 - z % 2)) for z in range(4) for x in (0, 1)]
        )

    from_x = after(from_x, k_inner_payload)
    (grad_normed,) = sums((kept, from_x))
    v_one = after(v_one, grad_normed)
    value_own, value_away = halves(code, (v_second, v_inner, v_one))
    grad_value_weight = owned(code, value_own, to_core(value_away))
    k_one, k_inner = after_all((k_one, k_inner), grad_value_weight)
    key_own, key_away = halves(code, (k_second, k_inner, k_one))
    grad_key_weight = owned(code, key_own, to_core(key_away))
    return (attention, grad_normed, grad_q, grad_key_weight, grad_value_weight)


def body(normed, q_raw, *rest):
    planes = (
        lax.axis_size("seq") == 16
        and lax.axis_size("uly") == 2
        and 4 * normed.shape[0] == WINDOW
        and q_raw.shape[1] == 8 * HD
    )
    return (body_planes if planes else body_general)(normed, q_raw, *rest)


def solution(mesh):
    return jax.shard_map(
        body,
        mesh=mesh,
        in_specs=(
            P("seq", "uly"),
            P("seq", "uly"),
            P("uly", "seq"),
            P("uly", "seq"),
            P(),
            P(),
            P(),
            P("seq", "uly"),
        ),
        out_specs=(
            P("seq", "uly"),
            P("seq", "uly"),
            P("seq", "uly"),
            P("uly", "seq"),
            P("uly", "seq"),
        ),
        check_vma=False,
    )
```

```python
import functools

import jax
import jax.numpy as jnp
from jax import lax
from jax.experimental import pallas as pl
from jax.experimental.pallas import tpu as pltpu
from jax.sharding import PartitionSpec as P

HD = 128
WINDOW = 1024


epsilon = 1e-06
query_scale = 168.0 ** (-0.5)


def from_behind(array, axis, by):
    devices = lax.axis_size(axis)
    pairs = [(i, i + by) for i in range(devices) if 0 <= i + by < devices]
    return lax.ppermute(array, axis, pairs)


def normalize(raw_vals, gain, factor):
    mean_sq = jnp.mean(raw_vals * raw_vals, axis=-1, keepdims=True)
    return raw_vals * lax.rsqrt(mean_sq + epsilon) * gain * factor


def attend_block(
    queries, key_block, value_block, grad_block, query_pos, key_pos, query_seg, key_seg
):
    scores = jnp.einsum("bhge,lhe->hgbl", queries, key_block, preferred_element_type=jnp.float32)
    allowed = (
        (key_pos[None, :] <= query_pos[:, None])
        & (key_pos[None, :] > query_pos[:, None] - WINDOW)
        & (key_seg[None, :] == query_seg[:, None])
    )
    exp_scores = jnp.where(allowed[None, None], jnp.exp(scores), 0.0)
    probs = exp_scores / jnp.sum(exp_scores, axis=-1, keepdims=True)
    weights = probs.astype(jnp.bfloat16)
    attended = jnp.einsum(
        "hgbl,lhe->bhge", weights, value_block, preferred_element_type=jnp.float32
    ).astype(jnp.bfloat16)
    dprob = jnp.einsum(
        "bhge,lhe->hgbl", grad_block, value_block, preferred_element_type=jnp.float32
    )
    delta_row = jnp.sum(probs * dprob, axis=-1, keepdims=True)
    dscore = (probs * (dprob - delta_row)).astype(jnp.bfloat16)
    dquery = jnp.einsum("hgbl,lhe->bhge", dscore, key_block, preferred_element_type=jnp.float32)
    dkey = jnp.einsum("hgbl,bhge->lhe", dscore, queries, preferred_element_type=jnp.float32)
    dvalue = jnp.einsum("hgbl,bhge->lhe", weights, grad_block, preferred_element_type=jnp.float32)
    return (attended, dquery, dkey, dvalue)


def body_general(normed, q_raw, key_weight, value_weight, q_gain, k_gain, segment_ids, grad_out):
    rows_here = normed.shape[0]
    heads_here = q_raw.shape[1] // (2 * HD)
    seq_index = lax.axis_index("seq")
    base_row = seq_index * rows_here
    weight_pair = (
        lax.all_gather(key_weight, "seq", axis=1, tiled=True),
        lax.all_gather(value_weight, "seq", axis=1, tiled=True),
    )
    key_term = jnp.dot(normed, weight_pair[0], preferred_element_type=jnp.float32)
    value_term = jnp.dot(normed, weight_pair[1], preferred_element_type=jnp.float32)
    key_raw, value_raw = (
        lax.psum_scatter(
            key_term.astype(jnp.bfloat16), "uly", scatter_dimension=1, tiled=True
        ).astype(jnp.float32),
        lax.psum_scatter(
            value_term.astype(jnp.bfloat16), "uly", scatter_dimension=1, tiled=True
        ).astype(jnp.float32),
    )
    key_in = key_raw.reshape(rows_here, heads_here, HD)
    keys_bf = normalize(key_in, k_gain, 1.0).astype(jnp.bfloat16)
    values_bf = value_raw.reshape(rows_here, heads_here, HD).astype(jnp.bfloat16)
    query_in = q_raw.astype(jnp.float32).reshape(rows_here, heads_here, 2, HD)
    queries = normalize(query_in, q_gain, query_scale).astype(jnp.bfloat16)
    grad_heads = grad_out.reshape(rows_here, heads_here, 2, HD)
    stacked = jnp.stack([keys_bf, values_bf])
    distance_most = -(-WINDOW // rows_here)
    pieces = []
    for distance in range(distance_most, 0, -1):
        first_row = max(0, distance * rows_here - WINDOW)
        pieces.append(from_behind(stacked, "seq", distance))
    pieces.append(stacked)
    extended = jnp.concatenate(pieces, axis=1)
    block_rows = min(512, rows_here)
    span_rows = block_rows + WINDOW
    count_blocks = rows_here // block_rows
    seg_pad = jnp.concatenate([jnp.full((WINDOW,), -1, jnp.int32), segment_ids])
    query_seg_all = lax.dynamic_slice_in_dim(segment_ids, base_row, rows_here, 0)
    key_seg_all = lax.dynamic_slice_in_dim(seg_pad, base_row, WINDOW + rows_here, 0)

    def step(grad_acc, block_index):
        begin_row = block_index * block_rows
        query_pos = base_row + begin_row + jnp.arange(block_rows, dtype=jnp.int32)
        key_pos = base_row + begin_row - WINDOW + jnp.arange(span_rows, dtype=jnp.int32)
        key_block = lax.dynamic_slice_in_dim(extended, begin_row, span_rows, 1)
        attended, dquery, dkey, dvalue = attend_block(
            lax.dynamic_slice_in_dim(queries, begin_row, block_rows, 0),
            key_block[0],
            key_block[1],
            lax.dynamic_slice_in_dim(grad_heads, begin_row, block_rows, 0),
            query_pos,
            key_pos,
            lax.dynamic_slice_in_dim(query_seg_all, begin_row, block_rows, 0),
            lax.dynamic_slice_in_dim(key_seg_all, begin_row, span_rows, 0),
        )
        update = jnp.stack([dkey, dvalue])
        grad_acc = lax.dynamic_update_slice_in_dim(
            grad_acc,
            lax.dynamic_slice_in_dim(grad_acc, begin_row, span_rows, 1) + update,
            begin_row,
            1,
        )
        return (grad_acc, (attended, dquery))

    zero_acc = jnp.zeros((2, WINDOW + rows_here, heads_here, HD), jnp.float32)
    grad_acc, (attended, dquery) = lax.scan(
        step, zero_acc, jnp.arange(count_blocks, dtype=jnp.int32)
    )
    attention = attended.reshape(rows_here, 2 * heads_here * HD)
    dquery = dquery.reshape(rows_here, heads_here, 2, HD)
    own_grads = grad_acc[:, WINDOW:]
    offset_row = 0
    for distance in range(distance_most, 0, -1):
        first_row = max(0, distance * rows_here - WINDOW)
        piece_rows = rows_here - first_row
        outgoing = grad_acc[:, offset_row : offset_row + piece_rows]
        returned = from_behind(outgoing.astype(jnp.bfloat16), "seq", -distance).astype(
            outgoing.dtype
        )
        own_grads = own_grads.at[:, first_row:].add(returned)
        offset_row = offset_row + piece_rows
    _, pull_query = jax.vjp(lambda raw_vals: normalize(raw_vals, q_gain, query_scale), query_in)
    grad_q = pull_query(dquery)[0].astype(jnp.bfloat16).reshape(rows_here, 2 * heads_here * HD)
    _, pull_key = jax.vjp(lambda raw_vals: normalize(raw_vals, k_gain, 1.0), key_in)
    key_grad = pull_key(own_grads[0])[0].astype(jnp.bfloat16).reshape(rows_here, heads_here * HD)
    value_grad = own_grads[1].astype(jnp.bfloat16).reshape(rows_here, heads_here * HD)
    key_all, value_all = (
        lax.all_gather(key_grad, "uly", axis=1, tiled=True),
        lax.all_gather(value_grad, "uly", axis=1, tiled=True),
    )
    dims_last = (((1,), (1,)), ((), ()))
    total = lax.dot_general(key_all, weight_pair[0], dims_last, preferred_element_type=jnp.float32)
    total = total + lax.dot_general(
        value_all, weight_pair[1], dims_last, preferred_element_type=jnp.float32
    )
    grad_normed = total.astype(jnp.bfloat16)
    dims_first = (((0,), (0,)), ((), ()))
    key_part = lax.dot_general(normed, key_all, dims_first, preferred_element_type=jnp.float32)
    value_part = lax.dot_general(normed, value_all, dims_first, preferred_element_type=jnp.float32)
    grad_key_weight = lax.psum_scatter(
        key_part.astype(jnp.bfloat16), "seq", scatter_dimension=1, tiled=True
    ).astype(jnp.float32)
    grad_value_weight = lax.psum_scatter(
        value_part.astype(jnp.bfloat16), "seq", scatter_dimension=1, tiled=True
    ).astype(jnp.float32)
    return (attention, grad_normed, grad_q, grad_key_weight, grad_value_weight)


MIB = 1 << 20
MASKED = 16384.0
NT = (((1,), (1,)), ((), ()))
HBM = pl.BlockSpec(memory_space=pltpu.HBM)
SMEM = pl.BlockSpec(memory_space=pltpu.SMEM)
VMEM = pl.BlockSpec(memory_space=pltpu.VMEM)


def at(z, x, c):
    return (z * 2 + x) * 2 + c


def move(array, rule):
    return lax.ppermute(array, "seq", [(at(*a), at(*b)) for a, b in rule])


def along_z(array, hops):
    return move(array, [((z, x, c), (to, x, c)) for z, c, to in hops for x in (0, 1)])


def swap_core(array):
    return move(
        array, [((z, x, c), (z, x, 1 - c)) for z in range(4) for x in (0, 1) for c in (0, 1)]
    )


def swap_x(array):
    return move(
        array, [((z, x, c), (z, 1 - x, c)) for z in range(4) for x in (0, 1) for c in (0, 1)]
    )


def swap_uly(array):
    return lax.ppermute(array, "uly", [(0, 1), (1, 0)])


def call(kernel, out_shape, vmem, **rest):
    return pl.pallas_call(
        kernel,
        out_shape=out_shape,
        compiler_params=pltpu.CompilerParams(vmem_limit_bytes=vmem * MIB),
        cost_estimate=pl.CostEstimate(flops=0, bytes_accessed=0, transcendentals=0),
        **rest,
    )


def shaped(shape, dtype=jnp.bfloat16):
    return jax.ShapeDtypeStruct(shape, dtype)


def after_all(arrays, *earlier):
    return lax.optimization_barrier(tuple(arrays) + earlier)[: len(arrays)]


def after(array, *earlier):
    return after_all((array,), *earlier)[0]


HOP_ONE = [(0, 0, 1), (3, 1, 2), (1, 1, 0), (2, 0, 3)]
HOP_INNER = [(1, 1, 2), (2, 0, 1)]
HOP_SECOND = [(1, 0, 2), (2, 1, 1)]
HOP_OUTER = [(1, 0, 0), (2, 1, 3)]
HOP_THIRD = [(2, 0, 3), (1, 1, 0)]
BACK_THIRD, BACK_OUTER, BACK_MID, BACK_INNER, BACK_ONE = (
    [(to, c, z) for z, c, to in hops]
    for hops in (HOP_THIRD, HOP_OUTER, HOP_SECOND, HOP_INNER, HOP_ONE)
)

CHAIN = ((0, 1, 1, 0, 3, 2, 5, 4), (4, 5, 2, 3, 0, 1, 1, 0))


def sums_kernel(counts, *refs):
    terms, outs = refs[: sum(counts)], refs[sum(counts) :]
    for out, count in zip(outs, counts):
        total = terms[0][...].astype(jnp.float32)
        for term in terms[1:count]:
            total = total + term[...].astype(jnp.float32)
        out[...] = total.astype(out.dtype)
        terms = terms[count:]


def sums(*groups):
    terms = [term for group in groups for term in group]
    return call(
        functools.partial(sums_kernel, [len(group) for group in groups]),
        [shaped(group[0].shape) for group in groups],
        12,
        in_specs=[VMEM] * len(terms),
        out_specs=[VMEM] * len(groups),
        name="sums",
    )(*terms)


def halves_kernel(code, a, b, c, own, away):
    width = own.shape[0]
    total = a[...].astype(jnp.float32) + b[...].astype(jnp.float32) + c[...].astype(jnp.float32)
    low = code[4] == 0
    own[...] = jnp.where(low, total[:width], total[width:])
    away[...] = jnp.where(low, total[width:], total[:width]).astype(jnp.bfloat16)


def halves(code, parts):
    width, features = parts[0].shape
    return call(
        halves_kernel,
        [shaped((width // 2, features), jnp.float32), shaped((width // 2, features))],
        12,
        in_specs=[SMEM] + [VMEM] * 3,
        out_specs=[VMEM] * 2,
        name="halves",
    )(code, *parts)


def owned_kernel(code, own, other, out):
    out[...] = jnp.where(code[6] == 1, own[...], other[...].astype(jnp.float32))


def owned(code, own, other):
    return call(
        owned_kernel,
        shaped(own.shape, jnp.float32),
        12,
        in_specs=[SMEM] + [VMEM] * 2,
        out_specs=VMEM,
        name="owned",
    )(code, own, other).T


def pack_kernel(first, second, out):
    out[0] = first[1]
    out[1] = second[1]


def pack(first, second):
    return call(
        pack_kernel, shaped(second.shape), 12, in_specs=[VMEM] * 2, out_specs=VMEM, name="pack"
    )(first, second)


def by_head_kernel(code, near, near_other, far, attention, grad_q):
    lanes = near.shape[3]
    core, x = code[4], code[5]
    for which, out in enumerate((attention, grad_q)):
        for k, side, source in (
            (core, x, near.at[0, which]),
            (1 - core, x, near_other.at[0, which]),
            (core, 1 - x, far.at[0, which]),
            (1 - core, 1 - x, far.at[1, which]),
        ):
            out[:, pl.ds(pl.multiple_of((2 * k + side) * lanes, lanes), lanes)] = source[...]


def by_head(code, near, near_other, far):
    _, _, rows, lanes = near.shape
    return call(
        by_head_kernel,
        [shaped((rows, 4 * lanes))] * 2,
        12,
        in_specs=[SMEM] + [VMEM] * 3,
        out_specs=[VMEM] * 2,
        name="by_head",
    )(code, near, near_other, far)


def slot_copies(code, slot_at, refs, buffer, sems, act):
    for k, ref in enumerate(refs):

        @pl.when(slot_at == k)
        def _():
            copy = pltpu.make_async_copy(ref, buffer, sems)
            copy.start() if act else copy.wait()


def project_kernel(code, *refs):
    acts, weights = refs[:4], refs[4:-4]
    mine, theirs, w_v, w_sem = refs[-4:]
    width = mine.shape[1]
    rows = acts[0].shape[0]

    def weight_copies(act):
        for slot in range(2):
            slot_copies(
                code, code[1 + slot], weights, w_v.at[pl.ds(slot * width, width)], w_sem.at[slot], act
            )

    weight_copies(True)
    weight_copies(False)
    for j in range(4):
        here = pl.ds(pl.multiple_of((code[0] ^ j) * rows, rows), rows)
        both = lax.dot_general(acts[j][...], w_v[...], NT, preferred_element_type=jnp.float32)
        mine[here, :] = both[:, :width].astype(jnp.bfloat16)
        theirs[here, :] = both[:, width:].astype(jnp.bfloat16)


def project(code, acts, weights):
    rows, features = acts[0].shape
    width = weights[0].shape[0]
    return call(
        project_kernel,
        [shaped((4 * rows, width)), shaped((4 * rows, width)), shaped((2 * width, features))],
        12,
        in_specs=[SMEM] + [VMEM] * 4 + [HBM] * len(weights),
        out_specs=[VMEM, VMEM, VMEM],
        scratch_shapes=[
            pltpu.SemaphoreType.DMA((2,)),
        ],
        name="project",
    )(code, *acts, *weights)


def normalized(raw, gain, factor):
    inverse = lax.rsqrt(jnp.mean(raw * raw, axis=-1, keepdims=True) + epsilon)
    return raw * inverse * gain * factor


def normalized_pull(raw, gain, factor, cotangent):
    inverse = lax.rsqrt(jnp.mean(raw * raw, axis=-1, keepdims=True) + epsilon)
    scaled = cotangent * gain * factor
    along = jnp.mean(scaled * raw, axis=-1, keepdims=True)
    return inverse * (scaled - raw * (inverse * inverse * along))


def dot(a, b):
    return jnp.dot(a, b, preferred_element_type=jnp.float32)


def scores_kernel(
    code, q_ref, go_ref, own_ref, before_ref, key_mark, query_mark, gain_ref,
    e_ref, stat_ref, dv_own, dv_before, keys_v, acc
):
    block = pl.program_id(0)
    rows = q_ref.shape[1]
    chunks = e_ref.shape[1] // rows
    half = own_ref.shape[0]

    @pl.when(block == 0)
    def _():
        keys_v[:half, :HD] = before_ref[...]
        keys_v[half:, :HD] = own_ref[...]
        keys_v[:, HD:] = key_mark[...]
        acc[...] = jnp.zeros_like(acc)

    key_at = lax.broadcasted_iota(jnp.int32, (rows, 2 * rows), 0)
    query_at = lax.broadcasted_iota(jnp.int32, (rows, 2 * rows), 1)
    behind = key_at <= jnp.where(query_at >= rows, query_at - rows, query_at)
    heads, grads = [], []
    for g in range(2):
        lanes = slice(g * HD, (g + 1) * HD)
        query = normalized(q_ref[0, :, lanes].astype(jnp.float32), gain_ref[...], query_scale)
        heads.append(jnp.concatenate([query.T.astype(jnp.bfloat16), query_mark[...]], axis=0))
        grads.append(go_ref[0, :, lanes].astype(jnp.float32).T)
    query_t = jnp.concatenate(heads, axis=1)
    span = pl.ds(pl.multiple_of(block * rows, rows), chunks * rows)
    e = jnp.exp(dot(keys_v[span, :], query_t))
    e = jnp.concatenate(
        [
            jnp.where(behind, 0.0, e[:rows]),
            e[rows:-rows],
            jnp.where(behind, e[-rows:], 0.0),
        ],
        axis=0,
    )
    total = jnp.sum(e, axis=0, keepdims=True)
    e = e.astype(jnp.bfloat16)
    e_ref[0] = e
    inverse = 1.0 / total
    stat_ref[0] = jnp.broadcast_to(inverse, stat_ref.shape[1:])
    grad = (jnp.concatenate(grads, axis=1) * inverse).T.astype(jnp.bfloat16)
    acc[span, :] = acc[span, :] + dot(e, grad)

    @pl.when(block == pl.num_programs(0) - 1)
    def _():
        dv_before[...] = acc[:half, :].astype(jnp.bfloat16)
        dv_own[...] = acc[half:, :]


def whole(shape):
    return pl.BlockSpec(shape, lambda b, code: (0,) * len(shape))


def attend_scores(code, q, go, keys, keys_before, key_mark, query_mark, gain):
    blocks, rows, _ = q.shape
    half = blocks * rows
    span = half + rows
    picked = pl.BlockSpec((1, rows, 2 * HD), lambda b, code: (b ^ code[0], 0, 0))
    return call(
        scores_kernel,
        [
            shaped((blocks, span, 2 * rows)),
            shaped((blocks, 8, 2 * rows), jnp.float32),
            shaped((half, HD), jnp.float32),
            shaped((half, HD)),
        ],
        14,
        grid_spec=pltpu.PrefetchScalarGridSpec(
            num_scalar_prefetch=1,
            grid=(blocks,),
            in_specs=[
                picked,
                picked,
                whole((half, HD)),
                whole((half, HD)),
                whole((2 * half, HD)),
                pl.BlockSpec((HD, rows), lambda b, code: (0, b)),
                whole((1, HD)),
            ],
            out_specs=[
                pl.BlockSpec((1, span, 2 * rows), lambda b, code: (b, 0, 0)),
                pl.BlockSpec((1, 8, 2 * rows), lambda b, code: (b, 0, 0)),
                whole((half, HD)),
                whole((half, HD)),
            ],
            scratch_shapes=[
                pltpu.VMEM((2 * half, 2 * HD), jnp.bfloat16),
                pltpu.VMEM((2 * half, HD), jnp.float32),
            ],
        ),
        name="attend_scores",
    )(code, q, go, keys, keys_before, key_mark, query_mark, gain)


def values_kernel(
    code, q_ref, go_ref, own_ref, before_ref, v_own, v_before, gain_ref, e_ref, stat_ref,
    kept, sent, dk_own, dk_before, values_v, values_t, keys_t, acc
):
    block = pl.program_id(0)
    rows = q_ref.shape[1]
    span_rows = e_ref.shape[1]
    half = own_ref.shape[0]

    @pl.when(block == 0)
    def _():
        values_v[:half, :] = v_before[...]
        values_v[half:, :] = v_own[...]
        values_t[...] = values_v[...].astype(jnp.float32).T.astype(jnp.bfloat16)
        keys_t[:, :half] = before_ref[...].astype(jnp.float32).T.astype(jnp.bfloat16)
        keys_t[:, half:] = own_ref[...].astype(jnp.float32).T.astype(jnp.bfloat16)
        acc[...] = jnp.zeros_like(acc)

    piece = block ^ code[0]
    odd = (piece % 2 == 1) & jnp.ones((rows, HD), jnp.bool_)

    def put(which, lanes, result):
        for target, here in ((kept, ~odd), (sent, odd)):
            at_piece = target.at[piece // 2, which, :, lanes]
            at_piece[...] = jnp.where(here, result, at_piece[...])

    span = pl.ds(pl.multiple_of(block * rows, rows), span_rows)
    raws = [q_ref[0, :, g * HD : (g + 1) * HD].astype(jnp.float32) for g in range(2)]
    queries = jnp.concatenate(
        [normalized(raw, gain_ref[...], query_scale).astype(jnp.bfloat16) for raw in raws], axis=0
    )
    grad_t = jnp.concatenate(
        [go_ref[0, :, g * HD : (g + 1) * HD].astype(jnp.float32).T for g in range(2)], axis=1
    )
    inverse = stat_ref[0, :1, :]
    e = e_ref[0]
    out_t = dot(values_t[:, span], e) * inverse
    along = jnp.sum(out_t * grad_t, axis=0, keepdims=True) * inverse
    scaled = (grad_t * inverse).astype(jnp.bfloat16)
    dprob = dot(values_v[span, :], scaled)
    dscore = e * (dprob - along).astype(jnp.bfloat16)
    acc[span, :] = acc[span, :] + dot(dscore, queries)
    dquery_t = dot(keys_t[:, span], dscore)
    for g in range(2):
        lanes = slice(g * HD, (g + 1) * HD)
        across = slice(g * rows, (g + 1) * rows)
        put(0, lanes, out_t[:, across].T.astype(jnp.bfloat16))
        pulled = normalized_pull(raws[g], gain_ref[...], query_scale, dquery_t[:, across].T)
        put(1, lanes, pulled.astype(jnp.bfloat16))

    @pl.when(block == pl.num_programs(0) - 1)
    def _():
        dk_before[...] = acc[:half, :].astype(jnp.bfloat16)
        dk_own[...] = acc[half:, :]


def attend_values(code, q, go, keys, keys_before, values, values_before, gain, e, stat):
    blocks, rows, _ = q.shape
    half = blocks * rows
    span = half + rows
    picked = pl.BlockSpec((1, rows, 2 * HD), lambda b, code: (b ^ code[0], 0, 0))
    return call(
        values_kernel,
        [
            shaped((2, 2, rows, 2 * HD)),
            shaped((2, 2, rows, 2 * HD)),
            shaped((half, HD), jnp.float32),
            shaped((half, HD)),
        ],
        16,
        grid_spec=pltpu.PrefetchScalarGridSpec(
            num_scalar_prefetch=1,
            grid=(blocks,),
            in_specs=[picked, picked]
            + [whole((half, HD))] * 4
            + [
                whole((1, HD)),
                pl.BlockSpec((1, span, 2 * rows), lambda b, code: (b, 0, 0)),
                pl.BlockSpec((1, 8, 2 * rows), lambda b, code: (b, 0, 0)),
            ],
            out_specs=[
                whole((2, 2, rows, 2 * HD)),
                whole((2, 2, rows, 2 * HD)),
                whole((half, HD)),
                whole((half, HD)),
            ],
            scratch_shapes=[
                pltpu.VMEM((2 * half, HD), jnp.bfloat16),
                pltpu.VMEM((HD, 2 * half), jnp.bfloat16),
                pltpu.VMEM((HD, 2 * half), jnp.bfloat16),
                pltpu.VMEM((2 * half, HD), jnp.float32),
            ],
        ),
        name="attend_values",
    )(code, q, go, keys, keys_before, values, values_before, gain, e, stat)


def weight_grad_kernel(code, mine, theirs, a0, a1, a2, a3, far, mid):
    acts = (a0, a1, a2, a3)
    rows, features = a0.shape
    width = far.shape[0]
    first = code[3] == 1
    grads = []
    for j in range(4):
        span = pl.ds(pl.multiple_of((code[0] ^ j) * rows, rows), rows)
        own = mine[span, :].astype(jnp.float32).T
        other = theirs[span, :].astype(jnp.float32).T
        both = (jnp.where(first, own, other), jnp.where(first, other, own))
        grads.append(jnp.concatenate(both, axis=0).astype(jnp.bfloat16))
    tile = features // 3
    for n in range(3):
        lanes = slice(n * tile, (n + 1) * tile)
        both = dot(grads[0], acts[0][:, lanes])
        for j in range(1, 4):
            both = both + dot(grads[j], acts[j][:, lanes])
        far[:, lanes] = both[:width].astype(jnp.bfloat16)
        mid[:, lanes] = both[width:].astype(jnp.bfloat16)


def weight_grad(code, mine, theirs, acts):
    rows, features = acts[0].shape
    width = mine.shape[1]
    return call(
        weight_grad_kernel,
        [shaped((width, features)), shaped((width, features))],
        12,
        in_specs=[SMEM] + [VMEM] * 6,
        out_specs=[VMEM, VMEM],
        name="weight_grad",
    )(code, mine, theirs, *acts)


def input_grad_kernel(piece, code, *refs):
    grads, weights, out = refs[:8], refs[8:12], refs[12]
    rows, features = out.shape
    span = pl.ds(pl.multiple_of((code[0] ^ piece) * rows, rows), rows)
    parts = [
        jnp.concatenate([ref[span, :] for ref in grads[2 * k : 2 * k + 2]], axis=1) for k in range(4)
    ]
    tile = features // 3
    for n in range(3):
        lanes = slice(n * tile, (n + 1) * tile)
        total = dot(parts[0], weights[0][:, lanes])
        for k in range(1, 4):
            total = total + dot(parts[k], weights[k][:, lanes])
        out[:, lanes] = total.astype(jnp.bfloat16)


def input_grad(code, piece, grads, weights, rows):
    features = weights[0].shape[1]
    return call(
        functools.partial(input_grad_kernel, piece),
        shaped((rows, features)),
        16,
        in_specs=[SMEM] + [VMEM] * 12,
        out_specs=VMEM,
        name="input_grad",
    )(code, *grads, *weights)


def body_planes(normed, q_raw, key_weight, value_weight, q_gain, k_gain, segment_ids, grad_out):
    rows, features = normed.shape
    half = 4 * rows
    width = key_weight.shape[1]
    place = lax.axis_index("seq")
    uly = lax.axis_index("uly")
    z, x, c = place // 4, (place // 2) % 2, place % 2

    on_line = z * 2 + c
    chosen = [
        jnp.asarray(CHAIN, jnp.int32)[slot, on_line] for slot in (uly, 1 - uly)
    ]
    inner = (z == 1) | (z == 2)
    first_is_own = jnp.where(inner, c, 1 - c) == uly
    code = jnp.stack([place % 4, *chosen, first_is_own, c, x, c == z % 2]).astype(jnp.int32)
    gain_q = q_gain.reshape(1, HD)

    def picked(first_is_low, low, high):
        return jnp.where(first_is_low, low, high)

    normed_x = swap_x(normed)

    def slab(weight):
        other = move(
            weight.T, [((z, x, 1 - z % 2), (z, x, z % 2)) for z in range(4) for x in (0, 1)]
        )
        both = (picked(c == 0, weight.T, other), picked(c == 0, other, weight.T))
        return jnp.concatenate(both, axis=0)

    key_slab = slab(key_weight)
    value_slab = slab(value_weight)

    k_one, k_inner = along_z(key_slab, HOP_ONE), along_z(key_slab, HOP_INNER)
    v_one, v_inner = along_z(value_slab, HOP_ONE), along_z(value_slab, HOP_INNER)
    normed_c = swap_core(after(normed, key_slab))
    k_one, k_inner = after_all((k_one, k_inner), code)
    k_second, k_outer = along_z(k_one, HOP_SECOND), along_z(k_inner, HOP_OUTER)
    v_one, v_inner = after_all((v_one, v_inner), k_one, k_inner)
    v_second, v_outer = along_z(v_one, HOP_SECOND), along_z(v_inner, HOP_OUTER)
    k_second, k_outer = after_all((k_second, k_outer), v_one, v_inner)
    k_third = along_z(k_second, HOP_THIRD)
    normed_x = after(normed_x, k_second, k_outer)
    normed_xc = swap_core(normed_x)

    def head(array, index):
        return array[:, index * 2 * HD : (index + 1) * 2 * HD]

    sources = after_all((q_raw, grad_out), normed_x)
    from_x = swap_x(
        jnp.stack([picked(x == 1, head(a, 2 * k), head(a, 2 * k + 1)) for a in sources for k in (0, 1)])
    )
    near = [picked(x == 0, head(a, 2 * k), head(a, 2 * k + 1)) for a in sources for k in (0, 1)]
    v_second, v_outer = after_all((v_second, v_outer), normed_x, k_second)
    v_third = along_z(v_second, HOP_THIRD)

    segments = after(segment_ids, v_second, v_outer)
    seg_pad = jnp.concatenate([jnp.full((half,), -1, jnp.int32), segments])
    key_seg = lax.dynamic_slice_in_dim(seg_pad, z * half, 2 * half, 0)
    query_seg = lax.dynamic_slice_in_dim(segments, z * half, half, 0)
    lane = lax.broadcasted_iota(jnp.int32, (2 * half, HD), 1)
    key_mark = jnp.where((lane < 2) & (lane != key_seg[:, None]), -MASKED, 0.0).astype(jnp.bfloat16)
    row = lax.broadcasted_iota(jnp.int32, (HD, half), 0)
    query_mark = jnp.where(row == query_seg[None, :], 1.0, 0.0).astype(jnp.bfloat16)

    forward = [(z, c, z + 1) for z in range(3) for c in (0, 1)]
    backward = [(z + 1, c, z) for z in range(3) for c in (0, 1)]

    acts = (normed, normed_c, normed_x, normed_xc)
    k_third = after(k_third, v_second, v_outer)
    key_weights = (key_slab, k_one, k_inner, k_second, k_outer, k_third)
    mine, theirs, key_w = project(code, acts, key_weights)
    key_far = swap_uly(theirs)
    from_x = after(from_x, theirs)
    arrays = [near[0], near[1], near[2], near[3], from_x[0], from_x[1], from_x[2], from_x[3]]
    from_core = swap_core(
        jnp.stack([picked(c == 1, arrays[2 * k], arrays[2 * k + 1]) for k in range(4)])
    )
    kept = [picked(c == 0, arrays[2 * k], arrays[2 * k + 1]) for k in range(4)]

    value_weights = (value_slab, v_one, v_inner, v_second, v_outer, after(v_third, theirs))
    value_mine, value_theirs, value_w = project(code, acts, value_weights)
    value_far = swap_uly(value_theirs)
    key_far = after(key_far, value_theirs)
    key_raw = mine.astype(jnp.float32) + key_far.astype(jnp.float32)
    keys = normalized(key_raw, k_gain, 1.0).astype(jnp.bfloat16)
    keys_before = along_z(keys, forward)
    value_far, from_core = after_all((value_far, from_core), keys)
    values = (value_mine.astype(jnp.float32) + value_far.astype(jnp.float32)).astype(jnp.bfloat16)
    values_before = along_z(values, forward)
    q = jnp.stack([kept[0], from_core[0], kept[2], from_core[2]])
    go = jnp.stack([kept[1], from_core[1], kept[3], from_core[3]])

    keys_before = after(keys_before, values)
    key_w_core, value_w_core = swap_core(key_w), swap_core(value_w)
    e, stat, dv_own, dv_before = attend_scores(
        code, q, go, keys, keys_before, key_mark, query_mark, gain_q
    )
    dv_back = along_z(dv_before, backward)
    values_before = after(values_before, e, key_w_core, value_w_core)
    near, sent_back, dk_own, dk_before = attend_values(
        code, q, go, keys, keys_before, values, values_before, gain_q, e, stat
    )
    dk_back = along_z(dk_before, backward)
    value_grad = (dv_own + after(dv_back, dk_own).astype(jnp.float32)).astype(jnp.bfloat16)
    value_grad_far = swap_uly(value_grad)

    near_other = swap_core(sent_back)
    far = pack(near, near_other)
    back_x = swap_x(far)

    v_first, v_second = weight_grad(code, value_grad, after(value_grad_far, far), acts)
    v_third, v_outer = along_z(v_second, BACK_THIRD), along_z(v_first, BACK_OUTER)
    dkey = dk_own + after(dk_back, v_first).astype(jnp.float32)
    key_grad = normalized_pull(key_raw, k_gain, 1.0, dkey).astype(jnp.bfloat16)
    key_grad_far = swap_uly(key_grad)
    grads = (key_grad, key_grad_far, value_grad, value_grad_far)
    grads_core = tuple(swap_core(grad) for grad in grads)
    k_first, k_second = weight_grad(code, key_grad, key_grad_far, acts)
    k_third = along_z(k_second, BACK_THIRD)
    back_x = after(back_x, k_first)
    grads = grads[:2] + after_all(grads_core[:2], back_x) + grads[2:] + grads_core[2:]
    weights = (key_w, key_w_core, value_w, value_w_core)
    away = input_grad(code, 2, grads, weights, rows)
    from_x = swap_x(away)
    v_third, v_outer = after_all((v_third, v_outer), away)
    v_mid_payload, v_inner_payload = sums((v_first, v_third), (v_second, v_outer))
    v_mid, v_inner = along_z(v_mid_payload, BACK_MID), along_z(v_inner_payload, BACK_INNER)
    k_third = after(k_third, v_mid_payload)
    (k_mid_payload,) = sums((k_first, k_third))
    key_grad_far = after(key_grad_far, k_mid_payload)
    kept = input_grad(code, 0, (key_grad, key_grad_far) + grads[2:], weights, rows)
    k_mid, k_outer = along_z(k_mid_payload, BACK_MID), along_z(after(k_first, k_third), BACK_OUTER)
    v_mid, v_inner = after_all((v_mid, v_inner), kept)
    (v_one_payload,) = sums((v_first, v_mid))
    v_one = along_z(v_one_payload, BACK_ONE)
    attention, grad_q = by_head(code, near, near_other, after(back_x, v_one_payload, v_inner))
    k_mid, k_outer = after_all((k_mid, k_outer), attention)
    k_one_payload, k_inner_payload = sums((k_first, k_mid), (k_second, k_outer))
    k_one, k_inner = along_z(k_one_payload, BACK_ONE), along_z(k_inner_payload, BACK_INNER)

    def to_core(away):
        return move(
            away, [((z, x, z % 2), (z, x, 1 - z % 2)) for z in range(4) for x in (0, 1)]
        )

    from_x = after(from_x, k_inner_payload)
    (grad_normed,) = sums((kept, from_x))
    v_one = after(v_one, grad_normed)
    value_own, value_away = halves(code, (v_second, v_inner, v_one))
    grad_value_weight = owned(code, value_own, to_core(value_away))
    k_one, k_inner = after_all((k_one, k_inner), grad_value_weight)
    key_own, key_away = halves(code, (k_second, k_inner, k_one))
    grad_key_weight = owned(code, key_own, to_core(key_away))
    return (attention, grad_normed, grad_q, grad_key_weight, grad_value_weight)


def body(normed, q_raw, *rest):
    planes = (
        lax.axis_size("seq") == 16
        and lax.axis_size("uly") == 2
        and 4 * normed.shape[0] == WINDOW
        and q_raw.shape[1] == 8 * HD
    )
    return (body_planes if planes else body_general)(normed, q_raw, *rest)


def solution(mesh):
    return jax.shard_map(
        body,
        mesh=mesh,
        in_specs=(
            P("seq", "uly"),
            P("seq", "uly"),
            P("uly", "seq"),
            P("uly", "seq"),
            P(),
            P(),
            P(),
            P("seq", "uly"),
        ),
        out_specs=(
            P("seq", "uly"),
            P("seq", "uly"),
            P("seq", "uly"),
            P("uly", "seq"),
            P("uly", "seq"),
        ),
        check_vma=False,
    )
```

```python
import functools

import jax
import jax.numpy as jnp
from jax import lax
from jax.experimental import pallas as pl
from jax.experimental.pallas import tpu as pltpu
from jax.sharding import PartitionSpec as P

HD = 128
WINDOW = 1024


epsilon = 1e-06
query_scale = 168.0 ** (-0.5)


def from_behind(array, axis, by):
    devices = lax.axis_size(axis)
    pairs = [(i, i + by) for i in range(devices) if 0 <= i + by < devices]
    return lax.ppermute(array, axis, pairs)


def normalize(raw_vals, gain, factor):
    mean_sq = jnp.mean(raw_vals * raw_vals, axis=-1, keepdims=True)
    return raw_vals * lax.rsqrt(mean_sq + epsilon) * gain * factor


def attend_block(
    queries, key_block, value_block, grad_block, query_pos, key_pos, query_seg, key_seg
):
    scores = jnp.einsum("bhge,lhe->hgbl", queries, key_block, preferred_element_type=jnp.float32)
    allowed = (
        (key_pos[None, :] <= query_pos[:, None])
        & (key_pos[None, :] > query_pos[:, None] - WINDOW)
        & (key_seg[None, :] == query_seg[:, None])
    )
    exp_scores = jnp.where(allowed[None, None], jnp.exp(scores), 0.0)
    probs = exp_scores / jnp.sum(exp_scores, axis=-1, keepdims=True)
    weights = probs.astype(jnp.bfloat16)
    attended = jnp.einsum(
        "hgbl,lhe->bhge", weights, value_block, preferred_element_type=jnp.float32
    ).astype(jnp.bfloat16)
    dprob = jnp.einsum(
        "bhge,lhe->hgbl", grad_block, value_block, preferred_element_type=jnp.float32
    )
    delta_row = jnp.sum(probs * dprob, axis=-1, keepdims=True)
    dscore = (probs * (dprob - delta_row)).astype(jnp.bfloat16)
    dquery = jnp.einsum("hgbl,lhe->bhge", dscore, key_block, preferred_element_type=jnp.float32)
    dkey = jnp.einsum("hgbl,bhge->lhe", dscore, queries, preferred_element_type=jnp.float32)
    dvalue = jnp.einsum("hgbl,bhge->lhe", weights, grad_block, preferred_element_type=jnp.float32)
    return (attended, dquery, dkey, dvalue)


def body_general(normed, q_raw, key_weight, value_weight, q_gain, k_gain, segment_ids, grad_out):
    rows_here = normed.shape[0]
    heads_here = q_raw.shape[1] // (2 * HD)
    seq_index = lax.axis_index("seq")
    base_row = seq_index * rows_here
    weight_pair = (
        lax.all_gather(key_weight, "seq", axis=1, tiled=True),
        lax.all_gather(value_weight, "seq", axis=1, tiled=True),
    )
    key_term = jnp.dot(normed, weight_pair[0], preferred_element_type=jnp.float32)
    value_term = jnp.dot(normed, weight_pair[1], preferred_element_type=jnp.float32)
    key_raw, value_raw = (
        lax.psum_scatter(
            key_term.astype(jnp.bfloat16), "uly", scatter_dimension=1, tiled=True
        ).astype(jnp.float32),
        lax.psum_scatter(
            value_term.astype(jnp.bfloat16), "uly", scatter_dimension=1, tiled=True
        ).astype(jnp.float32),
    )
    key_in = key_raw.reshape(rows_here, heads_here, HD)
    keys_bf = normalize(key_in, k_gain, 1.0).astype(jnp.bfloat16)
    values_bf = value_raw.reshape(rows_here, heads_here, HD).astype(jnp.bfloat16)
    query_in = q_raw.astype(jnp.float32).reshape(rows_here, heads_here, 2, HD)
    queries = normalize(query_in, q_gain, query_scale).astype(jnp.bfloat16)
    grad_heads = grad_out.reshape(rows_here, heads_here, 2, HD)
    stacked = jnp.stack([keys_bf, values_bf])
    distance_most = -(-WINDOW // rows_here)
    pieces = []
    for distance in range(distance_most, 0, -1):
        first_row = max(0, distance * rows_here - WINDOW)
        pieces.append(from_behind(stacked, "seq", distance))
    pieces.append(stacked)
    extended = jnp.concatenate(pieces, axis=1)
    block_rows = min(512, rows_here)
    span_rows = block_rows + WINDOW
    count_blocks = rows_here // block_rows
    seg_pad = jnp.concatenate([jnp.full((WINDOW,), -1, jnp.int32), segment_ids])
    query_seg_all = lax.dynamic_slice_in_dim(segment_ids, base_row, rows_here, 0)
    key_seg_all = lax.dynamic_slice_in_dim(seg_pad, base_row, WINDOW + rows_here, 0)

    def step(grad_acc, block_index):
        begin_row = block_index * block_rows
        query_pos = base_row + begin_row + jnp.arange(block_rows, dtype=jnp.int32)
        key_pos = base_row + begin_row - WINDOW + jnp.arange(span_rows, dtype=jnp.int32)
        key_block = lax.dynamic_slice_in_dim(extended, begin_row, span_rows, 1)
        attended, dquery, dkey, dvalue = attend_block(
            lax.dynamic_slice_in_dim(queries, begin_row, block_rows, 0),
            key_block[0],
            key_block[1],
            lax.dynamic_slice_in_dim(grad_heads, begin_row, block_rows, 0),
            query_pos,
            key_pos,
            lax.dynamic_slice_in_dim(query_seg_all, begin_row, block_rows, 0),
            lax.dynamic_slice_in_dim(key_seg_all, begin_row, span_rows, 0),
        )
        update = jnp.stack([dkey, dvalue])
        grad_acc = lax.dynamic_update_slice_in_dim(
            grad_acc,
            lax.dynamic_slice_in_dim(grad_acc, begin_row, span_rows, 1) + update,
            begin_row,
            1,
        )
        return (grad_acc, (attended, dquery))

    zero_acc = jnp.zeros((2, WINDOW + rows_here, heads_here, HD), jnp.float32)
    grad_acc, (attended, dquery) = lax.scan(
        step, zero_acc, jnp.arange(count_blocks, dtype=jnp.int32)
    )
    attention = attended.reshape(rows_here, 2 * heads_here * HD)
    dquery = dquery.reshape(rows_here, heads_here, 2, HD)
    own_grads = grad_acc[:, WINDOW:]
    offset_row = 0
    for distance in range(distance_most, 0, -1):
        first_row = max(0, distance * rows_here - WINDOW)
        piece_rows = rows_here - first_row
        outgoing = grad_acc[:, offset_row : offset_row + piece_rows]
        returned = from_behind(outgoing.astype(jnp.bfloat16), "seq", -distance).astype(
            outgoing.dtype
        )
        own_grads = own_grads.at[:, first_row:].add(returned)
        offset_row = offset_row + piece_rows
    _, pull_query = jax.vjp(lambda raw_vals: normalize(raw_vals, q_gain, query_scale), query_in)
    grad_q = pull_query(dquery)[0].astype(jnp.bfloat16).reshape(rows_here, 2 * heads_here * HD)
    _, pull_key = jax.vjp(lambda raw_vals: normalize(raw_vals, k_gain, 1.0), key_in)
    key_grad = pull_key(own_grads[0])[0].astype(jnp.bfloat16).reshape(rows_here, heads_here * HD)
    value_grad = own_grads[1].astype(jnp.bfloat16).reshape(rows_here, heads_here * HD)
    key_all, value_all = (
        lax.all_gather(key_grad, "uly", axis=1, tiled=True),
        lax.all_gather(value_grad, "uly", axis=1, tiled=True),
    )
    dims_last = (((1,), (1,)), ((), ()))
    total = lax.dot_general(key_all, weight_pair[0], dims_last, preferred_element_type=jnp.float32)
    total = total + lax.dot_general(
        value_all, weight_pair[1], dims_last, preferred_element_type=jnp.float32
    )
    grad_normed = total.astype(jnp.bfloat16)
    dims_first = (((0,), (0,)), ((), ()))
    key_part = lax.dot_general(normed, key_all, dims_first, preferred_element_type=jnp.float32)
    value_part = lax.dot_general(normed, value_all, dims_first, preferred_element_type=jnp.float32)
    grad_key_weight = lax.psum_scatter(
        key_part.astype(jnp.bfloat16), "seq", scatter_dimension=1, tiled=True
    ).astype(jnp.float32)
    grad_value_weight = lax.psum_scatter(
        value_part.astype(jnp.bfloat16), "seq", scatter_dimension=1, tiled=True
    ).astype(jnp.float32)
    return (attention, grad_normed, grad_q, grad_key_weight, grad_value_weight)


MIB = 1 << 20
MASKED = 16384.0
LOG2_E = 1.4426950408889634
NT = (((1,), (1,)), ((), ()))
HBM = pl.BlockSpec(memory_space=pltpu.HBM)
SMEM = pl.BlockSpec(memory_space=pltpu.SMEM)
VMEM = pl.BlockSpec(memory_space=pltpu.VMEM)


def at(z, x, c):
    return (z * 2 + x) * 2 + c


def move(array, rule):
    return lax.ppermute(array, "seq", [(at(*a), at(*b)) for a, b in rule])


def along_z(array, hops):
    return move(array, [((z, x, c), (to, x, c)) for z, c, to in hops for x in (0, 1)])


def swap_core(array):
    return move(
        array, [((z, x, c), (z, x, 1 - c)) for z in range(4) for x in (0, 1) for c in (0, 1)]
    )


def swap_x(array):
    return move(
        array, [((z, x, c), (z, 1 - x, c)) for z in range(4) for x in (0, 1) for c in (0, 1)]
    )


def swap_uly(array):
    return lax.ppermute(array, "uly", [(0, 1), (1, 0)])


def call(kernel, out_shape, vmem, **rest):
    return pl.pallas_call(
        kernel,
        out_shape=out_shape,
        compiler_params=pltpu.CompilerParams(vmem_limit_bytes=vmem * MIB),
        cost_estimate=pl.CostEstimate(flops=0, bytes_accessed=0, transcendentals=0),
        **rest,
    )


def shaped(shape, dtype=jnp.bfloat16):
    return jax.ShapeDtypeStruct(shape, dtype)


def after_all(arrays, *earlier):
    return lax.optimization_barrier(tuple(arrays) + earlier)[: len(arrays)]


def after(array, *earlier):
    return after_all((array,), *earlier)[0]


HOP_ONE = [(0, 0, 1), (3, 1, 2), (1, 1, 0), (2, 0, 3)]
HOP_INNER = [(1, 1, 2), (2, 0, 1)]
HOP_SECOND = [(1, 0, 2), (2, 1, 1)]
HOP_OUTER = [(1, 0, 0), (2, 1, 3)]
HOP_THIRD = [(2, 0, 3), (1, 1, 0)]
BACK_THIRD, BACK_OUTER, BACK_MID, BACK_INNER, BACK_ONE = (
    [(to, c, z) for z, c, to in hops]
    for hops in (HOP_THIRD, HOP_OUTER, HOP_SECOND, HOP_INNER, HOP_ONE)
)

CHAIN = ((0, 1, 1, 0, 3, 2, 5, 4), (4, 5, 2, 3, 0, 1, 1, 0))


def sums_kernel(counts, *refs):
    terms, outs = refs[: sum(counts)], refs[sum(counts) :]
    for out, count in zip(outs, counts):
        total = terms[0][...].astype(jnp.float32)
        for term in terms[1:count]:
            total = total + term[...].astype(jnp.float32)
        out[...] = total.astype(out.dtype)
        terms = terms[count:]


def sums(*groups):
    terms = [term for group in groups for term in group]
    return call(
        functools.partial(sums_kernel, [len(group) for group in groups]),
        [shaped(group[0].shape) for group in groups],
        12,
        in_specs=[VMEM] * len(terms),
        out_specs=[VMEM] * len(groups),
        name="sums",
    )(*terms)


def halves_kernel(code, a, b, c, own, away):
    width = own.shape[0]
    total = a[...].astype(jnp.float32) + b[...].astype(jnp.float32) + c[...].astype(jnp.float32)
    low = code[4] == 0
    own[...] = jnp.where(low, total[:width], total[width:])
    away[...] = jnp.where(low, total[width:], total[:width]).astype(jnp.bfloat16)


def halves(code, parts):
    width, features = parts[0].shape
    return call(
        halves_kernel,
        [shaped((width // 2, features), jnp.float32), shaped((width // 2, features))],
        12,
        in_specs=[SMEM] + [VMEM] * 3,
        out_specs=[VMEM] * 2,
        name="halves",
    )(code, *parts)


def owned_kernel(code, own, other, out):
    out[...] = jnp.where(code[6] == 1, own[...], other[...].astype(jnp.float32))


def owned(code, own, other):
    return call(
        owned_kernel,
        shaped(own.shape, jnp.float32),
        12,
        in_specs=[SMEM] + [VMEM] * 2,
        out_specs=VMEM,
        name="owned",
    )(code, own, other).T


def pack_kernel(first, second, out):
    out[0] = first[1]
    out[1] = second[1]


def pack(first, second):
    return call(
        pack_kernel, shaped(second.shape), 12, in_specs=[VMEM] * 2, out_specs=VMEM, name="pack"
    )(first, second)


def by_head_kernel(code, near, near_other, far, attention, grad_q):
    lanes = near.shape[3]
    core, x = code[4], code[5]
    for which, out in enumerate((attention, grad_q)):
        for k, side, source in (
            (core, x, near.at[0, which]),
            (1 - core, x, near_other.at[0, which]),
            (core, 1 - x, far.at[0, which]),
            (1 - core, 1 - x, far.at[1, which]),
        ):
            out[:, pl.ds(pl.multiple_of((2 * k + side) * lanes, lanes), lanes)] = source[...]


def by_head(code, near, near_other, far):
    _, _, rows, lanes = near.shape
    return call(
        by_head_kernel,
        [shaped((rows, 4 * lanes))] * 2,
        12,
        in_specs=[SMEM] + [VMEM] * 3,
        out_specs=[VMEM] * 2,
        name="by_head",
    )(code, near, near_other, far)


def slot_copies(code, slot_at, refs, buffer, sems, act):
    for k, ref in enumerate(refs):

        @pl.when(slot_at == k)
        def _():
            copy = pltpu.make_async_copy(ref, buffer, sems)
            copy.start() if act else copy.wait()


def project_kernel(code, *refs):
    acts, weights = refs[:4], refs[4:-4]
    mine, theirs, w_v, w_sem = refs[-4:]
    width = mine.shape[1]
    rows = acts[0].shape[0]

    def weight_copies(act):
        for slot in range(2):
            slot_copies(
                code, code[1 + slot], weights, w_v.at[pl.ds(slot * width, width)], w_sem.at[slot], act
            )

    weight_copies(True)
    weight_copies(False)
    for j in range(4):
        here = pl.ds(pl.multiple_of((code[0] ^ j) * rows, rows), rows)
        both = lax.dot_general(acts[j][...], w_v[...], NT, preferred_element_type=jnp.float32)
        mine[here, :] = both[:, :width].astype(jnp.bfloat16)
        theirs[here, :] = both[:, width:].astype(jnp.bfloat16)


def project(code, acts, weights):
    rows, features = acts[0].shape
    width = weights[0].shape[0]
    return call(
        project_kernel,
        [shaped((4 * rows, width)), shaped((4 * rows, width)), shaped((2 * width, features))],
        12,
        in_specs=[SMEM] + [VMEM] * 4 + [HBM] * len(weights),
        out_specs=[VMEM, VMEM, VMEM],
        scratch_shapes=[
            pltpu.SemaphoreType.DMA((2,)),
        ],
        name="project",
    )(code, *acts, *weights)


def normalized(raw, gain, factor):
    inverse = lax.rsqrt(jnp.mean(raw * raw, axis=-1, keepdims=True) + epsilon)
    return raw * inverse * gain * factor


def normalized_pull(raw, gain, factor, cotangent):
    inverse = lax.rsqrt(jnp.mean(raw * raw, axis=-1, keepdims=True) + epsilon)
    scaled = cotangent * gain * factor
    along = jnp.mean(scaled * raw, axis=-1, keepdims=True)
    return inverse * (scaled - raw * (inverse * inverse * along))


def dot(a, b):
    return jnp.dot(a, b, preferred_element_type=jnp.float32)


def scores_kernel(
    code, q_ref, go_ref, own_ref, before_ref, key_mark, query_mark, gain_ref,
    e_ref, stat_ref, dv_own, dv_before, keys_v, acc
):
    block = pl.program_id(0)
    rows = q_ref.shape[1]
    chunks = e_ref.shape[1] // rows
    half = own_ref.shape[0]

    @pl.when(block == 0)
    def _():
        keys_v[:half, :HD] = before_ref[...]
        keys_v[half:, :HD] = own_ref[...]
        keys_v[:, HD:] = key_mark[...]
        acc[...] = jnp.zeros_like(acc)

    key_at = lax.broadcasted_iota(jnp.int32, (rows, 2 * rows), 0)
    query_at = lax.broadcasted_iota(jnp.int32, (rows, 2 * rows), 1)
    behind = key_at <= jnp.where(query_at >= rows, query_at - rows, query_at)
    heads, grads = [], []
    for g in range(2):
        lanes = slice(g * HD, (g + 1) * HD)
        query = normalized(q_ref[0, :, lanes].astype(jnp.float32), gain_ref[...], query_scale * LOG2_E)
        heads.append(jnp.concatenate([query.T.astype(jnp.bfloat16), query_mark[...]], axis=0))
        grads.append(go_ref[0, :, lanes].astype(jnp.float32).T)
    query_t = jnp.concatenate(heads, axis=1)
    span = pl.ds(pl.multiple_of(block * rows, rows), chunks * rows)
    e = jnp.exp2(dot(keys_v[span, :], query_t))
    e = jnp.concatenate(
        [
            jnp.where(behind, 0.0, e[:rows]),
            e[rows:-rows],
            jnp.where(behind, e[-rows:], 0.0),
        ],
        axis=0,
    )
    total = jnp.sum(e, axis=0, keepdims=True)
    e = e.astype(jnp.bfloat16)
    e_ref[0] = e
    inverse = 1.0 / total
    stat_ref[0] = jnp.broadcast_to(inverse, stat_ref.shape[1:])
    grad = (jnp.concatenate(grads, axis=1) * inverse).T.astype(jnp.bfloat16)
    acc[span, :] = acc[span, :] + dot(e, grad)

    @pl.when(block == pl.num_programs(0) - 1)
    def _():
        dv_before[...] = acc[:half, :].astype(jnp.bfloat16)
        dv_own[...] = acc[half:, :]


def whole(shape):
    return pl.BlockSpec(shape, lambda b, code: (0,) * len(shape))


def attend_scores(code, q, go, keys, keys_before, key_mark, query_mark, gain):
    blocks, rows, _ = q.shape
    half = blocks * rows
    span = half + rows
    picked = pl.BlockSpec((1, rows, 2 * HD), lambda b, code: (b ^ code[0], 0, 0))
    return call(
        scores_kernel,
        [
            shaped((blocks, span, 2 * rows)),
            shaped((blocks, 8, 2 * rows), jnp.float32),
            shaped((half, HD), jnp.float32),
            shaped((half, HD)),
        ],
        14,
        grid_spec=pltpu.PrefetchScalarGridSpec(
            num_scalar_prefetch=1,
            grid=(blocks,),
            in_specs=[
                picked,
                picked,
                whole((half, HD)),
                whole((half, HD)),
                whole((2 * half, HD)),
                pl.BlockSpec((HD, rows), lambda b, code: (0, b)),
                whole((1, HD)),
            ],
            out_specs=[
                pl.BlockSpec((1, span, 2 * rows), lambda b, code: (b, 0, 0)),
                pl.BlockSpec((1, 8, 2 * rows), lambda b, code: (b, 0, 0)),
                whole((half, HD)),
                whole((half, HD)),
            ],
            scratch_shapes=[
                pltpu.VMEM((2 * half, 2 * HD), jnp.bfloat16),
                pltpu.VMEM((2 * half, HD), jnp.float32),
            ],
        ),
        name="attend_scores",
    )(code, q, go, keys, keys_before, key_mark, query_mark, gain)


def values_kernel(
    code, q_ref, go_ref, own_ref, before_ref, v_own, v_before, gain_ref, e_ref, stat_ref,
    kept, sent, dk_own, dk_before, values_v, values_t, keys_t, acc
):
    block = pl.program_id(0)
    rows = q_ref.shape[1]
    span_rows = e_ref.shape[1]
    half = own_ref.shape[0]

    @pl.when(block == 0)
    def _():
        values_v[:half, :] = v_before[...]
        values_v[half:, :] = v_own[...]
        values_t[...] = values_v[...].astype(jnp.float32).T.astype(jnp.bfloat16)
        keys_t[:, :half] = before_ref[...].astype(jnp.float32).T.astype(jnp.bfloat16)
        keys_t[:, half:] = own_ref[...].astype(jnp.float32).T.astype(jnp.bfloat16)
        acc[...] = jnp.zeros_like(acc)

    piece = block ^ code[0]
    odd = (piece % 2 == 1) & jnp.ones((rows, HD), jnp.bool_)

    def put(which, lanes, result):
        for target, here in ((kept, ~odd), (sent, odd)):
            at_piece = target.at[piece // 2, which, :, lanes]
            at_piece[...] = jnp.where(here, result, at_piece[...])

    span = pl.ds(pl.multiple_of(block * rows, rows), span_rows)
    raws = [q_ref[0, :, g * HD : (g + 1) * HD].astype(jnp.float32) for g in range(2)]
    queries = jnp.concatenate(
        [normalized(raw, gain_ref[...], query_scale).astype(jnp.bfloat16) for raw in raws], axis=0
    )
    grad_t = jnp.concatenate(
        [go_ref[0, :, g * HD : (g + 1) * HD].astype(jnp.float32).T for g in range(2)], axis=1
    )
    inverse = stat_ref[0, :1, :]
    e = e_ref[0]
    out_t = dot(values_t[:, span], e) * inverse
    along = jnp.sum(out_t * grad_t, axis=0, keepdims=True) * inverse
    scaled = (grad_t * inverse).astype(jnp.bfloat16)
    dprob = dot(values_v[span, :], scaled)
    dscore = e * (dprob - along).astype(jnp.bfloat16)
    acc[span, :] = acc[span, :] + dot(dscore, queries)
    dquery_t = dot(keys_t[:, span], dscore)
    for g in range(2):
        lanes = slice(g * HD, (g + 1) * HD)
        across = slice(g * rows, (g + 1) * rows)
        put(0, lanes, out_t[:, across].T.astype(jnp.bfloat16))
        pulled = normalized_pull(raws[g], gain_ref[...], query_scale, dquery_t[:, across].T)
        put(1, lanes, pulled.astype(jnp.bfloat16))

    @pl.when(block == pl.num_programs(0) - 1)
    def _():
        dk_before[...] = acc[:half, :].astype(jnp.bfloat16)
        dk_own[...] = acc[half:, :]


def attend_values(code, q, go, keys, keys_before, values, values_before, gain, e, stat):
    blocks, rows, _ = q.shape
    half = blocks * rows
    span = half + rows
    picked = pl.BlockSpec((1, rows, 2 * HD), lambda b, code: (b ^ code[0], 0, 0))
    return call(
        values_kernel,
        [
            shaped((2, 2, rows, 2 * HD)),
            shaped((2, 2, rows, 2 * HD)),
            shaped((half, HD), jnp.float32),
            shaped((half, HD)),
        ],
        16,
        grid_spec=pltpu.PrefetchScalarGridSpec(
            num_scalar_prefetch=1,
            grid=(blocks,),
            in_specs=[picked, picked]
            + [whole((half, HD))] * 4
            + [
                whole((1, HD)),
                pl.BlockSpec((1, span, 2 * rows), lambda b, code: (b, 0, 0)),
                pl.BlockSpec((1, 8, 2 * rows), lambda b, code: (b, 0, 0)),
            ],
            out_specs=[
                whole((2, 2, rows, 2 * HD)),
                whole((2, 2, rows, 2 * HD)),
                whole((half, HD)),
                whole((half, HD)),
            ],
            scratch_shapes=[
                pltpu.VMEM((2 * half, HD), jnp.bfloat16),
                pltpu.VMEM((HD, 2 * half), jnp.bfloat16),
                pltpu.VMEM((HD, 2 * half), jnp.bfloat16),
                pltpu.VMEM((2 * half, HD), jnp.float32),
            ],
        ),
        name="attend_values",
    )(code, q, go, keys, keys_before, values, values_before, gain, e, stat)


def weight_grad_kernel(code, mine, theirs, a0, a1, a2, a3, far, mid):
    acts = (a0, a1, a2, a3)
    rows, features = a0.shape
    width = far.shape[0]
    first = code[3] == 1
    grads = []
    for j in range(4):
        span = pl.ds(pl.multiple_of((code[0] ^ j) * rows, rows), rows)
        own = mine[span, :].astype(jnp.float32).T
        other = theirs[span, :].astype(jnp.float32).T
        both = (jnp.where(first, own, other), jnp.where(first, other, own))
        grads.append(jnp.concatenate(both, axis=0).astype(jnp.bfloat16))
    tile = features // 3
    for n in range(3):
        lanes = slice(n * tile, (n + 1) * tile)
        both = dot(grads[0], acts[0][:, lanes])
        for j in range(1, 4):
            both = both + dot(grads[j], acts[j][:, lanes])
        far[:, lanes] = both[:width].astype(jnp.bfloat16)
        mid[:, lanes] = both[width:].astype(jnp.bfloat16)


def weight_grad(code, mine, theirs, acts):
    rows, features = acts[0].shape
    width = mine.shape[1]
    return call(
        weight_grad_kernel,
        [shaped((width, features)), shaped((width, features))],
        12,
        in_specs=[SMEM] + [VMEM] * 6,
        out_specs=[VMEM, VMEM],
        name="weight_grad",
    )(code, mine, theirs, *acts)


def input_grad_kernel(piece, code, *refs):
    grads, weights, out = refs[:8], refs[8:12], refs[12]
    rows, features = out.shape
    span = pl.ds(pl.multiple_of((code[0] ^ piece) * rows, rows), rows)
    parts = [
        jnp.concatenate([ref[span, :] for ref in grads[2 * k : 2 * k + 2]], axis=1) for k in range(4)
    ]
    tile = features // 3
    for n in range(3):
        lanes = slice(n * tile, (n + 1) * tile)
        total = dot(parts[0], weights[0][:, lanes])
        for k in range(1, 4):
            total = total + dot(parts[k], weights[k][:, lanes])
        out[:, lanes] = total.astype(jnp.bfloat16)


def input_grad(code, piece, grads, weights, rows):
    features = weights[0].shape[1]
    return call(
        functools.partial(input_grad_kernel, piece),
        shaped((rows, features)),
        16,
        in_specs=[SMEM] + [VMEM] * 12,
        out_specs=VMEM,
        name="input_grad",
    )(code, *grads, *weights)


def body_planes(normed, q_raw, key_weight, value_weight, q_gain, k_gain, segment_ids, grad_out):
    rows, features = normed.shape
    half = 4 * rows
    width = key_weight.shape[1]
    place = lax.axis_index("seq")
    uly = lax.axis_index("uly")
    z, x, c = place // 4, (place // 2) % 2, place % 2

    on_line = z * 2 + c
    chosen = [
        jnp.asarray(CHAIN, jnp.int32)[slot, on_line] for slot in (uly, 1 - uly)
    ]
    inner = (z == 1) | (z == 2)
    first_is_own = jnp.where(inner, c, 1 - c) == uly
    code = jnp.stack([place % 4, *chosen, first_is_own, c, x, c == z % 2]).astype(jnp.int32)
    gain_q = q_gain.reshape(1, HD)

    def picked(first_is_low, low, high):
        return jnp.where(first_is_low, low, high)

    normed_x = swap_x(normed)

    def slab(weight):
        other = move(
            weight.T, [((z, x, 1 - z % 2), (z, x, z % 2)) for z in range(4) for x in (0, 1)]
        )
        both = (picked(c == 0, weight.T, other), picked(c == 0, other, weight.T))
        return jnp.concatenate(both, axis=0)

    key_slab = slab(key_weight)
    value_slab = slab(value_weight)

    k_one, k_inner = along_z(key_slab, HOP_ONE), along_z(key_slab, HOP_INNER)
    v_one, v_inner = along_z(value_slab, HOP_ONE), along_z(value_slab, HOP_INNER)
    normed_c = swap_core(after(normed, key_slab))
    k_one, k_inner = after_all((k_one, k_inner), code)
    k_second, k_outer = along_z(k_one, HOP_SECOND), along_z(k_inner, HOP_OUTER)
    v_one, v_inner = after_all((v_one, v_inner), k_one, k_inner)
    v_second, v_outer = along_z(v_one, HOP_SECOND), along_z(v_inner, HOP_OUTER)
    k_second, k_outer = after_all((k_second, k_outer), v_one, v_inner)
    k_third = along_z(k_second, HOP_THIRD)
    normed_x = after(normed_x, k_second, k_outer)
    normed_xc = swap_core(normed_x)

    def head(array, index):
        return array[:, index * 2 * HD : (index + 1) * 2 * HD]

    sources = after_all((q_raw, grad_out), normed_x)
    from_x = swap_x(
        jnp.stack([picked(x == 1, head(a, 2 * k), head(a, 2 * k + 1)) for a in sources for k in (0, 1)])
    )
    near = [picked(x == 0, head(a, 2 * k), head(a, 2 * k + 1)) for a in sources for k in (0, 1)]
    v_second, v_outer = after_all((v_second, v_outer), normed_x, k_second)
    v_third = along_z(v_second, HOP_THIRD)

    segments = after(segment_ids, v_second, v_outer)
    seg_pad = jnp.concatenate([jnp.full((half,), -1, jnp.int32), segments])
    key_seg = lax.dynamic_slice_in_dim(seg_pad, z * half, 2 * half, 0)
    query_seg = lax.dynamic_slice_in_dim(segments, z * half, half, 0)
    lane = lax.broadcasted_iota(jnp.int32, (2 * half, HD), 1)
    key_mark = jnp.where((lane < 2) & (lane != key_seg[:, None]), -MASKED, 0.0).astype(jnp.bfloat16)
    row = lax.broadcasted_iota(jnp.int32, (HD, half), 0)
    query_mark = jnp.where(row == query_seg[None, :], 1.0, 0.0).astype(jnp.bfloat16)

    forward = [(z, c, z + 1) for z in range(3) for c in (0, 1)]
    backward = [(z + 1, c, z) for z in range(3) for c in (0, 1)]

    acts = (normed, normed_c, normed_x, normed_xc)
    k_third = after(k_third, v_second, v_outer)
    key_weights = (key_slab, k_one, k_inner, k_second, k_outer, k_third)
    mine, theirs, key_w = project(code, acts, key_weights)
    key_far = swap_uly(theirs)
    from_x = after(from_x, theirs)
    arrays = [near[0], near[1], near[2], near[3], from_x[0], from_x[1], from_x[2], from_x[3]]
    from_core = swap_core(
        jnp.stack([picked(c == 1, arrays[2 * k], arrays[2 * k + 1]) for k in range(4)])
    )
    kept = [picked(c == 0, arrays[2 * k], arrays[2 * k + 1]) for k in range(4)]

    value_weights = (value_slab, v_one, v_inner, v_second, v_outer, after(v_third, theirs))
    value_mine, value_theirs, value_w = project(code, acts, value_weights)
    value_far = swap_uly(value_theirs)
    key_far = after(key_far, value_theirs)
    key_raw = mine.astype(jnp.float32) + key_far.astype(jnp.float32)
    keys = normalized(key_raw, k_gain, 1.0).astype(jnp.bfloat16)
    keys_before = along_z(keys, forward)
    value_far, from_core = after_all((value_far, from_core), keys)
    values = (value_mine.astype(jnp.float32) + value_far.astype(jnp.float32)).astype(jnp.bfloat16)
    values_before = along_z(values, forward)
    q = jnp.stack([kept[0], from_core[0], kept[2], from_core[2]])
    go = jnp.stack([kept[1], from_core[1], kept[3], from_core[3]])

    keys_before = after(keys_before, values)
    key_w_core, value_w_core = swap_core(key_w), swap_core(value_w)
    e, stat, dv_own, dv_before = attend_scores(
        code, q, go, keys, keys_before, key_mark, query_mark, gain_q
    )
    dv_back = along_z(dv_before, backward)
    values_before = after(values_before, e, key_w_core, value_w_core)
    near, sent_back, dk_own, dk_before = attend_values(
        code, q, go, keys, keys_before, values, values_before, gain_q, e, stat
    )
    dk_back = along_z(dk_before, backward)
    value_grad = (dv_own + after(dv_back, dk_own).astype(jnp.float32)).astype(jnp.bfloat16)
    value_grad_far = swap_uly(value_grad)

    near_other = swap_core(sent_back)
    far = pack(near, near_other)
    back_x = swap_x(far)

    v_first, v_second = weight_grad(code, value_grad, after(value_grad_far, far), acts)
    v_third, v_outer = along_z(v_second, BACK_THIRD), along_z(v_first, BACK_OUTER)
    dkey = dk_own + after(dk_back, v_first).astype(jnp.float32)
    key_grad = normalized_pull(key_raw, k_gain, 1.0, dkey).astype(jnp.bfloat16)
    key_grad_far = swap_uly(key_grad)
    grads = (key_grad, key_grad_far, value_grad, value_grad_far)
    grads_core = tuple(swap_core(grad) for grad in grads)
    k_first, k_second = weight_grad(code, key_grad, key_grad_far, acts)
    k_third = along_z(k_second, BACK_THIRD)
    back_x = after(back_x, k_first)
    grads = grads[:2] + after_all(grads_core[:2], back_x) + grads[2:] + grads_core[2:]
    weights = (key_w, key_w_core, value_w, value_w_core)
    away = input_grad(code, 2, grads, weights, rows)
    from_x = swap_x(away)
    v_third, v_outer = after_all((v_third, v_outer), away)
    v_mid_payload, v_inner_payload = sums((v_first, v_third), (v_second, v_outer))
    v_mid, v_inner = along_z(v_mid_payload, BACK_MID), along_z(v_inner_payload, BACK_INNER)
    k_third = after(k_third, v_mid_payload)
    (k_mid_payload,) = sums((k_first, k_third))
    key_grad_far = after(key_grad_far, k_mid_payload)
    kept = input_grad(code, 0, (key_grad, key_grad_far) + grads[2:], weights, rows)
    k_mid, k_outer = along_z(k_mid_payload, BACK_MID), along_z(after(k_first, k_third), BACK_OUTER)
    v_mid, v_inner = after_all((v_mid, v_inner), kept)
    (v_one_payload,) = sums((v_first, v_mid))
    v_one = along_z(v_one_payload, BACK_ONE)
    attention, grad_q = by_head(code, near, near_other, after(back_x, v_one_payload, v_inner))
    k_mid, k_outer = after_all((k_mid, k_outer), attention)
    k_one_payload, k_inner_payload = sums((k_first, k_mid), (k_second, k_outer))
    k_one, k_inner = along_z(k_one_payload, BACK_ONE), along_z(k_inner_payload, BACK_INNER)

    def to_core(away):
        return move(
            away, [((z, x, z % 2), (z, x, 1 - z % 2)) for z in range(4) for x in (0, 1)]
        )

    from_x = after(from_x, k_inner_payload)
    (grad_normed,) = sums((kept, from_x))
    v_one = after(v_one, grad_normed)
    value_own, value_away = halves(code, (v_second, v_inner, v_one))
    grad_value_weight = owned(code, value_own, to_core(value_away))
    k_one, k_inner = after_all((k_one, k_inner), grad_value_weight)
    key_own, key_away = halves(code, (k_second, k_inner, k_one))
    grad_key_weight = owned(code, key_own, to_core(key_away))
    return (attention, grad_normed, grad_q, grad_key_weight, grad_value_weight)


def body(normed, q_raw, *rest):
    planes = (
        lax.axis_size("seq") == 16
        and lax.axis_size("uly") == 2
        and 4 * normed.shape[0] == WINDOW
        and q_raw.shape[1] == 8 * HD
    )
    return (body_planes if planes else body_general)(normed, q_raw, *rest)


def solution(mesh):
    return jax.shard_map(
        body,
        mesh=mesh,
        in_specs=(
            P("seq", "uly"),
            P("seq", "uly"),
            P("uly", "seq"),
            P("uly", "seq"),
            P(),
            P(),
            P(),
            P("seq", "uly"),
        ),
        out_specs=(
            P("seq", "uly"),
            P("seq", "uly"),
            P("seq", "uly"),
            P("uly", "seq"),
            P("uly", "seq"),
        ),
        check_vma=False,
    )
```
